128 devices in a mesh: dp: 128 (over y, x, z, core).
Axes of the slice: x: 4, y: 4, z: 4, core: 2. Of those that a mesh axis runs over, the one named last changes fastest.
Arguments:
- features: bfloat16 [1024, 784, 192], P('dp'), may hold values from -21 to 21
- batchnorm_scale: float32 [192], replicated, may hold values from 0.1 to 1.9
- batchnorm_bias: float32 [192], replicated, may hold values from -3 to 3
- w_short: bfloat16 [192, 384], replicated, may hold values from -0.4375 to 0.4375
- ln1_gain: float32 [192], replicated, may hold values from 0.1 to 1.9
- ln1_bias: float32 [192], replicated, may hold values from -3 to 3
- w_qkv: bfloat16 [192, 1152], replicated, may hold values from -0.4375 to 0.4375
- rel_table: float32 [12, 729], replicated, may hold values from -4 to 4
- w_out: bfloat16 [384, 384], replicated, may hold values from -0.875 to 0.875
- ln2_gain: float32 [384], replicated, may hold values from 0.1 to 1.9
- ln2_bias: float32 [384], replicated, may hold values from -3 to 3
- w_fc1: bfloat16 [384, 1536], replicated, may hold values from -0.3125 to 0.3125
- fc1_bias: float32 [1536], replicated, may hold values from -3 to 3
- w_fc2: bfloat16 [1536, 384], replicated, may hold values from -0.15625 to 0.15625
- fc2_bias: float32 [384], replicated, may hold values from -3 to 3
- cotangent: bfloat16 [1024, 196, 384], P('dp'), may hold values from -6 to 6
Outputs:
- layer_out: float32 [1024, 196, 384], P('dp')
- grad_features: float32 [1024, 784, 192], P('dp')
- batchnorm_scale_gradient: float32 [192], replicated
- grad_bn_bias: float32 [192], replicated
- grad_w_short: float32 [192, 384], replicated
- grad_ln1_gain: float32 [192], replicated
- grad_ln1_bias: float32 [192], replicated
- grad_w_qkv: float32 [192, 1152], replicated
- grad_rel_table: float32 [12, 729], replicated
- grad_w_out: float32 [384, 384], replicated
- grad_ln2_gain: float32 [384], replicated
- grad_ln2_bias: float32 [384], replicated
- grad_w_fc1: float32 [384, 1536], replicated
- grad_fc1_bias: float32 [1536], replicated
- grad_w_fc2: float32 [1536, 384], replicated
- grad_fc2_bias: float32 [384], replicated
The draws below stay inside these ranges and needn't reach their ends.
All inputs are finite; a program needn't handle non-finite values.
Results may differ from the reference program's by a relative error of at most 0.012.
The reference program's roundings to bfloat16 on the way count: a program that leaves them out, or rounds other values in their place, can miss the bound.
Values sent between devices are 32-bit elements; how exact they have to be, the bound alone decides.
No kernel may reach another device: no remote copies, remote signals or barrier semaphores. Data moves between devices by JAX's collectives and lax.ppermute only.
A program may use at most 192 MiB of HBM per device.

```python
import jax
import jax.numpy as jnp
from jax import lax

D_IN = 192
D = 384
HEADS = 12
HEAD = 32
FF = 1536
SIDE = 14
TOK = 196
PRE_ROWS = 784
REL = 729
CROPS = 1024


def draw_features(key, part):
    key = jax.random.fold_in(key, 11)
    noise_key, shift_key = jax.random.split(key)
    position = jnp.arange(CROPS, dtype=jnp.float32) / max(CROPS - 1, 1)
    noise = jax.random.truncated_normal(noise_key, -6.0, 6.0, (CROPS, PRE_ROWS, D_IN), jnp.float32)
    factor = 1.0 + 2.0 * position
    shift_vec = jax.random.uniform(shift_key, (D_IN,), jnp.float32, -1.0, 1.0)
    return (factor[:, None, None] * (noise + shift_vec)).astype(jnp.bfloat16)


def level_of(key, extent, pieces, least, largest):
    def one(dim, blocks):
        draws = jax.random.uniform(jax.random.fold_in(jax.random.fold_in(key, 6), dim), (blocks,), jnp.float32, least / len(pieces), largest / len(pieces))
        return jnp.repeat(jnp.exp(draws), extent[dim] // blocks).reshape((-1,) + (1,) * (len(extent) - dim - 1))

    level = one(*pieces[0])
    for cut in pieces[1:]:
        level = level * one(*cut)
    return level


def normal_values(rng, shape, scale, reach, cuts=(), held_as=jnp.bfloat16):
    factor_of = level_of(rng, shape, cuts, -0.22, 0.18) if cuts else 1.0
    result = jax.random.normal(rng, shape, jnp.float32) * scale * factor_of
    return jnp.minimum(jnp.maximum(result, -reach), reach).astype(held_as)


def setup_inputs(seed: int = 0) -> dict:
    key_of = jax.random.split(jax.random.key(seed), 17)
    features = draw_features(jax.random.fold_in(key_of[16], 71), 0)
    batchnorm_scale = jnp.clip(1.0 + 0.18 * jax.random.normal(key_of[1], (D_IN,), jnp.float32), 0.1, 1.9)
    batchnorm_bias = normal_values(key_of[2], (D_IN,), 0.5, 3.0, (), jnp.float32)
    w_short = normal_values(key_of[3], (D_IN, D), D_IN ** -0.5, 0.4375)
    ln1_gain = jnp.clip(1.0 + 0.18 * jax.random.normal(key_of[4], (D_IN,), jnp.float32), 0.1, 1.9)
    ln1_bias = normal_values(key_of[5], (D_IN,), 0.5, 3.0, (), jnp.float32)
    w_qkv = normal_values(key_of[6], (D_IN, 3 * D), D_IN ** -0.5, 0.4375)
    rel_table = normal_values(key_of[7], (HEADS, REL), 1.0, 4.0, (), jnp.float32)
    w_out = normal_values(key_of[8], (D, D), (D // 8) ** -0.5, 0.875)
    ln2_gain = jnp.clip(1.0 + 0.18 * jax.random.normal(key_of[9], (D,), jnp.float32), 0.1, 1.9)
    ln2_bias = normal_values(key_of[10], (D,), 0.5, 3.0, (), jnp.float32)
    w_fc1 = normal_values(key_of[11], (D, FF), D ** -0.5, 0.3125)
    fc1_bias = normal_values(key_of[12], (FF,), 0.5, 3.0, (), jnp.float32)
    w_fc2 = normal_values(key_of[13], (FF, D), FF ** -0.5, 0.15625)
    fc2_bias = normal_values(key_of[14], (D,), 0.5, 3.0, (), jnp.float32)
    cotangent = normal_values(key_of[15], (CROPS, TOK, D), 1.0, 6.0, ((0, 128),))
    return dict(features=features, batchnorm_scale=batchnorm_scale, batchnorm_bias=batchnorm_bias, w_short=w_short, ln1_gain=ln1_gain, ln1_bias=ln1_bias, w_qkv=w_qkv, rel_table=rel_table, w_out=w_out, ln2_gain=ln2_gain, ln2_bias=ln2_bias, w_fc1=w_fc1, fc1_bias=fc1_bias, w_fc2=w_fc2, fc2_bias=fc2_bias, cotangent=cotangent)


EPS = 1e-05
HIGH = lax.Precision.HIGHEST

@jax.custom_vjp
def low(v):
    return lax.optimization_barrier(v.astype(jnp.bfloat16)).astype(jnp.float32)

@jax.custom_vjp
def low_back(v):
    return v

def low_keep(v):
    return (low(v), None)

def low_pass(kept, grad):
    return (grad,)

def back_keep(v):
    return (v, None)

def back_low(kept, grad):
    return (low(grad),)
low.defvjp(low_keep, low_pass)
low_back.defvjp(back_keep, back_low)

def rel_index():
    position = jnp.arange(TOK, dtype=jnp.int32)
    row_pos = position // SIDE
    col_pos = position % SIDE
    return ((row_pos[:, None] - row_pos[None, :] + SIDE - 1) * (2 * SIDE - 1) + col_pos[:, None] - col_pos[None, :] + SIDE - 1).astype(jnp.int32)

def layer_norm(values, gain_vec, shift_vec):
    centre = values - lax.optimization_barrier(jnp.mean(values, axis=-1, keepdims=True))
    spread = lax.optimization_barrier(jnp.mean(centre * centre, axis=-1, keepdims=True))
    return centre * lax.rsqrt(spread + EPS) * gain_vec + shift_vec

def pooling(values):
    crop_count = values.shape[0]
    grid = values.reshape(crop_count, SIDE, 2, SIDE, 2, values.shape[-1])
    return jax.nn.logsumexp(grid, axis=(2, 4)).reshape(crop_count, TOK, values.shape[-1])

def matmul_full(left, right):
    return jnp.einsum('...i,ij->...j', left, right, precision=HIGH)

def attend(packed, bias):
    query = packed[:, :D].reshape(TOK, HEADS, HEAD)
    key_part = packed[:, D:2 * D].reshape(TOK, HEADS, HEAD)
    value_part = packed[:, 2 * D:].reshape(TOK, HEADS, HEAD)
    scores = low_back(jnp.einsum('ihd,jhd->hij', query, key_part, precision=HIGH) * HEAD ** (-0.5) + bias)
    probs = low(jnp.exp(scores - jax.nn.logsumexp(scores, axis=-1, keepdims=True)))
    mixed = jnp.einsum('hij,jhd->ihd', probs, value_part, precision=HIGH).reshape(TOK, D)
    return low(low_back(mixed))

def forward(features, batchnorm_scale, batchnorm_bias, w_short, ln1_gain, ln1_bias, w_qkv, rel_table, w_out, ln2_gain, ln2_bias, w_fc1, fc1_bias, w_fc2, fc2_bias):
    bn_mean = lax.optimization_barrier(jnp.mean(features, axis=(0, 1)))
    centre = features - bn_mean
    bn_var = lax.optimization_barrier(jnp.mean(centre * centre, axis=(0, 1)))
    normalized_output = centre * lax.rsqrt(bn_var + EPS) * batchnorm_scale + batchnorm_bias
    pooled = pooling(normalized_output)
    short = low_back(matmul_full(low(pooled), w_short))
    first_norm = low(layer_norm(pooled, ln1_gain, ln1_bias))
    packed = low(low_back(matmul_full(first_norm, w_qkv)))
    bias = rel_table[:, rel_index()]
    mixed = lax.map(jax.checkpoint(lambda one: attend(one, bias)), packed)
    branch = low_back(matmul_full(mixed, w_out))
    resid = short + branch
    second_norm = low(layer_norm(resid, ln2_gain, ln2_bias))
    pre_act = low_back(matmul_full(second_norm, w_fc1) + fc1_bias)
    hidden = low(jax.nn.gelu(pre_act, approximate=False))
    return resid + low_back(matmul_full(hidden, w_fc2) + fc2_bias)

def reference(features, batchnorm_scale, batchnorm_bias, w_short, ln1_gain, ln1_bias, w_qkv, rel_table, w_out, ln2_gain, ln2_bias, w_fc1, fc1_bias, w_fc2, fc2_bias, cotangent):
    inputs = (features.astype(jnp.float32), batchnorm_scale, batchnorm_bias, w_short.astype(jnp.float32), ln1_gain, ln1_bias, w_qkv.astype(jnp.float32), rel_table, w_out.astype(jnp.float32), ln2_gain, ln2_bias, w_fc1.astype(jnp.float32), fc1_bias, w_fc2.astype(jnp.float32), fc2_bias)
    layer_out, back_fn = jax.vjp(forward, *inputs)
    grads = back_fn(cotangent.astype(jnp.float32))
    return (layer_out, grads[0], grads[1], grads[2], grads[3], grads[4], grads[5], grads[6], grads[7], grads[8], grads[9], grads[10], grads[11], grads[12], grads[13], grads[14])
```

```python
import jax
import jax.numpy as jnp
import numpy as np
from jax import lax
from jax.experimental import pallas as pl
from jax.experimental.pallas import tpu as pltpu
from jax.sharding import PartitionSpec as P

HEADS = 12
HEAD = 32
SIDE = 14
TOK = 196
TP = 208
GRID2 = 2 * SIDE
CELLS = 784
D_IN = 192
D = 384
FF = 1536
CROPS = 8
ROWS = TOK * CROPS
ROWS_P = TP * CROPS
REL = 27
TAB = 768
SPREAD = 384

EPS = 1e-05
FLOAT = jnp.float32
HALF = jnp.bfloat16
LOG2E = 1.4426950408889634
SCALE = HEAD ** (-0.5)
NN = (((1,), (0,)), ((), ()))
NT = (((1,), (1,)), ((), ()))
TN = (((0,), (0,)), ((), ()))
VMEM_LIMIT = 56 * 1024 * 1024


def dot(left, right, dims=NN):
    return lax.dot_general(left, right, dims, preferred_element_type=FLOAT)


def split3(value):
    hi = value.astype(HALF)
    rest = value - hi.astype(FLOAT)
    mid = rest.astype(HALF)
    lo = (rest - mid.astype(FLOAT)).astype(HALF)
    return hi, mid, lo


def params(limit=VMEM_LIMIT):
    return pltpu.CompilerParams(vmem_limit_bytes=limit)


def cost(flops, bytes_accessed, transcendentals=0):
    return pl.CostEstimate(
        flops=int(flops), bytes_accessed=int(bytes_accessed), transcendentals=int(transcendentals)
    )


def whole(shape):
    return pl.BlockSpec(shape, lambda *_: (0,) * len(shape))


def select_matrix():
    table = np.zeros((4 * TP, CELLS), np.float32)
    for part in range(4):
        a, b = divmod(part, 2)
        for t in range(TOK):
            i, j = divmod(t, SIDE)
            table[part * TP + t, (2 * i + a) * GRID2 + 2 * j + b] = 1.0
    return table


def spread_matrix():
    table = np.zeros((SPREAD, TP), np.float32)
    for t in range(TOK):
        i, j = divmod(t, SIDE)
        table[REL * i + j, t] = 1.0
    return table


def reverse_spread_matrix():
    table = np.zeros((TP, SPREAD), np.float32)
    for t in range(TOK):
        i, j = divmod(t, SIDE)
        table[t, 364 - (REL * i + j)] = 1.0
    return table


def stats_kernel(x_ref, out_ref):
    pieces = []
    step = 32
    for block in range(D_IN // step):
        rows = slice(block * step, (block + 1) * step)
        total = x_ref[0, rows, :].astype(FLOAT)
        for crop in range(1, CROPS):
            total = total + x_ref[crop, rows, :].astype(FLOAT)
        total = jnp.sum(total, axis=1, keepdims=True)
        mean = total * (1.0 / (CROPS * CELLS))
        square = jnp.zeros((step, CELLS), FLOAT)
        for crop in range(CROPS):
            centre = x_ref[crop, rows, :].astype(FLOAT) - mean
            square = square + centre * centre
        square = jnp.sum(square, axis=1, keepdims=True)
        lane = lax.broadcasted_iota(jnp.int32, (step, 128), 1)
        pieces.append(jnp.where(lane == 0, mean, jnp.where(lane == 1, square, 0.0)))
    turned = jnp.concatenate(pieces, axis=0).T
    pad = jnp.zeros((1, 64), FLOAT)
    row = jnp.concatenate([turned[0:1], pad, turned[1:2], pad], axis=1)
    out_ref[...] = jnp.broadcast_to(row[None], out_ref.shape)


def local_stats(cells, copies):
    return pl.pallas_call(
        stats_kernel,
        out_shape=jax.ShapeDtypeStruct((copies, 1, 512), FLOAT),
        compiler_params=params(),
        name="stats",
        cost_estimate=cost(8e6, 2.8e6),
    )(cells)


def batch_coefficients(gathered):
    count = gathered.shape[0]
    means = gathered[:, 0, 0:D_IN]
    squares = gathered[:, 0, 256 : 256 + D_IN]
    mean = jnp.sum(means, axis=0, keepdims=True) * (1.0 / count)
    off = means - mean
    local = float(CROPS * CELLS)
    var = jnp.sum(squares, axis=0, keepdims=True) + local * jnp.sum(
        off * off, axis=0, keepdims=True
    )
    return mean, lax.rsqrt(var * (1.0 / (local * count)) + EPS)


def select_kernel(s_ref, x_ref, out_ref):
    out_ref[0] = dot(s_ref[...], x_ref[0], NT).astype(HALF)


def select_cells(picks, cells):
    return pl.pallas_call(
        select_kernel,
        grid=(CROPS,),
        in_specs=[
            whole((4 * TP, CELLS)),
            pl.BlockSpec((1, D_IN, CELLS), lambda c: (c, 0, 0)),
        ],
        out_specs=pl.BlockSpec((1, 4 * TP, D_IN), lambda c: (c, 0, 0)),
        out_shape=jax.ShapeDtypeStruct((CROPS, 4 * TP, D_IN), HALF),
        compiler_params=params(),
        name="select_cells",
        cost_estimate=cost(3e9, 7e6),
    )(picks, cells)


def bias_kernel(table_ref, spread_ref, out_ref, rows_ref):
    table = table_ref[0] * LOG2E
    base = pltpu.roll(jnp.broadcast_to(table, (16, TAB)), 0, 1, stride=1, stride_axis=0)
    for r in range(SIDE):
        rolled = pltpu.roll(base, (TAB - 364 + REL * r) % TAB, 1)
        rows_ref[SIDE * r : SIDE * (r + 1), :] = rolled[:SIDE, :SPREAD]
    rows_ref[TOK:, :] = jnp.zeros((TP - TOK, SPREAD), FLOAT)
    value = jnp.zeros((TP, TP), FLOAT)
    for part in split3(rows_ref[...]):
        value = value + dot(part, spread_ref[...])
    row = lax.broadcasted_iota(jnp.int32, (TP, TP), 0)
    out_ref[0] = jnp.where(row < TOK, value, -1e30)


def expand_bias(rel_table, spread):
    table = jnp.pad(rel_table, ((0, 0), (0, TAB - REL * REL))).reshape(HEADS, 1, TAB)
    return pl.pallas_call(
        bias_kernel,
        grid=(HEADS,),
        in_specs=[
            pl.BlockSpec((1, 1, TAB), lambda h: (h, 0, 0)),
            whole((SPREAD, TP)),
        ],
        out_specs=pl.BlockSpec((1, TP, TP), lambda h: (h, 0, 0)),
        out_shape=jax.ShapeDtypeStruct((HEADS, TP, TP), FLOAT),
        scratch_shapes=[pltpu.VMEM((TP, SPREAD), FLOAT)],
        compiler_params=params(),
        name="expand_bias",
        cost_estimate=cost(2e9, 3e6),
    )(table, spread)


def table_kernel(d_ref, spread_ref, out_ref, rows_ref):
    value = jnp.zeros((TP, SPREAD), FLOAT)
    for part in split3(d_ref[0]):
        value = value + dot(part, spread_ref[...])
    rows_ref[:, :SPREAD] = value
    rows_ref[:, SPREAD:] = jnp.zeros((TP, TAB - SPREAD), FLOAT)
    total = jnp.zeros((16, TAB), FLOAT)
    for r in range(SIDE):
        total = total + pltpu.roll(rows_ref[SIDE * r : SIDE * r + 16, :], REL * r, 1)
    row = lax.broadcasted_iota(jnp.int32, (16, TAB), 0)
    total = pltpu.roll(jnp.where(row < SIDE, total, 0.0), 0, 1, stride=1, stride_axis=0)
    out_ref[0] = jnp.sum(total, axis=0, keepdims=True)


def reduce_table(grad_bias, spread):
    return pl.pallas_call(
        table_kernel,
        grid=(HEADS,),
        in_specs=[
            pl.BlockSpec((1, TP, TP), lambda h: (h, 0, 0)),
            whole((TP, SPREAD)),
        ],
        out_specs=pl.BlockSpec((1, 1, TAB), lambda h: (h, 0, 0)),
        out_shape=jax.ShapeDtypeStruct((HEADS, 1, TAB), FLOAT),
        scratch_shapes=[pltpu.VMEM((TP, TAB), FLOAT)],
        compiler_params=params(),
        name="reduce_table",
        cost_estimate=cost(2e9, 3e6),
    )(grad_bias, spread)


def normalised(x, coef_mean, coef_inv, scale, bias):
    return (x - coef_mean) * coef_inv * scale + bias


def pool_parts(x_ref, mean, inv, scale, bias):
    parts = [
        normalised(x_ref[0, part * TP : (part + 1) * TP, :].astype(FLOAT), mean, inv, scale, bias)
        for part in range(4)
    ]
    return parts


def norm_rows(value):
    centre = value - jnp.mean(value, axis=-1, keepdims=True)
    inverse = lax.rsqrt(jnp.mean(centre * centre, axis=-1, keepdims=True) + EPS)
    return centre * inverse, inverse


def put_rows(ref, crop, value):
    for group in range(ref.shape[0]):
        piece = value[:, group * 128 : (group + 1) * 128]
        if piece.shape[1] < 128:
            rest = jnp.zeros((piece.shape[0], 128 - piece.shape[1]), piece.dtype)
            piece = jnp.concatenate([piece, rest], axis=1)
        ref[group, pl.ds(crop, TP, stride=CROPS), :] = piece


def take_rows(ref, crop):
    pieces = [ref[group, pl.ds(crop, TP, stride=CROPS), :] for group in range(ref.shape[0])]
    return jnp.concatenate(pieces, axis=1)


def head_masks():
    lane = lax.broadcasted_iota(jnp.int32, (1, 128), 1)
    return [(lane // HEAD == k).astype(HALF) for k in range(4)]


def attention_kernel(
    gathered_ref,
    x_ref,
    bn_scale_ref,
    bn_bias_ref,
    gain_ref,
    shift_ref,
    w_ref,
    bias_ref,
    qkv_ref,
    probs_ref,
    attn_ref,
    pooled_ref,
    coef_ref,
):
    crop = pl.program_id(0)

    @pl.when(crop == 0)
    def _():
        mean, inv = batch_coefficients(gathered_ref[...])
        coef_ref[...] = jnp.zeros_like(coef_ref)
        coef_ref[0:1, :] = mean
        coef_ref[1:2, :] = inv

    mean = coef_ref[0:1, :]
    inv = coef_ref[1:2, :]
    parts = pool_parts(x_ref, mean, inv, bn_scale_ref[...], bn_bias_ref[...])
    top = jnp.maximum(jnp.maximum(parts[0], parts[1]), jnp.maximum(parts[2], parts[3]))
    pooled = top + jnp.log(sum(jnp.exp(part - top) for part in parts))
    put_rows(pooled_ref, crop, pooled)
    z, _ = norm_rows(pooled)
    first = (z * gain_ref[...] + shift_ref[...]).astype(HALF)
    qkv_ref[0] = dot(first, w_ref[...]).astype(HALF)
    value_t = qkv_ref[0, :, 2 * D :].astype(FLOAT).T.astype(HALF)
    masks = head_masks()
    heads = []
    for head in range(HEADS):
        group = head // 4
        lanes = slice(group * 128, (group + 1) * 128)
        query = qkv_ref[0, :, lanes] * masks[head % 4]
        key = qkv_ref[0, :, D + group * 128 : D + (group + 1) * 128]
        scores = dot(key, query, NT) * (SCALE * LOG2E) + bias_ref[head]
        weight = jnp.exp2(scores - jnp.max(scores, axis=0, keepdims=True))
        weight = weight * (1.0 / jnp.sum(weight, axis=0, keepdims=True))
        probs = weight.astype(HALF)
        probs_ref[0, head] = probs
        heads.append(dot(value_t[head * HEAD : (head + 1) * HEAD, :], probs))
    attn = jnp.concatenate(heads, axis=0).T
    put_rows(attn_ref, crop, attn.astype(HALF).astype(FLOAT))


def attention(gathered, picked, bn_scale, bn_bias, gain, shift, w_qkv, bias):
    return pl.pallas_call(
        attention_kernel,
        grid=(CROPS,),
        in_specs=[
            whole(gathered.shape),
            pl.BlockSpec((1, 4 * TP, D_IN), lambda c: (c, 0, 0)),
            whole((1, D_IN)),
            whole((1, D_IN)),
            whole((1, D_IN)),
            whole((1, D_IN)),
            whole((D_IN, 3 * D)),
            whole((HEADS, TP, TP)),
        ],
        out_specs=[
            pl.BlockSpec((1, TP, 3 * D), lambda c: (c, 0, 0)),
            pl.BlockSpec((1, HEADS, TP, TP), lambda c: (c, 0, 0, 0)),
            whole((3, ROWS_P, 128)),
            whole((2, ROWS_P, 128)),
            whole((8, D_IN)),
        ],
        out_shape=[
            jax.ShapeDtypeStruct((CROPS, TP, 3 * D), HALF),
            jax.ShapeDtypeStruct((CROPS, HEADS, TP, TP), HALF),
            jax.ShapeDtypeStruct((3, ROWS_P, 128), FLOAT),
            jax.ShapeDtypeStruct((2, ROWS_P, 128), FLOAT),
            jax.ShapeDtypeStruct((8, D_IN), FLOAT),
        ],
        compiler_params=params(),
        name="attention",
        cost_estimate=cost(4e9, 2.5e7, 4e6),
    )(gathered, picked, bn_scale, bn_bias, gain, shift, w_qkv, bias)


ERFC_P = 0.315
ERFC = (
    0.12566069143336625,
    0.12585512941590216,
    0.11090152008791473,
    0.10280489691671746,
    0.002058691612166641,
    0.12931269519223043,
    -0.13178668519368678,
    0.03519319657675152,
)


def normal_parts(u):
    size = jnp.abs(u)
    bell = jnp.exp2(u * u * (-0.5 * LOG2E))
    t = 1.0 / (1.0 + ERFC_P * size)
    series = jnp.full_like(t, ERFC[-1])
    for factor in ERFC[-2::-1]:
        series = series * t + factor
    tail = series * t * bell
    return jnp.where(u < 0, tail, 1.0 - tail), bell * (1.0 / np.sqrt(2 * np.pi))


HALF_ROWS = 5632
PIECES = 64
LATE_ROWS = 2048
AT_OUT0 = FF // 128 * D
AT_SHORT0 = AT_OUT0 + 2 * D
AT_SUMS = AT_SHORT0 + D_IN
AT_OUT1 = FF // 128 * D
AT_SHORT1 = AT_OUT1 + D

FC_ROWS = 224
FC_STEPS = ROWS // FC_ROWS
FC_COLS = 512


def feed_kernel(
    core_ref,
    attn_ref,
    pooled_ref,
    cot_ref,
    w_short_ref,
    w_out_ref,
    gain_ref,
    shift_ref,
    w1_ref,
    b1_ref,
    w2_ref,
    b2_ref,
    out_ref,
    dattn_ref,
    dshort_ref,
    message_ref,
    sums1_ref,
    sums_ref,
):
    step = pl.program_id(0)
    core = core_ref[0]
    first_half = pl.multiple_of(core * HALF_ROWS, HALF_ROWS)
    second_half = pl.multiple_of((1 - core) * HALF_ROWS, HALF_ROWS)

    def add(base, at, value):
        count = value.shape[0]
        for k in range(value.shape[1] // 128):
            place = pl.ds(pl.multiple_of(base + at + k * count, 8), count)
            message_ref[place, :] += value[:, k * 128 : (k + 1) * 128]

    @pl.when(step == 0)
    def _():
        message_ref[...] = jnp.zeros_like(message_ref)
        sums1_ref[...] = jnp.zeros_like(sums1_ref)
        sums_ref[...] = jnp.zeros_like(sums_ref)
        dattn_ref[:, ROWS:, :] = jnp.zeros((3, ROWS_P - ROWS, 128), FLOAT)
        dshort_ref[:, ROWS:, :] = jnp.zeros((2, ROWS_P - ROWS, 128), FLOAT)

    rows = pl.ds(pl.multiple_of(step * FC_ROWS, FC_ROWS), FC_ROWS)
    attn_wide = jnp.concatenate([attn_ref[k] for k in range(3)], axis=1)
    pooled_wide = jnp.concatenate([pooled_ref[k] for k in range(2)], axis=1)[:, :D_IN]
    attn = attn_wide.astype(HALF)
    pooled = pooled_wide.astype(HALF)
    cot = cot_ref[...]
    y1 = dot(pooled, w_short_ref[...]) + dot(attn, w_out_ref[...])
    z, inverse = norm_rows(y1)
    second = (z * gain_ref[...] + shift_ref[...]).astype(HALF)
    out = y1 + b2_ref[...]
    back = jnp.zeros((FC_ROWS, D), FLOAT)
    second_t = second.astype(FLOAT).T.astype(HALF)
    cot_t = cot.astype(FLOAT).T.astype(HALF)
    for block in range(FF // FC_COLS):
        cols = slice(block * FC_COLS, (block + 1) * FC_COLS)
        u = dot(second, w1_ref[:, cols]) + b1_ref[:, cols]
        cdf, bell = normal_parts(u)
        hidden = (u * cdf).astype(HALF)
        dhidden = dot(cot, w2_ref[cols, :], NT)
        du = (dhidden * (cdf + u * bell)).astype(HALF)
        out = out + dot(hidden, w2_ref[cols, :])
        back = back + dot(du, w1_ref[:, cols], NT)
        at = block * (FC_COLS // 128) * D
        add(first_half, at, dot(second_t, du))
        add(second_half, at, dot(cot_t, hidden))
        sums1_ref[:, cols] += jnp.sum(du.astype(FLOAT), axis=0, keepdims=True)
    out_ref[...] = out
    wide_cot = cot.astype(FLOAT)
    dz = back * gain_ref[...]
    dy1 = wide_cot + inverse * (
        dz
        - jnp.mean(dz, axis=-1, keepdims=True)
        - z * jnp.mean(dz * z, axis=-1, keepdims=True)
    )
    low = dy1.astype(HALF)
    dattn = dot(low, w_out_ref[...], NT).astype(HALF).astype(FLOAT)
    for k in range(3):
        dattn_ref[k, rows, :] = dattn[:, k * 128 : (k + 1) * 128]
    dshort = dot(low, w_short_ref[...], NT)
    dshort_ref[0, rows, :] = dshort[:, :128]
    dshort_ref[1, rows, :] = jnp.concatenate(
        [dshort[:, 128:], jnp.zeros((FC_ROWS, 256 - D_IN), FLOAT)], axis=1
    )
    gout = dot(attn_wide.T.astype(HALF), low)
    add(first_half, AT_OUT0, gout[:, : 2 * 128])
    add(second_half, AT_OUT1, gout[:, 2 * 128 :])
    gshort = dot(pooled_wide.T.astype(HALF), low)
    add(first_half, AT_SHORT0, gshort[:, :128])
    add(second_half, AT_SHORT1, gshort[:, 128:])
    sums_ref[0:1, :] += jnp.sum(back * z, axis=0, keepdims=True)
    sums_ref[1:2, :] += jnp.sum(back, axis=0, keepdims=True)
    sums_ref[2:3, :] += jnp.sum(wide_cot, axis=0, keepdims=True)

    @pl.when(step == FC_STEPS - 1)
    def _():
        pieces = [sums1_ref[:, k * 128 : (k + 1) * 128] for k in range(FF // 128)]
        for line in range(3):
            pieces += [sums_ref[line : line + 1, k * 128 : (k + 1) * 128] for k in range(3)]
        pieces.append(jnp.zeros((3, 128), FLOAT))
        message_ref[pl.ds(pl.multiple_of(first_half + AT_SUMS, 8), 24), :] = jnp.concatenate(
            pieces, axis=0
        )


def feed_forward(core, attn, pooled, cot, w_short, w_out, gain, shift, w1, b1, w2, b2):
    row_block = lambda width: pl.BlockSpec((FC_ROWS, width), lambda i: (i, 0))
    lane_block = lambda groups: pl.BlockSpec((groups, FC_ROWS, 128), lambda i: (0, i, 0))
    return pl.pallas_call(
        feed_kernel,
        grid=(FC_STEPS,),
        in_specs=[
            pl.BlockSpec(memory_space=pltpu.SMEM),
            lane_block(3),
            lane_block(2),
            row_block(D),
            whole((D_IN, D)),
            whole((D, D)),
            whole((1, D)),
            whole((1, D)),
            whole((D, FF)),
            whole((1, FF)),
            whole((FF, D)),
            whole((1, D)),
        ],
        out_specs=[
            row_block(D),
            whole((3, ROWS_P, 128)),
            whole((2, ROWS_P, 128)),
            whole((2 * HALF_ROWS, 128)),
        ],
        out_shape=[
            jax.ShapeDtypeStruct((ROWS, D), FLOAT),
            jax.ShapeDtypeStruct((3, ROWS_P, 128), FLOAT),
            jax.ShapeDtypeStruct((2, ROWS_P, 128), FLOAT),
            jax.ShapeDtypeStruct((2 * HALF_ROWS, 128), FLOAT),
        ],
        scratch_shapes=[pltpu.VMEM((1, FF), FLOAT), pltpu.VMEM((8, D), FLOAT)],
        compiler_params=params(),
        name="feed_forward",
        cost_estimate=cost(1.2e10, 2e7, 3e6),
    )(core, attn, pooled, cot, w_short, w_out, gain, shift, w1, b1, w2, b2)


def unpack_kernel(
    core_ref, own_ref, other_ref, g1_ref, g2_ref, gout_ref, gshort_ref, sums1_ref, sums_ref
):
    def first(ref):
        for k in range(FF // 128):
            g1_ref[:, k * 128 : (k + 1) * 128] = ref[k * D : (k + 1) * D, :]
        for k in range(2):
            at = AT_OUT0 + k * D
            gout_ref[:, k * 128 : (k + 1) * 128] = ref[at : at + D, :]
        gshort_ref[:, :128] = ref[AT_SHORT0 : AT_SHORT0 + D_IN, :]
        lines = ref[AT_SUMS : AT_SUMS + 24, :]
        for k in range(FF // 128):
            sums1_ref[:, k * 128 : (k + 1) * 128] = lines[k : k + 1, :]
        sums_ref[...] = jnp.zeros_like(sums_ref)
        for line in range(3):
            for k in range(3):
                at = FF // 128 + line * 3 + k
                sums_ref[line : line + 1, k * 128 : (k + 1) * 128] = lines[at : at + 1, :]

    def second(ref):
        for k in range(FF // 128):
            g2_ref[k * 128 : (k + 1) * 128, :] = ref[k * D : (k + 1) * D, :].T
        gout_ref[:, 2 * 128 :] = ref[AT_OUT1 : AT_OUT1 + D, :]
        for k in range(2):
            at = AT_SHORT1 + k * D_IN
            gshort_ref[:, (k + 1) * 128 : (k + 2) * 128] = ref[at : at + D_IN, :]

    @pl.when(core_ref[0] == 0)
    def _():
        first(own_ref)
        second(other_ref)

    @pl.when(core_ref[0] != 0)
    def _():
        first(other_ref)
        second(own_ref)


def unpack(core, own, other):
    shapes = [(D, FF), (FF, D), (D, D), (D_IN, D), (1, FF), (8, D)]
    return pl.pallas_call(
        unpack_kernel,
        in_specs=[
            pl.BlockSpec(memory_space=pltpu.SMEM),
            whole((HALF_ROWS, 128)),
            whole((HALF_ROWS, 128)),
        ],
        out_specs=[whole(shape) for shape in shapes],
        out_shape=[jax.ShapeDtypeStruct(shape, FLOAT) for shape in shapes],
        compiler_params=params(),
        name="unpack",
        cost_estimate=cost(1e6, 1.2e7),
    )(core, own, other)


def back_kernel(
    coef_ref,
    x_ref,
    qkv_ref,
    probs_ref,
    dattn_ref,
    dshort_ref,
    bn_scale_ref,
    bn_bias_ref,
    gain_ref,
    shift_ref,
    w_ref,
    dbias_ref,
    gw_ref,
    sums_ref,
    dcells_ref,
):
    crop = pl.program_id(0)

    @pl.when(crop == 0)
    def _():
        dbias_ref[...] = jnp.zeros_like(dbias_ref)
        gw_ref[...] = jnp.zeros_like(gw_ref)
        sums_ref[...] = jnp.zeros_like(sums_ref)

    dattn = take_rows(dattn_ref, crop).astype(HALF)
    key_t = qkv_ref[0, :, D : 2 * D].astype(FLOAT).T.astype(HALF)
    masks = head_masks()
    dquery_t, dkeys, dvalues = [], [], []
    for group in range(3):
        lanes = slice(group * 128, (group + 1) * 128)
        query_all = qkv_ref[0, :, lanes]
        value = qkv_ref[0, :, 2 * D + group * 128 : 2 * D + (group + 1) * 128]
        dkey = jnp.zeros((TP, 128), FLOAT)
        dvalue = jnp.zeros((TP, 128), FLOAT)
        for k in range(4):
            head = group * 4 + k
            grad = dattn[:, lanes] * masks[k]
            query = query_all * masks[k]
            probs = probs_ref[0, head]
            wide = probs.astype(FLOAT)
            dprobs = dot(value, grad, NT)
            shared = jnp.sum(dprobs * wide, axis=0, keepdims=True)
            dscores = (wide * (dprobs - shared)).astype(HALF)
            dbias_ref[head] += dscores.astype(FLOAT)
            dvalue = dvalue + dot(probs, grad)
            dkey = dkey + dot(dscores, query)
            dquery_t.append(dot(key_t[head * HEAD : (head + 1) * HEAD, :], dscores))
        dkeys.append(dkey)
        dvalues.append(dvalue)
    dquery = jnp.concatenate(dquery_t, axis=0).T
    dqkv = jnp.concatenate(
        [dquery * SCALE] + [dkey * SCALE for dkey in dkeys] + dvalues, axis=1
    ).astype(HALF)
    parts = pool_parts(x_ref, coef_ref[0:1, :], coef_ref[1:2, :], bn_scale_ref[...], bn_bias_ref[...])
    top = jnp.maximum(jnp.maximum(parts[0], parts[1]), jnp.maximum(parts[2], parts[3]))
    pooled = top + jnp.log(sum(jnp.exp(part - top) for part in parts))
    z, inverse = norm_rows(pooled)
    first_t = (z * gain_ref[...] + shift_ref[...]).T.astype(HALF)
    gw_ref[...] += dot(first_t, dqkv)
    dfirst = dot(dqkv, w_ref[...], NT)
    dz = dfirst * gain_ref[...]
    dpooled = take_rows(dshort_ref, crop)[:, :D_IN] + inverse * (
        dz
        - jnp.mean(dz, axis=-1, keepdims=True)
        - z * jnp.mean(dz * z, axis=-1, keepdims=True)
    )
    sums_ref[0:1, :] += jnp.sum(dfirst * z, axis=0, keepdims=True)
    sums_ref[1:2, :] += jnp.sum(dfirst, axis=0, keepdims=True)
    along = jnp.zeros((TP, D_IN), FLOAT)
    total = jnp.zeros((TP, D_IN), FLOAT)
    for part in range(4):
        dpart = dpooled * jnp.exp(parts[part] - pooled)
        dcells_ref[0, part * TP : (part + 1) * TP, :] = dpart
        raw = x_ref[0, part * TP : (part + 1) * TP, :].astype(FLOAT)
        along = along + dpart * (raw - coef_ref[0:1, :])
        total = total + dpart
    sums_ref[2:3, :] += jnp.sum(along, axis=0, keepdims=True) * coef_ref[1:2, :]
    sums_ref[3:4, :] += jnp.sum(total, axis=0, keepdims=True)


def attention_back(coef, picked, qkv, probs, dattn, dshort, bn_scale, bn_bias, gain, shift, w_qkv):
    return pl.pallas_call(
        back_kernel,
        grid=(CROPS,),
        in_specs=[
            whole((8, D_IN)),
            pl.BlockSpec((1, 4 * TP, D_IN), lambda c: (c, 0, 0)),
            pl.BlockSpec((1, TP, 3 * D), lambda c: (c, 0, 0)),
            pl.BlockSpec((1, HEADS, TP, TP), lambda c: (c, 0, 0, 0)),
            whole((3, ROWS_P, 128)),
            whole((2, ROWS_P, 128)),
            whole((1, D_IN)),
            whole((1, D_IN)),
            whole((1, D_IN)),
            whole((1, D_IN)),
            whole((D_IN, 3 * D)),
        ],
        out_specs=[
            whole((HEADS, TP, TP)),
            whole((D_IN, 3 * D)),
            whole((8, D_IN)),
            pl.BlockSpec((1, 4 * TP, D_IN), lambda c: (c, 0, 0)),
        ],
        out_shape=[
            jax.ShapeDtypeStruct((HEADS, TP, TP), FLOAT),
            jax.ShapeDtypeStruct((D_IN, 3 * D), FLOAT),
            jax.ShapeDtypeStruct((8, D_IN), FLOAT),
            jax.ShapeDtypeStruct((CROPS, 4 * TP, D_IN), FLOAT),
        ],
        compiler_params=params(),
        name="attention_back",
        cost_estimate=cost(6e9, 4e7, 2e6),
    )(coef, picked, qkv, probs, dattn, dshort, bn_scale, bn_bias, gain, shift, w_qkv)


def scatter_kernel(s_ref, d_ref, out_ref):
    value = d_ref[0]
    hi = value.astype(HALF)
    lo = (value - hi.astype(FLOAT)).astype(HALF)
    out_ref[0] = dot(hi, s_ref[...], TN) + dot(lo, s_ref[...], TN)


def scatter_cells(picks, dcells):
    return pl.pallas_call(
        scatter_kernel,
        grid=(CROPS,),
        in_specs=[
            whole((4 * TP, CELLS)),
            pl.BlockSpec((1, 4 * TP, D_IN), lambda c: (c, 0, 0)),
        ],
        out_specs=pl.BlockSpec((1, D_IN, CELLS), lambda c: (c, 0, 0)),
        out_shape=jax.ShapeDtypeStruct((CROPS, D_IN, CELLS), FLOAT),
        compiler_params=params(),
        name="scatter_cells",
        cost_estimate=cost(6e9, 1.2e7),
    )(picks, dcells)


def column(row):
    return jnp.broadcast_to(row, (128, D_IN)).T[:, 0:1]


def cells_kernel(gathered_ref, coef_ref, scale_ref, d_ref, x_ref, out_ref, sums_ref, cols_ref):
    @pl.when(pl.program_id(0) == 0)
    def _():
        gathered = gathered_ref[...]
        total = jnp.sum(gathered, axis=0)
        along = total[:, 0:D_IN]
        plain = total[:, 256 : 256 + D_IN]
        sums_ref[...] = jnp.zeros_like(sums_ref)
        sums_ref[0:1, :] = along
        sums_ref[1:2, :] = plain
        mean = coef_ref[0:1, :]
        inv = coef_ref[1:2, :]
        factor = inv * scale_ref[...]
        count = 1.0 / float(gathered.shape[0] * CROPS * CELLS)
        slope = factor * along * inv * count
        cols_ref[:, 0:1] = column(factor)
        cols_ref[:, 1:2] = column(factor * plain * count)
        cols_ref[:, 2:3] = column(slope)
        cols_ref[:, 3:4] = column(mean)

    out_ref[0] = (
        d_ref[0] * cols_ref[:, 0:1]
        - cols_ref[:, 1:2]
        - (x_ref[0].astype(FLOAT) - cols_ref[:, 3:4]) * cols_ref[:, 2:3]
    )


def cell_gradient(gathered, coef, bn_scale, dcells, cells):
    crop_block = pl.BlockSpec((1, D_IN, CELLS), lambda c: (c, 0, 0))
    return pl.pallas_call(
        cells_kernel,
        grid=(CROPS,),
        in_specs=[
            whole(gathered.shape),
            whole((8, D_IN)),
            whole((1, D_IN)),
            crop_block,
            crop_block,
        ],
        out_specs=[crop_block, whole((8, D_IN))],
        out_shape=[
            jax.ShapeDtypeStruct((CROPS, D_IN, CELLS), FLOAT),
            jax.ShapeDtypeStruct((8, D_IN), FLOAT),
        ],
        scratch_shapes=[pltpu.VMEM((D_IN, 128), FLOAT)],
        compiler_params=params(),
        name="cell_gradient",
        cost_estimate=cost(1e7, 1.5e7),
    )(gathered, coef, bn_scale, dcells, cells)


CHIPS = ("y", "x", "z")
ALL = ("y", "x", "z", "core")


def gather_rows(copies):
    if copies.shape[0] == 1:
        return copies
    return lax.all_to_all(copies, ALL, 0, 0)


def sum_early(message, count):
    if count == 1:
        return message[0], message[1]
    swap = [(0, 1), (1, 0)]
    mine = message[0] + lax.ppermute(message[1], "core", swap)
    pieces = lax.all_to_all(mine.reshape(PIECES, -1, 128), CHIPS, 0, 0)
    piece = jnp.sum(pieces, axis=0)
    copies = jnp.broadcast_to(piece[None], pieces.shape)
    own = lax.all_to_all(copies, CHIPS, 0, 0).reshape(HALF_ROWS, 128)
    return own, lax.ppermute(own, "core", swap)


def sum_late(message, count):
    if count == 1:
        return message
    pieces = lax.all_to_all(message.reshape(count, -1, 128), ALL, 0, 0)
    copies = jnp.broadcast_to(jnp.sum(pieces, axis=0)[None], pieces.shape)
    return lax.all_to_all(copies, ALL, 0, 0).reshape(LATE_ROWS, 128)


def on_device(
    count,
    features,
    bn_scale,
    bn_bias,
    w_short,
    ln1_gain,
    ln1_bias,
    w_qkv,
    rel_table,
    w_out,
    ln2_gain,
    ln2_bias,
    w_fc1,
    fc1_bias,
    w_fc2,
    fc2_bias,
    cotangent,
):
    row = lambda v: v.reshape(1, -1)
    picks = jnp.asarray(select_matrix(), HALF)
    spread = jnp.asarray(spread_matrix(), HALF)
    spread_back = jnp.asarray(reverse_spread_matrix(), HALF)
    core = lax.axis_index("core").astype(jnp.int32).reshape(1)
    cells = features.transpose(0, 2, 1)
    cot = cotangent.transpose(1, 0, 2).reshape(ROWS, D)
    stats = gather_rows(local_stats(cells, count))
    picked = select_cells(picks, cells)
    bias = expand_bias(rel_table, spread)
    qkv, probs, attn, pooled, coef = attention(
        stats, picked, row(bn_scale), row(bn_bias), row(ln1_gain), row(ln1_bias), w_qkv, bias
    )
    out, dattn, dshort, message = feed_forward(
        core,
        attn,
        pooled,
        cot,
        w_short,
        w_out,
        row(ln2_gain),
        row(ln2_bias),
        w_fc1,
        row(fc1_bias),
        w_fc2,
        row(fc2_bias),
    )
    own, other = sum_early(message.reshape(2, HALF_ROWS, 128), count)
    dbias, gqkv, sums, dcells = attention_back(
        coef,
        picked,
        qkv,
        probs,
        dattn,
        dshort,
        row(bn_scale),
        row(bn_bias),
        row(ln1_gain),
        row(ln1_bias),
        w_qkv,
    )
    bn_message = jnp.pad(sums[2:4], ((0, 0), (0, 256 - D_IN))).reshape(1, 1, 512)
    gathered = gather_rows(jnp.broadcast_to(bn_message, (count, 1, 512)))
    scattered = scatter_cells(picks, dcells)
    table = reduce_table(dbias, spread_back)
    late = jnp.concatenate(
        [gqkv[:, k * 128 : (k + 1) * 128] for k in range(9)]
        + [
            table.reshape(HEADS * 6, 128),
            jnp.pad(sums[0:2], ((0, 0), (0, 256 - D_IN))).reshape(4, 128),
        ],
        axis=0,
    )
    late = sum_late(jnp.pad(late, ((0, LATE_ROWS - late.shape[0]), (0, 0))), count)
    grad_cells, bn_sums = cell_gradient(gathered, coef, row(bn_scale), scattered, cells)
    g1, g2, gout, gshort, sums1, sums2 = unpack(core, own, other)
    gqkv = jnp.concatenate([late[k * D_IN : (k + 1) * D_IN] for k in range(9)], axis=1)
    at = 9 * D_IN
    grad_table = late[at : at + HEADS * 6].reshape(HEADS, TAB)[:, : REL * REL][:, ::-1]
    sums = late[at + HEADS * 6 : at + HEADS * 6 + 4].reshape(2, 256)[:, :D_IN]
    return (
        out.reshape(TOK, CROPS, D).transpose(1, 0, 2),
        grad_cells.transpose(0, 2, 1),
        bn_sums[0],
        bn_sums[1],
        gshort,
        sums[0],
        sums[1],
        gqkv,
        grad_table,
        gout,
        sums2[0],
        sums2[1],
        g1,
        sums1[0],
        g2,
        sums2[2],
    )


def solution(mesh):
    count = mesh.size
    shape = (4, 4, 4, 2) if count == 128 else (1, 1, 1, 1)
    grid = jax.sharding.Mesh(mesh.devices.reshape(shape), ALL)
    split = P(ALL, None, None)
    same = P()
    in_specs = (split,) + (same,) * 14 + (split,)
    out_specs = (split, split) + (same,) * 14

    def run(*args):
        return on_device(count, *args)

    return jax.shard_map(run, mesh=grid, in_specs=in_specs, out_specs=out_specs, check_vma=False)
```

```python
import functools

import jax
import jax.numpy as jnp
import numpy as np
from jax import lax
from jax.experimental import pallas as pl
from jax.experimental.pallas import tpu as pltpu
from jax.sharding import PartitionSpec as P

HEADS = 12
HEAD = 32
SIDE = 14
TOK = 196
TP = 208
GRID2 = 2 * SIDE
CELLS = 784
D_IN = 192
D = 384
FF = 1536
CROPS = 8
ROWS = TOK * CROPS
ROWS_P = TP * CROPS
LATE = 2048
REL = 27
TAB = 768
SPREAD = 384

EPS = 1e-05
FLOAT = jnp.float32
HALF = jnp.bfloat16
LOG2E = 1.4426950408889634
LN2 = 0.6931471805599453
SCALE = HEAD ** (-0.5)
NN = (((1,), (0,)), ((), ()))
NT = (((1,), (1,)), ((), ()))
TN = (((0,), (0,)), ((), ()))
VMEM_LIMIT = 56 * 1024 * 1024


def dot(left, right, dims=NN):
    return lax.dot_general(left, right, dims, preferred_element_type=FLOAT)


def split2(value):
    hi = value.astype(HALF)
    return hi, (value - hi.astype(FLOAT)).astype(HALF)


def params(limit=VMEM_LIMIT):
    return pltpu.CompilerParams(vmem_limit_bytes=limit)


def cost(flops, bytes_accessed, transcendentals=0):
    return pl.CostEstimate(
        flops=int(flops), bytes_accessed=int(bytes_accessed), transcendentals=int(transcendentals)
    )


def whole(shape):
    return pl.BlockSpec(shape, lambda *_: (0,) * len(shape))


CHUNKS = (
    (0, 48, 0, 256),
    (48, 80, 0, 512),
    (80, 112, 256, 512),
    (112, 144, 256, 768),
    (144, 176, 512, 768),
    (176, TP, 512, CELLS),
)
CELL_CHUNKS = ((0, 256, 0, 80), (256, 512, 48, 144), (512, CELLS, 112, TP))


def cell_of(part, token):
    i, j = divmod(token, SIDE)
    a, b = divmod(part, 2)
    return (2 * i + a) * GRID2 + 2 * j + b


def select_matrix():
    rows = []
    for first, last, low, high in CHUNKS:
        for part in range(4):
            block = np.zeros((last - first, CELLS), np.float32)
            for t in range(first, min(last, TOK)):
                assert low <= cell_of(part, t) < high
                block[t - first, cell_of(part, t)] = 1.0
            rows.append(block)
    return np.concatenate(rows)


def scatter_matrix():
    table = np.zeros((4 * TP, CELLS), np.float32)
    for low, high, first, last in CELL_CHUNKS:
        for part in range(4):
            for t in range(TOK):
                if low <= cell_of(part, t) < high:
                    assert first <= t < last
                    table[part * TP + t, cell_of(part, t)] = 1.0
    return table


def spread_matrix():
    table = np.zeros((SPREAD, TP), np.float32)
    for t in range(TOK):
        i, j = divmod(t, SIDE)
        table[REL * i + j, t] = 1.0
    return table


def stats_kernel(x_ref, out_ref):
    pieces = []
    step = 32
    for block in range(D_IN // step):
        rows = slice(block * step, (block + 1) * step)
        total = x_ref[0, rows, :].astype(FLOAT)
        for crop in range(1, CROPS):
            total = total + x_ref[crop, rows, :].astype(FLOAT)
        total = jnp.sum(total, axis=1, keepdims=True)
        mean = total * (1.0 / (CROPS * CELLS))
        square = jnp.zeros((step, CELLS), FLOAT)
        for crop in range(CROPS):
            centre = x_ref[crop, rows, :].astype(FLOAT) - mean
            square = square + centre * centre
        square = jnp.sum(square, axis=1, keepdims=True)
        lane = lax.broadcasted_iota(jnp.int32, (step, 128), 1)
        pieces.append(jnp.where(lane == 0, mean, jnp.where(lane == 1, square, 0.0)))
    turned = jnp.concatenate(pieces, axis=0).T
    pad = jnp.zeros((1, 64), FLOAT)
    row = jnp.concatenate([turned[0:1], pad, turned[1:2], pad], axis=1)
    out_ref[...] = jnp.broadcast_to(row[None], out_ref.shape)


def local_stats(cells, copies):
    return pl.pallas_call(
        stats_kernel,
        out_shape=jax.ShapeDtypeStruct((copies, 1, 512), FLOAT),
        compiler_params=params(),
        name="stats",
        cost_estimate=cost(8e6, 2.8e6),
    )(cells)


def batch_coefficients(gathered):
    count = gathered.shape[0]
    means = gathered[:, 0, 0:D_IN]
    squares = gathered[:, 0, 256 : 256 + D_IN]
    mean = jnp.sum(means, axis=0, keepdims=True) * (1.0 / count)
    off = means - mean
    local = float(CROPS * CELLS)
    var = jnp.sum(squares, axis=0, keepdims=True) + local * jnp.sum(
        off * off, axis=0, keepdims=True
    )
    return mean, lax.rsqrt(var * (1.0 / (local * count)) + EPS)


def select_kernel(s_ref, x_ref, out_ref):
    for k in range(x_ref.shape[0]):
        at = 0
        for first, last, low, high in CHUNKS:
            size = last - first
            picked = dot(s_ref[at : at + 4 * size, low:high], x_ref[k, :, low:high], NT).astype(HALF)
            for part in range(4):
                start = part * TP + first
                out_ref[k, start : start + size, :] = picked[part * size : (part + 1) * size]
            at += 4 * size


def select_cells(picks, cells):
    each = 2
    return pl.pallas_call(
        select_kernel,
        grid=(CROPS // each,),
        in_specs=[
            whole((4 * TP, CELLS)),
            pl.BlockSpec((each, D_IN, CELLS), lambda c: (c, 0, 0)),
        ],
        out_specs=pl.BlockSpec((each, 4 * TP, D_IN), lambda c: (c, 0, 0)),
        out_shape=jax.ShapeDtypeStruct((CROPS, 4 * TP, D_IN), HALF),
        compiler_params=params(),
        name="select_cells",
        cost_estimate=cost(3e9, 7e6),
    )(picks, cells)


def bias_kernel(table_ref, spread_ref, out_ref, rows_ref):
    row = lax.broadcasted_iota(jnp.int32, (TP, TP), 0)
    for head in range(HEADS):
        pad = jnp.zeros((1, TAB - REL * REL), FLOAT)
        table = jnp.concatenate([table_ref[head : head + 1, :] * LOG2E, pad], axis=1)
        base = pltpu.roll(jnp.broadcast_to(table, (16, TAB)), 0, 1, stride=1, stride_axis=0)
        for r in range(SIDE):
            rolled = pltpu.roll(base, (TAB - 364 + REL * r) % TAB, 1)
            rows_ref[head, SIDE * r : SIDE * (r + 1), :] = rolled[:SIDE, :SPREAD]
        rows_ref[head, TOK:, :] = jnp.zeros((TP - TOK, SPREAD), FLOAT)
        hi, lo = split2(rows_ref[head])
        value = dot(hi, spread_ref[...]) + dot(lo, spread_ref[...])
        out_ref[head] = jnp.where(row < TOK, value, -1e30)


def expand_bias(rel_table, spread):
    return pl.pallas_call(
        bias_kernel,
        in_specs=[whole((HEADS, REL * REL)), whole((SPREAD, TP))],
        out_specs=whole((HEADS, TP, TP)),
        out_shape=jax.ShapeDtypeStruct((HEADS, TP, TP), FLOAT),
        scratch_shapes=[pltpu.VMEM((HEADS, TP, SPREAD), FLOAT)],
        compiler_params=params(),
        name="expand_bias",
        cost_estimate=cost(2e9, 3e6),
    )(rel_table, spread)


def late_kernel(
    core_ref, dbias_ref, spread_ref, gw_ref, sums_ref, keep_ref, send_ref, rows_ref
):
    row = lax.broadcasted_iota(jnp.int32, (16, TAB), 0)
    lines = []
    for head in range(HEADS):
        hi, lo = split2(dbias_ref[head])
        rows_ref[head, :, :SPREAD] = dot(hi, spread_ref[...]) + dot(lo, spread_ref[...])
        rows_ref[head, :, SPREAD:] = jnp.zeros((TP, TAB - SPREAD), FLOAT)
        total = rows_ref[head, 0:16, :]
        for r in range(1, SIDE):
            piece = rows_ref[head, SIDE * r : SIDE * r + 16, :]
            total = total + pltpu.roll(piece, TAB - REL * r, 1)
        total = jnp.where(row < SIDE, total, 0.0)
        total = jnp.concatenate([total[c : c + 1, :] for c in range(15, -1, -1)], axis=0)
        total = pltpu.roll(total, 0, 1, stride=1, stride_axis=0)
        total = jnp.sum(total, axis=0, keepdims=True)
        total = pltpu.roll(total, 364 - 15, 1)
        lines += [total[:, k * 128 : (k + 1) * 128] for k in range(TAB // 128)]
    pad = jnp.zeros((1, 256 - D_IN), FLOAT)

    def wide(k):
        value = jnp.concatenate([sums_ref[k : k + 1, :], pad], axis=1)
        return [value[:, :128], value[:, 128:]]

    lines += wide(0) + wide(1)
    lines.append(jnp.zeros((80 - len(lines), 128), FLOAT))
    lines = jnp.concatenate(lines, axis=0)
    totals = jnp.concatenate(wide(2) + wide(3) + [jnp.zeros((4, 128), FLOAT)], axis=0)
    totals = jnp.broadcast_to(totals[None], (PIECES, 8, 128))
    blocks = [gw_ref[:, k * 128 : (k + 1) * 128] for k in range(9)]
    blocks = [block.reshape(D_IN // 32, 2, 16, 128) for block in blocks]

    def write(ref, half):
        size = D_IN // 32
        for k in range(9):
            ref[k * size : (k + 1) * size, 0:16, :] = blocks[k][:, half]
        at = 9 * size
        for piece in range(half, 5, 2):
            ref[at + piece // 2, 0:16, :] = lines[piece * 16 : (piece + 1) * 16, :]
        at += 3 - half
        ref[at:, 0:16, :] = jnp.zeros((PIECES - at, 16, 128), FLOAT)
        ref[:, 16:24, :] = totals

    @pl.when(core_ref[0] == 0)
    def _():
        write(keep_ref, 0)
        write(send_ref, 1)

    @pl.when(core_ref[0] != 0)
    def _():
        write(keep_ref, 1)
        write(send_ref, 0)


def late_message(core, dbias, spread, gw, sums):
    shape = (PIECES, 24, 128)
    return pl.pallas_call(
        late_kernel,
        in_specs=[pl.BlockSpec(memory_space=pltpu.SMEM)]
        + [whole(a.shape) for a in (dbias, spread, gw, sums)],
        out_specs=[whole(shape)] * 2,
        out_shape=[jax.ShapeDtypeStruct(shape, FLOAT)] * 2,
        scratch_shapes=[pltpu.VMEM((HEADS, TP, TAB), FLOAT)],
        compiler_params=params(),
        name="late_message",
        cost_estimate=cost(2e9, 5e6),
    )(core, dbias, spread, gw, sums)


def line(ref):
    return ref[...].reshape(1, ref.shape[0])


def bn_parts(x_ref, coef_ref, scale_ref, bias_ref):
    mean = coef_ref[0:1, :]
    factor = coef_ref[1:2, :] * line(scale_ref) * LOG2E
    shift = line(bias_ref) * LOG2E
    return [
        (x_ref[0, part * TP : (part + 1) * TP, :].astype(FLOAT) - mean) * factor + shift
        for part in range(4)
    ]


def norm_rows(value):
    centre = value - jnp.mean(value, axis=-1, keepdims=True)
    inverse = lax.rsqrt(jnp.mean(centre * centre, axis=-1, keepdims=True) + EPS)
    return centre * inverse, inverse


def put_rows(ref, crop, value):
    for group in range(ref.shape[0]):
        piece = value[:, group * 128 : (group + 1) * 128]
        if piece.shape[1] < 128:
            rest = jnp.zeros((piece.shape[0], 128 - piece.shape[1]), piece.dtype)
            piece = jnp.concatenate([piece, rest], axis=1)
        ref[group, pl.ds(crop, TP, stride=CROPS), :] = piece


def take_rows(ref, crop):
    pieces = [ref[group, pl.ds(crop, TP, stride=CROPS), :] for group in range(ref.shape[0])]
    return jnp.concatenate(pieces, axis=1)


def head_masks():
    lane = lax.broadcasted_iota(jnp.int32, (1, 128), 1)
    return [(lane // HEAD == k).astype(HALF) for k in range(4)]


def attention_kernel(
    gathered_ref,
    x_ref,
    bn_scale_ref,
    bn_bias_ref,
    gain_ref,
    shift_ref,
    w_ref,
    bias_ref,
    qkv_ref,
    probs_ref,
    attn_ref,
    pooled_ref,
    plain_ref,
    coef_ref,
    s_ref,
):
    crop = pl.program_id(0)

    @pl.when(crop == 0)
    def _():
        mean, inv = batch_coefficients(gathered_ref[...])
        coef_ref[...] = jnp.zeros_like(coef_ref)
        coef_ref[0:1, :] = mean
        coef_ref[1:2, :] = inv

    parts = bn_parts(x_ref, coef_ref, bn_scale_ref, bn_bias_ref)
    top = jnp.maximum(jnp.maximum(parts[0], parts[1]), jnp.maximum(parts[2], parts[3]))
    total = jnp.exp2(parts[0] - top)
    for part in range(1, 4):
        total = total + jnp.exp2(parts[part] - top)
    pooled = top * LN2 + jnp.log(total)
    put_rows(pooled_ref, crop, pooled)
    plain_ref[0] = pooled
    z, _ = norm_rows(pooled)
    first = (z * line(gain_ref) + line(shift_ref)).astype(HALF)
    qkv_ref[0] = dot(first, w_ref[...]).astype(HALF)
    value_t = qkv_ref[0, :, 2 * D :].astype(FLOAT).T.astype(HALF)
    masks = head_masks()

    def start(head):
        group = head // 4
        query = qkv_ref[0, :, group * 128 : (group + 1) * 128] * masks[head % 4]
        key = qkv_ref[0, :, D + group * 128 : D + (group + 1) * 128]
        s_ref[head % 3] = dot(key, query, NT)

    def finish(head):
        rows = slice(head * HEAD, (head + 1) * HEAD)
        return dot(value_t[rows, :], probs_ref[0, head])

    heads = []
    start(0)
    for head in range(HEADS):
        if head + 1 < HEADS:
            start(head + 1)
        for cols in (slice(0, 128), slice(128, TP)):
            scores = s_ref[head % 3, :, cols] * (SCALE * LOG2E) + bias_ref[head, :, cols]
            weight = jnp.exp2(scores - jnp.max(scores, axis=0, keepdims=True))
            weight = weight * (1.0 / jnp.sum(weight, axis=0, keepdims=True))
            probs_ref[0, head, :, cols] = weight.astype(HALF)
        if head > 0:
            heads.append(finish(head - 1))
    heads.append(finish(HEADS - 1))
    put_rows(attn_ref, crop, jnp.concatenate(heads, axis=0).T)


def attention(gathered, picked, bn_scale, bn_bias, gain, shift, w_qkv, bias):
    return pl.pallas_call(
        attention_kernel,
        grid=(CROPS,),
        in_specs=[
            whole(gathered.shape),
            pl.BlockSpec((1, 4 * TP, D_IN), lambda c: (c, 0, 0)),
            whole((D_IN,)),
            whole((D_IN,)),
            whole((D_IN,)),
            whole((D_IN,)),
            whole((D_IN, 3 * D)),
            whole((HEADS, TP, TP)),
        ],
        out_specs=[
            pl.BlockSpec((1, TP, 3 * D), lambda c: (c, 0, 0)),
            pl.BlockSpec((1, HEADS, TP, TP), lambda c: (c, 0, 0, 0)),
            whole((3, ROWS_P, 128)),
            whole((2, ROWS_P, 128)),
            pl.BlockSpec((1, TP, D_IN), lambda c: (c, 0, 0)),
            whole((8, D_IN)),
        ],
        out_shape=[
            jax.ShapeDtypeStruct((CROPS, TP, 3 * D), HALF),
            jax.ShapeDtypeStruct((CROPS, HEADS, TP, TP), HALF),
            jax.ShapeDtypeStruct((3, ROWS_P, 128), FLOAT),
            jax.ShapeDtypeStruct((2, ROWS_P, 128), FLOAT),
            jax.ShapeDtypeStruct((CROPS, TP, D_IN), FLOAT),
            jax.ShapeDtypeStruct((8, D_IN), FLOAT),
        ],
        scratch_shapes=[pltpu.VMEM((3, TP, TP), FLOAT)],
        compiler_params=params(),
        name="attention",
        cost_estimate=cost(4e9, 2.5e7, 4e6),
    )(gathered, picked, bn_scale, bn_bias, gain, shift, w_qkv, bias)


def normal_parts(u):
    cdf = lax.erf(u * np.float32(np.sqrt(0.5))) * 0.5 + 0.5
    return cdf, jnp.exp2(u * u * (-0.5 * LOG2E)) * (u * np.float32(1.0 / np.sqrt(2 * np.pi)))


PIECES = 64
EARLY = 88
HALF_ROWS = PIECES * EARLY
BOTH = EARLY + 16
AT_OUT0 = FF // 128 * D
AT_SHORT0 = AT_OUT0 + 2 * D
AT_SUMS = AT_SHORT0 + D_IN
AT_OUT1 = FF // 128 * D
AT_SHORT1 = AT_OUT1 + D

FC_COLS = 768


def feed_kernel(
    core_ref,
    attn_ref,
    pooled_ref,
    cot_ref,
    w_short_ref,
    w_out_ref,
    gain_ref,
    shift_ref,
    w1_ref,
    b1_ref,
    w2_ref,
    b2_ref,
    out_ref,
    dattn_ref,
    dshort_ref,
    shared_ref,
    keep_ref,
    send_ref,
    message_ref,
    sems,
):
    core = core_ref[0]
    first_half, second_half = 0, 1

    def put(half, at, value):
        count = value.shape[0]
        for k in range(value.shape[1] // 128):
            message_ref[half, at + k * count : at + (k + 1) * count, :] = value[
                :, k * 128 : (k + 1) * 128
            ]

    shipped = []

    def ship(half, at, end):
        sem = sems.at[len(shipped)]
        rows = pl.ds(at, end - at)
        to_keep = pltpu.make_async_copy(message_ref.at[half, rows], keep_ref.at[rows], sem)
        to_send = pltpu.make_async_copy(message_ref.at[half, rows], send_ref.at[rows], sem)

        @pl.when(core == half)
        def _():
            to_keep.start()

        @pl.when(core != half)
        def _():
            to_send.start()

        shipped.append(to_keep)

    attn_wide = jnp.concatenate([attn_ref[k, :ROWS] for k in range(3)], axis=1)
    pooled_wide = jnp.concatenate([pooled_ref[k, :ROWS] for k in range(2)], axis=1)[:, :D_IN]
    cot = cot_ref[...]
    y1 = dot(pooled_wide.astype(HALF), w_short_ref[...]) + dot(
        attn_wide.astype(HALF), w_out_ref[...]
    )
    z, inverse = norm_rows(y1)
    gain = line(gain_ref)
    second = (z * gain + line(shift_ref)).astype(HALF)
    out = y1 + line(b2_ref)
    b1 = line(b1_ref)
    back = jnp.zeros((ROWS, D), FLOAT)
    second_t = second.astype(FLOAT).T.astype(HALF)
    cot_t = cot.astype(FLOAT).T.astype(HALF)
    sums1 = []
    for block in range(FF // FC_COLS):
        cols = slice(block * FC_COLS, (block + 1) * FC_COLS)
        u = dot(second, w1_ref[:, cols]) + b1[:, cols]
        cdf, slope = normal_parts(u)
        hidden = (u * cdf).astype(HALF)
        dhidden = dot(cot, w2_ref[cols, :], NT)
        du = dhidden * (cdf + slope)
        sums1.append(jnp.sum(du, axis=0, keepdims=True))
        du = du.astype(HALF)
        out = out + dot(hidden, w2_ref[cols, :])
        back = back + dot(du, w1_ref[:, cols], NT)
        at = block * (FC_COLS // 128) * D
        put(first_half, at, dot(second_t, du))
        put(second_half, at, dot(cot_t, hidden))
        ship(first_half, at, at + FC_COLS // 128 * D)
        ship(second_half, at, at + FC_COLS // 128 * D)
    out_ref[...] = out
    wide_cot = cot.astype(FLOAT)
    dz = back * gain
    dy1 = wide_cot + inverse * (
        dz
        - jnp.mean(dz, axis=-1, keepdims=True)
        - z * jnp.mean(dz * z, axis=-1, keepdims=True)
    )
    low = dy1.astype(HALF)
    dattn = dot(low, w_out_ref[...], NT).astype(HALF).astype(FLOAT)
    for k in range(3):
        dattn_ref[k, :ROWS, :] = dattn[:, k * 128 : (k + 1) * 128]
    dattn_ref[:, ROWS:, :] = jnp.zeros((3, ROWS_P - ROWS, 128), FLOAT)
    dshort = dot(low, w_short_ref[...], NT)
    dshort_ref[0, :ROWS, :] = dshort[:, :128]
    dshort_ref[1, :ROWS, :] = jnp.concatenate(
        [dshort[:, 128:], jnp.zeros((ROWS, 256 - D_IN), FLOAT)], axis=1
    )
    dshort_ref[:, ROWS:, :] = jnp.zeros((2, ROWS_P - ROWS, 128), FLOAT)
    lane = lax.broadcasted_iota(jnp.int32, (D, 128), 0) // HEAD
    column = lax.broadcasted_iota(jnp.int32, (D, 128), 1)
    ones = (lane == column).astype(HALF)
    product = attn_wide * dattn
    high = product.astype(HALF)
    rest = (product - high.astype(FLOAT)).astype(HALF)
    shared_ref[:ROWS, :] = dot(high, ones) + dot(rest, ones)
    shared_ref[ROWS:, :] = jnp.zeros((ROWS_P - ROWS, 128), FLOAT)
    gout = dot(attn_wide.T.astype(HALF), low)
    put(first_half, AT_OUT0, gout[:, : 2 * 128])
    put(second_half, AT_OUT1, gout[:, 2 * 128 :])
    gshort = dot(pooled_wide.T.astype(HALF), low)
    put(first_half, AT_SHORT0, gshort[:, :128])
    put(second_half, AT_SHORT1, gshort[:, 128:])
    lines = [
        jnp.sum(back * z, axis=0, keepdims=True),
        jnp.sum(back, axis=0, keepdims=True),
        jnp.sum(wide_cot, axis=0, keepdims=True),
    ]
    flat = jnp.concatenate(sums1 + lines, axis=1)
    pieces = [flat[:, k * 128 : (k + 1) * 128] for k in range((FF + 3 * D) // 128)]
    pieces.append(jnp.zeros((3, 128), FLOAT))
    put(first_half, AT_SUMS, jnp.concatenate(pieces, axis=0))
    end0 = AT_SUMS + 24
    end1 = AT_SHORT1 + 2 * D_IN
    put(first_half, end0, jnp.zeros((HALF_ROWS - end0, 128), FLOAT))
    put(second_half, end1, jnp.zeros((HALF_ROWS - end1, 128), FLOAT))
    ship(first_half, AT_OUT0, HALF_ROWS)
    ship(second_half, AT_OUT1, HALF_ROWS)
    for copy in shipped:
        copy.wait()


def feed_forward(core, attn, pooled, cot, w_short, w_out, gain, shift, w1, b1, w2, b2):
    out_shapes = [
        (ROWS, D),
        (3, ROWS_P, 128),
        (2, ROWS_P, 128),
        (ROWS_P, 128),
        (HALF_ROWS, 128),
        (HALF_ROWS, 128),
    ]
    arrays = (attn, pooled, cot, w_short, w_out, gain, shift, w1, b1, w2, b2)
    return pl.pallas_call(
        feed_kernel,
        in_specs=[pl.BlockSpec(memory_space=pltpu.SMEM)] + [whole(a.shape) for a in arrays],
        out_specs=[whole(shape) for shape in out_shapes[:-2]]
        + [pl.BlockSpec(memory_space=pl.ANY)] * 2,
        out_shape=[jax.ShapeDtypeStruct(shape, FLOAT) for shape in out_shapes],
        scratch_shapes=[
            pltpu.VMEM((2, HALF_ROWS, 128), FLOAT),
            pltpu.SemaphoreType.DMA((2 * FF // FC_COLS + 2,)),
        ],
        compiler_params=params(),
        name="feed_forward",
        cost_estimate=cost(1.2e10, 2e7, 3e6),
    )(core, *arrays)


def rows_sum(ref):
    total = ref[0]
    for k in range(1, ref.shape[0]):
        total = total + ref[k]
    return total


def early_sum_kernel(pieces_ref, out_ref):
    out_ref[...] = rows_sum(pieces_ref)


def early_sum(pieces):
    return pl.pallas_call(
        early_sum_kernel,
        in_specs=[whole(pieces.shape)],
        out_specs=whole(pieces.shape[1:]),
        out_shape=jax.ShapeDtypeStruct(pieces.shape[1:], FLOAT),
        compiler_params=params(),
        name="early_sum",
        cost_estimate=cost(1e6, 3e6),
    )(pieces)


def add_kernel(after_ref, a_ref, b_ref, out_ref):
    out_ref[...] = a_ref[...] + b_ref[...]


def add_after(after, a, b):
    return pl.pallas_call(
        add_kernel,
        in_specs=[pl.BlockSpec(memory_space=pl.ANY), whole(a.shape), whole(b.shape)],
        out_specs=whole(a.shape),
        out_shape=jax.ShapeDtypeStruct(a.shape, FLOAT),
        compiler_params=params(),
        name="add_after",
        cost_estimate=cost(a.size, 12 * a.size),
    )(after, a, b)


def copies_kernel(after_ref, early_ref, late_ref, copies_ref, totals_ref):
    late = rows_sum(late_ref)
    both = jnp.concatenate([early_ref[...], late[:16]], axis=0)
    copies_ref[...] = jnp.broadcast_to(both[None], copies_ref.shape)
    totals_ref[...] = late[16:24]


def sum_and_copy(after, early, late):
    shapes = [(PIECES, BOTH, 128), (8, 128)]
    return pl.pallas_call(
        copies_kernel,
        in_specs=[pl.BlockSpec(memory_space=pl.ANY), whole(early.shape), whole(late.shape)],
        out_specs=[whole(shape) for shape in shapes],
        out_shape=[jax.ShapeDtypeStruct(shape, FLOAT) for shape in shapes],
        compiler_params=params(),
        name="sum_and_copy",
        cost_estimate=cost(1e6, 5e6),
    )(after, early, late)


def touch_kernel(after_ref, in_ref, out_ref):
    del after_ref, in_ref, out_ref


def pass_after(after, value):
    return pl.pallas_call(
        touch_kernel,
        in_specs=[pl.BlockSpec(memory_space=pl.ANY)] * 2,
        out_specs=pl.BlockSpec(memory_space=pl.ANY),
        out_shape=jax.ShapeDtypeStruct(value.shape, value.dtype),
        input_output_aliases={1: 0},
        compiler_params=params(),
        name="pass_after",
        cost_estimate=cost(1, 1),
    )(after, value)


def unpack_kernel(
    core_ref,
    own_ref,
    other_ref,
    g1_ref,
    g2_ref,
    gout_ref,
    gshort_ref,
    db1_ref,
    dgain2_ref,
    dshift2_ref,
    db2_ref,
    gqkv_ref,
    table_ref,
    dgain1_ref,
    dshift1_ref,
):
    def read(ref, at, count):
        pieces = []
        while count:
            piece, row = divmod(at, EARLY)
            size = min(count, EARLY - row)
            pieces.append(ref[piece, row : row + size, :])
            at, count = at + size, count - size
        return pieces[0] if len(pieces) == 1 else jnp.concatenate(pieces, axis=0)

    def first(ref):
        for k in range(FF // 128):
            g1_ref[:, k * 128 : (k + 1) * 128] = read(ref, k * D, D)
        for k in range(2):
            gout_ref[:, k * 128 : (k + 1) * 128] = read(ref, AT_OUT0 + k * D, D)
        gshort_ref[:, :128] = read(ref, AT_SHORT0, D_IN)
        lines = read(ref, AT_SUMS, 24)
        flat = jnp.concatenate([lines[k : k + 1, :] for k in range(21)], axis=1)
        db1_ref[...] = flat[:, :FF].reshape(FF)
        for k, target in enumerate((dgain2_ref, dshift2_ref, db2_ref)):
            target[...] = flat[:, FF + k * D : FF + (k + 1) * D].reshape(D)

    def second(ref):
        for k in range(FF // 128):
            g2_ref[k * 128 : (k + 1) * 128, :] = read(ref, k * D, D).T
        gout_ref[:, 2 * 128 :] = read(ref, AT_OUT1, D)
        for k in range(2):
            gshort_ref[:, (k + 1) * 128 : (k + 2) * 128] = read(ref, AT_SHORT1 + k * D_IN, D_IN)

    def late(refs):
        def read_late(at, count):
            pieces = []
            for d in range(at // 16, (at + count) // 16):
                pieces.append(refs[d % 2][d // 2, EARLY:BOTH, :])
            return jnp.concatenate(pieces, axis=0)

        for k in range(9):
            gqkv_ref[:, k * 128 : (k + 1) * 128] = read_late(k * D_IN, D_IN)
        lines = read_late(9 * D_IN, 80)
        per = TAB // 128
        columns = []
        for k in range(per):
            rows = [lines[h * per + k : h * per + k + 1, :] for h in range(HEADS)]
            columns.append(jnp.concatenate(rows, axis=0))
        table_ref[...] = jnp.concatenate(columns, axis=1)[:, : REL * REL]
        for k, target in enumerate((dgain1_ref, dshift1_ref)):
            at = HEADS * per + 2 * k
            both = jnp.concatenate([lines[at : at + 1, :], lines[at + 1 : at + 2, :]], axis=1)
            target[...] = both[:, :D_IN].reshape(D_IN)

    @pl.when(core_ref[0] == 0)
    def _():
        first(own_ref)
        second(other_ref)
        late((own_ref, other_ref))

    @pl.when(core_ref[0] != 0)
    def _():
        first(other_ref)
        second(own_ref)
        late((other_ref, own_ref))


def unpack(core, own, other):
    shapes = [
        (D, FF),
        (FF, D),
        (D, D),
        (D_IN, D),
        (FF,),
        (D,),
        (D,),
        (D,),
        (D_IN, 3 * D),
        (HEADS, REL * REL),
        (D_IN,),
        (D_IN,),
    ]
    return pl.pallas_call(
        unpack_kernel,
        in_specs=[
            pl.BlockSpec(memory_space=pltpu.SMEM),
            whole((PIECES, BOTH, 128)),
            whole((PIECES, BOTH, 128)),
        ],
        out_specs=[whole(shape) for shape in shapes],
        out_shape=[jax.ShapeDtypeStruct(shape, FLOAT) for shape in shapes],
        compiler_params=params(),
        name="unpack",
        cost_estimate=cost(1e6, 1.2e7),
    )(core, own, other)


def back_kernel(
    after_ref,
    coef_ref,
    x_ref,
    plain_ref,
    qkv_ref,
    probs_ref,
    dattn_ref,
    dshort_ref,
    shared_ref,
    bn_scale_ref,
    bn_bias_ref,
    gain_ref,
    shift_ref,
    w_ref,
    dbias_ref,
    gw_ref,
    sums_ref,
    dcells_ref,
    dp_ref,
    ds_ref,
):
    crop = pl.program_id(0)

    @pl.when(crop == 0)
    def _():
        dbias_ref[...] = jnp.zeros_like(dbias_ref)
        gw_ref[...] = jnp.zeros_like(gw_ref)
        sums_ref[...] = jnp.zeros_like(sums_ref)

    dattn = take_rows(dattn_ref, crop).astype(HALF)
    shared = shared_ref[pl.ds(crop, TP, stride=CROPS), :].T
    key_t = qkv_ref[0, :, D : 2 * D].astype(FLOAT).T.astype(HALF)
    masks = head_masks()
    dquery_t, dkeys, dvalues = [], [], []

    def start(head):
        group = head // 4
        grad = dattn[:, group * 128 : (group + 1) * 128] * masks[head % 4]
        value = qkv_ref[0, :, 2 * D + group * 128 : 2 * D + (group + 1) * 128]
        dp_ref[head % 3] = dot(value, grad, NT)
        dvalues.append(dot(probs_ref[0, head], grad))

    def finish(head):
        group = head // 4
        query = qkv_ref[0, :, group * 128 : (group + 1) * 128] * masks[head % 4]
        dscores = ds_ref[head % 2]
        dkeys.append(dot(dscores, query))
        dquery_t.append(dot(key_t[head * HEAD : (head + 1) * HEAD, :], dscores))

    start(0)
    for head in range(HEADS):
        if head + 1 < HEADS:
            start(head + 1)
        for cols in (slice(0, 128), slice(128, TP)):
            probs = probs_ref[0, head, :, cols].astype(FLOAT)
            dscores = probs * (dp_ref[head % 3, :, cols] - shared[head : head + 1, cols])
            dbias_ref[head, :, cols] += dscores
            ds_ref[head % 2, :, cols] = dscores.astype(HALF)
        if head > 0:
            finish(head - 1)
    finish(HEADS - 1)
    group_sum = lambda items, g: sum(items[4 * g + 1 : 4 * g + 4], items[4 * g])
    dquery = jnp.concatenate(dquery_t, axis=0).T * SCALE
    dqkv = jnp.concatenate(
        [dquery]
        + [group_sum(dkeys, g) * SCALE for g in range(3)]
        + [group_sum(dvalues, g) for g in range(3)],
        axis=1,
    ).astype(HALF)
    pooled = plain_ref[0]
    z, inverse = norm_rows(pooled)
    gain = line(gain_ref)
    first_t = (z * gain + line(shift_ref)).T.astype(HALF)
    gw_ref[...] += dot(first_t, dqkv)
    dfirst = dot(dqkv, w_ref[...], NT)
    dz = dfirst * gain
    dpooled = take_rows(dshort_ref, crop)[:, :D_IN] + inverse * (
        dz
        - jnp.mean(dz, axis=-1, keepdims=True)
        - z * jnp.mean(dz * z, axis=-1, keepdims=True)
    )
    sums_ref[0:1, :] += jnp.sum(dfirst * z, axis=0, keepdims=True)
    sums_ref[1:2, :] += jnp.sum(dfirst, axis=0, keepdims=True)
    level = pooled * LOG2E
    parts = bn_parts(x_ref, coef_ref, bn_scale_ref, bn_bias_ref)
    along = jnp.zeros((TP, D_IN), FLOAT)
    total = jnp.zeros((TP, D_IN), FLOAT)
    for part in range(4):
        dpart = dpooled * jnp.exp2(parts[part] - level)
        dcells_ref[0, part * TP : (part + 1) * TP, :] = dpart.astype(HALF)
        raw = x_ref[0, part * TP : (part + 1) * TP, :].astype(FLOAT)
        along = along + dpart * (raw - coef_ref[0:1, :])
        total = total + dpart
    sums_ref[2:3, :] += jnp.sum(along, axis=0, keepdims=True) * coef_ref[1:2, :]
    sums_ref[3:4, :] += jnp.sum(total, axis=0, keepdims=True)


def attention_back(
    after, coef, picked, plain, qkv, probs, dattn, dshort, shared, bn_scale, bn_bias, gain, shift, w_qkv
):
    return pl.pallas_call(
        back_kernel,
        grid=(CROPS,),
        in_specs=[
            pl.BlockSpec(memory_space=pl.ANY),
            whole((8, D_IN)),
            pl.BlockSpec((1, 4 * TP, D_IN), lambda c: (c, 0, 0)),
            pl.BlockSpec((1, TP, D_IN), lambda c: (c, 0, 0)),
            pl.BlockSpec((1, TP, 3 * D), lambda c: (c, 0, 0)),
            pl.BlockSpec((1, HEADS, TP, TP), lambda c: (c, 0, 0, 0)),
            whole((3, ROWS_P, 128)),
            whole((2, ROWS_P, 128)),
            whole((ROWS_P, 128)),
            whole((D_IN,)),
            whole((D_IN,)),
            whole((D_IN,)),
            whole((D_IN,)),
            whole((D_IN, 3 * D)),
        ],
        out_specs=[
            whole((HEADS, TP, TP)),
            whole((D_IN, 3 * D)),
            whole((8, D_IN)),
            pl.BlockSpec((1, 4 * TP, D_IN), lambda c: (c, 0, 0)),
        ],
        out_shape=[
            jax.ShapeDtypeStruct((HEADS, TP, TP), FLOAT),
            jax.ShapeDtypeStruct((D_IN, 3 * D), FLOAT),
            jax.ShapeDtypeStruct((8, D_IN), FLOAT),
            jax.ShapeDtypeStruct((CROPS, 4 * TP, D_IN), HALF),
        ],
        scratch_shapes=[pltpu.VMEM((3, TP, TP), FLOAT), pltpu.VMEM((2, TP, TP), HALF)],
        compiler_params=params(),
        name="attention_back",
        cost_estimate=cost(6e9, 4e7, 2e6),
    )(after, coef, picked, plain, qkv, probs, dattn, dshort, shared, bn_scale, bn_bias, gain, shift, w_qkv)


def scatter_kernel(s_ref, d_ref, out_ref):
    for k in range(d_ref.shape[0]):
        for low, high, first, last in CELL_CHUNKS:
            value = None
            for part in range(4):
                rows = slice(part * TP + first, part * TP + last)
                term = dot(d_ref[k, rows, :], s_ref[rows, low:high], TN)
                value = term if value is None else value + term
            out_ref[k, :, low:high] = value.astype(HALF)


def scatter_cells(places, dcells):
    each = 2
    return pl.pallas_call(
        scatter_kernel,
        grid=(CROPS // each,),
        in_specs=[
            whole((4 * TP, CELLS)),
            pl.BlockSpec((each, 4 * TP, D_IN), lambda c: (c, 0, 0)),
        ],
        out_specs=pl.BlockSpec((each, D_IN, CELLS), lambda c: (c, 0, 0)),
        out_shape=jax.ShapeDtypeStruct((CROPS, D_IN, CELLS), HALF),
        compiler_params=params(),
        name="scatter_cells",
        cost_estimate=cost(3e9, 8e6),
    )(places, dcells)


def column(row):
    return jnp.broadcast_to(row, (128, D_IN)).T[:, 0:1]


def cells_kernel(count, totals_ref, coef_ref, scale_ref, d_ref, x_ref, out_ref, dscale_ref, dshift_ref, cols_ref):
    @pl.when(pl.program_id(0) == 0)
    def _():
        rest = slice(0, D_IN - 128)
        along = jnp.concatenate([totals_ref[0:1, :], totals_ref[1:2, rest]], axis=1)
        plain = jnp.concatenate([totals_ref[2:3, :], totals_ref[3:4, rest]], axis=1)
        dscale_ref[...] = along.reshape(D_IN)
        dshift_ref[...] = plain.reshape(D_IN)
        mean = coef_ref[0:1, :]
        inv = coef_ref[1:2, :]
        factor = inv * line(scale_ref)
        share = 1.0 / float(count * CROPS * CELLS)
        slope = factor * along * inv * share
        cols_ref[:, 0:1] = column(factor)
        cols_ref[:, 1:2] = column(factor * plain * share)
        cols_ref[:, 2:3] = column(slope)
        cols_ref[:, 3:4] = column(mean)

    out_ref[0] = (
        d_ref[0].astype(FLOAT) * cols_ref[:, 0:1]
        - cols_ref[:, 1:2]
        - (x_ref[0].astype(FLOAT) - cols_ref[:, 3:4]) * cols_ref[:, 2:3]
    )


def cell_gradient(count, totals, coef, bn_scale, dcells, cells):
    crop_block = pl.BlockSpec((1, D_IN, CELLS), lambda c: (c, 0, 0))
    return pl.pallas_call(
        functools.partial(cells_kernel, count),
        grid=(CROPS,),
        in_specs=[
            whole((8, 128)),
            whole((8, D_IN)),
            whole((D_IN,)),
            crop_block,
            crop_block,
        ],
        out_specs=[crop_block, whole((D_IN,)), whole((D_IN,))],
        out_shape=[
            jax.ShapeDtypeStruct((CROPS, D_IN, CELLS), FLOAT),
            jax.ShapeDtypeStruct((D_IN,), FLOAT),
            jax.ShapeDtypeStruct((D_IN,), FLOAT),
        ],
        scratch_shapes=[pltpu.VMEM((D_IN, 128), FLOAT)],
        compiler_params=params(),
        name="cell_gradient",
        cost_estimate=cost(1e7, 1.5e7),
    )(totals, coef, bn_scale, dcells, cells)


CHIPS = ("y", "x", "z")
ALL = ("y", "x", "z", "core")


def gather_rows(copies):
    if copies.shape[0] == 1:
        return copies
    return lax.all_to_all(copies, ALL, 0, 0)


def on_device(
    count,
    features,
    bn_scale,
    bn_bias,
    w_short,
    ln1_gain,
    ln1_bias,
    w_qkv,
    rel_table,
    w_out,
    ln2_gain,
    ln2_bias,
    w_fc1,
    fc1_bias,
    w_fc2,
    fc2_bias,
    cotangent,
):
    picks = jnp.asarray(select_matrix(), HALF)
    places = jnp.asarray(scatter_matrix(), HALF)
    spread = jnp.asarray(spread_matrix(), HALF)
    spread_back = jnp.asarray(spread_matrix().T, HALF)
    core = lax.axis_index("core").astype(jnp.int32).reshape(1)
    cells = features.transpose(0, 2, 1)
    cot = cotangent.transpose(1, 0, 2).reshape(ROWS, D)
    stats = gather_rows(local_stats(cells, count))
    picked = select_cells(picks, cells)
    bias = expand_bias(rel_table, spread)
    qkv, probs, attn, pooled, plain, coef = attention(
        stats, picked, bn_scale, bn_bias, ln1_gain, ln1_bias, w_qkv, bias
    )
    out, dattn, dshort, shared, keep, send = feed_forward(
        core,
        attn,
        pooled,
        cot,
        w_short,
        w_out,
        ln2_gain,
        ln2_bias,
        w_fc1,
        fc1_bias,
        w_fc2,
        fc2_bias,
    )
    swap = [(0, 1), (1, 0)]
    mine = keep if count == 1 else keep + lax.ppermute(send, "core", swap)
    pieces = mine.reshape(PIECES, EARLY, 128)
    if count > 1:
        pieces = lax.all_to_all(pieces, CHIPS, 0, 0)
    dbias, gqkv, sums, dcells = attention_back(
        mine,
        coef,
        picked,
        plain,
        qkv,
        probs,
        dattn,
        dshort,
        shared,
        bn_scale,
        bn_bias,
        ln1_gain,
        ln1_bias,
        w_qkv,
    )
    late_keep, late_send = late_message(core, dbias, spread_back, gqkv, sums)
    scattered = scatter_cells(places, dcells)
    if count > 1:
        late = add_after(pieces, late_keep, lax.ppermute(late_send, "core", swap))
        late = lax.all_to_all(late, CHIPS, 0, 0)
        copies, totals = sum_and_copy(scattered, early_sum(pieces), late)
        own = lax.all_to_all(copies, CHIPS, 0, 0)
    else:
        totals = late_keep[0, 16:24]
    grad_cells, dscale, dshift = cell_gradient(count, totals, coef, bn_scale, scattered, cells)
    if count > 1:
        own = pass_after(grad_cells, own)
        other = lax.ppermute(own, "core", swap)
    else:
        own = jnp.concatenate([pieces, late_keep[:, :16]], axis=1)
        other = jnp.concatenate([send.reshape(PIECES, EARLY, 128), late_send[:, :16]], axis=1)
    g1, g2, gout, gshort, db1, dgain2, dshift2, db2, gqkv, table, dgain1, dshift1 = unpack(
        core, own, other
    )
    return (
        out.reshape(TOK, CROPS, D).transpose(1, 0, 2),
        grad_cells.transpose(0, 2, 1),
        dscale,
        dshift,
        gshort,
        dgain1,
        dshift1,
        gqkv,
        table,
        gout,
        dgain2,
        dshift2,
        g1,
        db1,
        g2,
        db2,
    )


def solution(mesh):
    count = mesh.size
    shape = (4, 4, 4, 2) if count == 128 else (1, 1, 1, 1)
    grid = jax.sharding.Mesh(mesh.devices.reshape(shape), ALL)
    split = P(ALL, None, None)
    same = P()
    in_specs = (split,) + (same,) * 14 + (split,)
    out_specs = (split, split) + (same,) * 14

    def run(*args):
        return on_device(count, *args)

    return jax.shard_map(run, mesh=grid, in_specs=in_specs, out_specs=out_specs, check_vma=False)
```

```python
import functools

import jax
import jax.numpy as jnp
import numpy as np
from jax import lax
from jax.experimental import pallas as pl
from jax.experimental.pallas import tpu as pltpu
from jax.sharding import PartitionSpec as P

HEADS = 12
HEAD = 32
SIDE = 14
TOK = 196
TP = 208
GRID2 = 2 * SIDE
CELLS = 784
D_IN = 192
D = 384
FF = 1536
CROPS = 8
ROWS = TOK * CROPS
ROWS_P = TP * CROPS
REL = 27
TAB = 768
SPREAD = 384

EPS = 1e-05
FLOAT = jnp.float32
HALF = jnp.bfloat16
LOG2E = 1.4426950408889634
LN2 = 0.6931471805599453
SCALE = HEAD ** (-0.5)
NN = (((1,), (0,)), ((), ()))
NT = (((1,), (1,)), ((), ()))
TN = (((0,), (0,)), ((), ()))
VMEM_LIMIT = 64000000


def dot(left, right, dims=NN):
    return lax.dot_general(left, right, dims, preferred_element_type=FLOAT)


def split2(value):
    hi = value.astype(HALF)
    return hi, (value - hi.astype(FLOAT)).astype(HALF)


def params(limit=VMEM_LIMIT):
    return pltpu.CompilerParams(vmem_limit_bytes=limit)


def cost(flops, bytes_accessed, transcendentals=0):
    return pl.CostEstimate(
        flops=int(flops), bytes_accessed=int(bytes_accessed), transcendentals=int(transcendentals)
    )


def whole(shape):
    return pl.BlockSpec(shape, lambda *_: (0,) * len(shape))


CHUNKS = (
    (0, 48, 0, 256),
    (48, 80, 0, 512),
    (80, 112, 256, 512),
    (112, 144, 256, 768),
    (144, 176, 512, 768),
    (176, TP, 512, CELLS),
)
CELL_CHUNKS = ((0, 256, 0, 80), (256, 512, 48, 144), (512, CELLS, 112, TP))


def cell_of(part, token):
    i, j = divmod(token, SIDE)
    a, b = divmod(part, 2)
    return (2 * i + a) * GRID2 + 2 * j + b


def select_matrix():
    rows = []
    for first, last, low, high in CHUNKS:
        for part in range(4):
            block = np.zeros((last - first, CELLS), np.float32)
            for t in range(first, min(last, TOK)):
                assert low <= cell_of(part, t) < high
                block[t - first, cell_of(part, t)] = 1.0
            rows.append(block)
    return np.concatenate(rows)


def scatter_matrix():
    table = np.zeros((4 * TP, CELLS), np.float32)
    for low, high, first, last in CELL_CHUNKS:
        for part in range(4):
            for t in range(TOK):
                if low <= cell_of(part, t) < high:
                    assert first <= t < last
                    table[part * TP + t, cell_of(part, t)] = 1.0
    return table


def spread_matrix():
    table = np.zeros((SPREAD, TP), np.float32)
    for t in range(TOK):
        i, j = divmod(t, SIDE)
        table[REL * i + j, t] = 1.0
    return table


def stats_kernel(x_ref, out_ref):
    pieces = []
    step = 32
    for block in range(D_IN // step):
        rows = slice(block * step, (block + 1) * step)
        total = x_ref[0, rows, :].astype(FLOAT)
        for crop in range(1, CROPS):
            total = total + x_ref[crop, rows, :].astype(FLOAT)
        total = jnp.sum(total, axis=1, keepdims=True)
        mean = total * (1.0 / (CROPS * CELLS))
        square = jnp.zeros((step, CELLS), FLOAT)
        for crop in range(CROPS):
            centre = x_ref[crop, rows, :].astype(FLOAT) - mean
            square = square + centre * centre
        square = jnp.sum(square, axis=1, keepdims=True)
        lane = lax.broadcasted_iota(jnp.int32, (step, 128), 1)
        pieces.append(jnp.where(lane == 0, mean, jnp.where(lane == 1, square, 0.0)))
    turned = jnp.concatenate(pieces, axis=0).T
    pad = jnp.zeros((1, 64), FLOAT)
    row = jnp.concatenate([turned[0:1], pad, turned[1:2], pad], axis=1)
    out_ref[...] = jnp.broadcast_to(row[None], out_ref.shape)


def local_stats(cells, copies):
    return pl.pallas_call(
        stats_kernel,
        out_shape=jax.ShapeDtypeStruct((copies, 1, 512), FLOAT),
        compiler_params=params(16 << 20),
        name="stats",
        cost_estimate=cost(8e6, 2.8e6),
    )(cells)


def batch_coefficients(gathered):
    count = gathered.shape[0]
    means = gathered[:, 0, 0:D_IN]
    squares = gathered[:, 0, 256 : 256 + D_IN]
    mean = jnp.sum(means, axis=0, keepdims=True) * (1.0 / count)
    off = means - mean
    local = float(CROPS * CELLS)
    var = jnp.sum(squares, axis=0, keepdims=True) + local * jnp.sum(
        off * off, axis=0, keepdims=True
    )
    return mean, lax.rsqrt(var * (1.0 / (local * count)) + EPS)


def select_cells(s_ref, x_ref, out_ref):
    at = 0
    for first, last, low, high in CHUNKS:
        size = last - first
        picked = dot(s_ref[at : at + 4 * size, low:high], x_ref[0, :, low:high], NT).astype(HALF)
        for part in range(4):
            start = part * TP + first
            out_ref[start : start + size, :] = picked[part * size : (part + 1) * size]
        at += 4 * size


def bias_kernel(table_ref, spread_ref, out_ref, rows_ref):
    row = lax.broadcasted_iota(jnp.int32, (TP, TP), 0)
    for head in range(HEADS):
        pad = jnp.zeros((1, TAB - REL * REL), FLOAT)
        table = jnp.concatenate([table_ref[head : head + 1, :] * LOG2E, pad], axis=1)
        base = pltpu.roll(jnp.broadcast_to(table, (16, TAB)), 0, 1, stride=1, stride_axis=0)
        for r in range(SIDE):
            rolled = pltpu.roll(base, (TAB - 364 + REL * r) % TAB, 1)
            rows_ref[head, SIDE * r : SIDE * (r + 1), :] = rolled[:SIDE, :SPREAD]
        rows_ref[head, TOK:, :] = jnp.zeros((TP - TOK, SPREAD), FLOAT)
        hi, lo = split2(rows_ref[head])
        value = dot(hi, spread_ref[...]) + dot(lo, spread_ref[...])
        out_ref[head] = jnp.where(row < TOK, value, -1e30)


def expand_bias(rel_table, spread):
    return pl.pallas_call(
        bias_kernel,
        in_specs=[whole((HEADS, REL * REL)), whole((SPREAD, TP))],
        out_specs=whole((HEADS, TP, TP)),
        out_shape=jax.ShapeDtypeStruct((HEADS, TP, TP), FLOAT),
        scratch_shapes=[pltpu.VMEM((HEADS, TP, SPREAD), FLOAT)],
        compiler_params=params(24 << 20),
        name="expand_bias",
        cost_estimate=cost(2e9, 3e6),
    )(rel_table, spread)


def late_kernel(
    core_ref, dbias_ref, spread_ref, gw_ref, sums_ref, keep_ref, send_ref, rows_ref
):
    row = lax.broadcasted_iota(jnp.int32, (16, TAB), 0)
    lines = []
    for head in range(HEADS):
        hi, lo = split2(dbias_ref[head])
        rows_ref[head, :, :SPREAD] = dot(hi, spread_ref[...]) + dot(lo, spread_ref[...])
        rows_ref[head, :, SPREAD:] = jnp.zeros((TP, TAB - SPREAD), FLOAT)
        total = rows_ref[head, 0:16, :]
        for r in range(1, SIDE):
            piece = rows_ref[head, SIDE * r : SIDE * r + 16, :]
            total = total + pltpu.roll(piece, TAB - REL * r, 1)
        total = jnp.where(row < SIDE, total, 0.0)
        total = jnp.concatenate([total[c : c + 1, :] for c in range(15, -1, -1)], axis=0)
        total = pltpu.roll(total, 0, 1, stride=1, stride_axis=0)
        total = jnp.sum(total, axis=0, keepdims=True)
        total = pltpu.roll(total, 364 - 15, 1)
        lines += [total[:, k * 128 : (k + 1) * 128] for k in range(TAB // 128)]
    pad = jnp.zeros((1, 256 - D_IN), FLOAT)

    def wide(k):
        value = jnp.concatenate([sums_ref[k : k + 1, :], pad], axis=1)
        return [value[:, :128], value[:, 128:]]

    lines += wide(0) + wide(1)
    lines.append(jnp.zeros((80 - len(lines), 128), FLOAT))
    lines = jnp.concatenate(lines, axis=0).reshape(5, LATE, 128)
    totals = jnp.concatenate(wide(2) + wide(3) + [jnp.zeros((4, 128), FLOAT)], axis=0)
    totals = jnp.broadcast_to(totals[None], (PIECES, SUMS, 128))

    def write(ref, half):
        size = D_IN // 2 // LATE
        rows = slice(half * (D_IN // 2), (half + 1) * (D_IN // 2))
        for k in range(9):
            block = gw_ref[rows, k * 128 : (k + 1) * 128].reshape(size, LATE, 128)
            ref[k * size : (k + 1) * size, :LATE, :] = block
        at = 9 * size
        ref[at : at + 5, :LATE, :] = lines
        ref[at + 5 :, :LATE, :] = jnp.zeros((PIECES - at - 5, LATE, 128), FLOAT)
        ref[:, LATE:, :] = totals

    @pl.when(core_ref[0] == 0)
    def _():
        write(keep_ref, 0)
        write(send_ref, 1)

    @pl.when(core_ref[0] != 0)
    def _():
        write(keep_ref, 1)
        write(send_ref, 0)


def late_message(core, dbias, spread, gw, sums):
    shape = (PIECES, LATE + SUMS, 128)
    return pl.pallas_call(
        late_kernel,
        in_specs=[pl.BlockSpec(memory_space=pltpu.SMEM)]
        + [whole(a.shape) for a in (dbias, spread, gw, sums)],
        out_specs=[whole(shape)] * 2,
        out_shape=[jax.ShapeDtypeStruct(shape, FLOAT)] * 2,
        scratch_shapes=[pltpu.VMEM((HEADS, TP, TAB), FLOAT)],
        compiler_params=params(26 << 20),
        name="late_message",
        cost_estimate=cost(2e9, 5e6),
    )(core, dbias, spread, gw, sums)


def line(ref):
    return ref[...].reshape(1, ref.shape[0])


def bn_parts(x_ref, coef_ref, scale_ref, bias_ref):
    mean = coef_ref[0:1, :]
    factor = coef_ref[1:2, :] * line(scale_ref) * LOG2E
    shift = line(bias_ref) * LOG2E
    return [
        (x_ref[0, part * TP : (part + 1) * TP, :].astype(FLOAT) - mean) * factor + shift
        for part in range(4)
    ]


def norm_rows(value):
    centre = value - jnp.mean(value, axis=-1, keepdims=True)
    inverse = lax.rsqrt(jnp.mean(centre * centre, axis=-1, keepdims=True) + EPS)
    return centre * inverse, inverse


def put_rows(ref, crop, value):
    for group in range(ref.shape[0]):
        piece = value[:, group * 128 : (group + 1) * 128]
        if piece.shape[1] < 128:
            rest = jnp.zeros((piece.shape[0], 128 - piece.shape[1]), piece.dtype)
            piece = jnp.concatenate([piece, rest], axis=1)
        ref[group, pl.ds(crop, TP, stride=CROPS), :] = piece


def take_rows(ref, crop):
    pieces = [ref[group, pl.ds(crop, TP, stride=CROPS), :] for group in range(ref.shape[0])]
    return jnp.concatenate(pieces, axis=1)


def head_masks():
    lane = lax.broadcasted_iota(jnp.int32, (1, 128), 1)
    return [(lane // HEAD == k).astype(HALF) for k in range(4)]


def attend(
    crop,
    x_ref,
    next_ref,
    picks_ref,
    picked_ref,
    coef_ref,
    bn_scale_ref,
    bn_bias_ref,
    gain_ref,
    shift_ref,
    w_ref,
    bias_ref,
    qkv_ref,
    probs_ref,
    attn_ref,
    pooled_ref,
    plain_ref,
    s_ref,
):
    x_ref[0] = picked_ref[...]
    parts = bn_parts(x_ref, coef_ref, bn_scale_ref, bn_bias_ref)
    top = jnp.maximum(jnp.maximum(parts[0], parts[1]), jnp.maximum(parts[2], parts[3]))
    total = jnp.exp2(parts[0] - top)
    for part in range(1, 4):
        total = total + jnp.exp2(parts[part] - top)
    pooled = top * LN2 + jnp.log(total)
    put_rows(pooled_ref, crop, pooled)
    plain_ref[0] = pooled
    z, _ = norm_rows(pooled)
    first = (z * line(gain_ref) + line(shift_ref)).astype(HALF)
    qkv_ref[0] = dot(first, w_ref[...]).astype(HALF)
    value_t = qkv_ref[0, :, 2 * D :].astype(FLOAT).T.astype(HALF)
    masks = head_masks()

    def start(head):
        group = head // 4
        query = qkv_ref[0, :, group * 128 : (group + 1) * 128] * masks[head % 4]
        key = qkv_ref[0, :, D + group * 128 : D + (group + 1) * 128]
        s_ref[head % 3] = dot(key, query, NT)

    def finish(head):
        rows = slice(head * HEAD, (head + 1) * HEAD)
        return dot(value_t[rows, :], probs_ref[0, head])

    heads = []
    start(0)
    for head in range(HEADS):
        if head + 1 < HEADS:
            start(head + 1)
        if head == 2:
            select_cells(picks_ref, next_ref, picked_ref)
        for cols in (slice(0, 128), slice(128, TP)):
            scores = s_ref[head % 3, :, cols] * (SCALE * LOG2E) + bias_ref[head, :, cols]
            weight = jnp.exp2(scores - jnp.max(scores, axis=0, keepdims=True))
            weight = weight * (1.0 / jnp.sum(weight, axis=0, keepdims=True))
            probs_ref[0, head, :, cols] = weight.astype(HALF)
        if head > 0:
            heads.append(finish(head - 1))
    heads.append(finish(HEADS - 1))
    put_rows(attn_ref, crop, jnp.concatenate(heads, axis=0).T)


def normal_parts(u):
    cdf = lax.erf(u * np.float32(np.sqrt(0.5))) * 0.5 + 0.5
    return cdf, jnp.exp2(u * u * (-0.5 * LOG2E)) * (u * np.float32(1.0 / np.sqrt(2 * np.pi)))


PIECES = 64
EARLY = 88
LATE = 16
SUMS = 8
HALF_ROWS = PIECES * EARLY
ROWS_2 = EARLY + LATE + SUMS
AT_G2 = FF // 128 * (D // 2)
AT_OUT = AT_G2 + FF // 2 // 128 * D
AT_SHORT = AT_OUT + 3 * D // 2
AT_LINES = AT_SHORT + 3 * D_IN // 2
AT_END = AT_LINES + 24
FC_COLS = 768


def feed(
    core,
    attn_ref,
    pooled_ref,
    cot_ref,
    w_short_ref,
    w_out_ref,
    gain_ref,
    shift_ref,
    w1_ref,
    b1_ref,
    w2_ref,
    b2_ref,
    result_ref,
    dattn_ref,
    dshort_ref,
    shared_ref,
    message_ref,
    result_hbm,
    dattn_hbm,
    dshort_hbm,
    shared_hbm,
    keep_ref,
    send_ref,
    sems,
    store_sems,
):
    stores = []

    def store(source, target):
        stores.append(pltpu.make_async_copy(source, target, store_sems.at[len(stores)]))
        stores[-1].start()

    def put(half, at, value):
        count = value.shape[0]
        for k in range(value.shape[1] // 128):
            message_ref[half, at + k * count : at + (k + 1) * count, :] = value[
                :, k * 128 : (k + 1) * 128
            ]

    shipped = []

    def ship(half, at, end):
        sem = sems.at[len(shipped)]
        rows = pl.ds(at, end - at)
        to_keep = pltpu.make_async_copy(message_ref.at[half, rows], keep_ref.at[rows], sem)
        to_send = pltpu.make_async_copy(message_ref.at[half, rows], send_ref.at[rows], sem)

        @pl.when(core == half)
        def _():
            to_keep.start()

        @pl.when(core != half)
        def _():
            to_send.start()

        shipped.append(to_keep)

    def attn_all():
        return jnp.concatenate([attn_ref[k, :ROWS] for k in range(3)], axis=1)

    def pooled_all():
        return jnp.concatenate([pooled_ref[k, :ROWS] for k in range(2)], axis=1)[:, :D_IN]

    y1 = dot(pooled_all().astype(HALF), w_short_ref[...]) + dot(
        attn_all().astype(HALF), w_out_ref[...]
    )
    z, inverse = norm_rows(y1)
    gain = line(gain_ref)
    second = (z * gain + line(shift_ref)).astype(HALF)
    result_ref[...] = y1 + line(b2_ref)
    b1 = line(b1_ref)
    back = jnp.zeros((ROWS, D), FLOAT)
    second_t = second.astype(FLOAT).T.astype(HALF)
    cot = cot_ref[...]
    cot_t = cot.astype(FLOAT).T.astype(HALF)
    sums1 = []
    for block in range(FF // FC_COLS):
        cols = slice(block * FC_COLS, (block + 1) * FC_COLS)
        u = dot(second, w1_ref[:, cols]) + b1[:, cols]
        cdf, slope = normal_parts(u)
        hidden = (u * cdf).astype(HALF)
        dhidden = dot(cot, w2_ref[cols, :], NT)
        du = dhidden * (cdf + slope)
        sums1.append(jnp.sum(du, axis=0, keepdims=True))
        du = du.astype(HALF)
        result_ref[...] += dot(hidden, w2_ref[cols, :])
        back = back + dot(du, w1_ref[:, cols], NT)
        g1 = dot(second_t, du)
        at = block * (FC_COLS // 128) * (D // 2)
        for half in range(2):
            put(half, at, g1[half * (D // 2) : (half + 1) * (D // 2)])
            ship(half, at, at + FC_COLS // 128 * (D // 2))
        put(block, AT_G2, dot(cot_t, hidden))
        ship(block, AT_G2, AT_OUT)
    store(result_ref, result_hbm)
    dz = back * gain
    dy1 = cot_ref[...].astype(FLOAT) + inverse * (
        dz
        - jnp.mean(dz, axis=-1, keepdims=True)
        - z * jnp.mean(dz * z, axis=-1, keepdims=True)
    )
    low = dy1.astype(HALF)
    dattn = dot(low, w_out_ref[...], NT).astype(HALF).astype(FLOAT)
    for k in range(3):
        dattn_ref[k, :ROWS, :] = dattn[:, k * 128 : (k + 1) * 128]
    dattn_ref[:, ROWS:, :] = jnp.zeros((3, ROWS_P - ROWS, 128), FLOAT)
    store(dattn_ref, dattn_hbm)
    dshort = dot(low, w_short_ref[...], NT)
    dshort_ref[0, :ROWS, :] = dshort[:, :128]
    dshort_ref[1, :ROWS, :] = jnp.concatenate(
        [dshort[:, 128:], jnp.zeros((ROWS, 256 - D_IN), FLOAT)], axis=1
    )
    dshort_ref[:, ROWS:, :] = jnp.zeros((2, ROWS_P - ROWS, 128), FLOAT)
    store(dshort_ref, dshort_hbm)
    lane = lax.broadcasted_iota(jnp.int32, (D, 128), 0) // HEAD
    column = lax.broadcasted_iota(jnp.int32, (D, 128), 1)
    ones = (lane == column).astype(HALF)
    product = attn_all() * dattn
    high = product.astype(HALF)
    rest = (product - high.astype(FLOAT)).astype(HALF)
    shared_ref[:ROWS, :] = dot(high, ones) + dot(rest, ones)
    shared_ref[ROWS:, :] = jnp.zeros((ROWS_P - ROWS, 128), FLOAT)
    store(shared_ref, shared_hbm)
    gout = dot(attn_all().T.astype(HALF), low)
    gshort = dot(pooled_all().T.astype(HALF), low)
    lines = [
        jnp.sum(back * z, axis=0, keepdims=True),
        jnp.sum(back, axis=0, keepdims=True),
        jnp.sum(cot_ref[...].astype(FLOAT), axis=0, keepdims=True),
    ]
    flat = jnp.concatenate(sums1 + lines, axis=1)
    pieces = [flat[:, k * 128 : (k + 1) * 128] for k in range((FF + 3 * D) // 128)]
    pieces.append(jnp.zeros((3, 128), FLOAT))
    lines = jnp.concatenate(pieces, axis=0)
    for half in range(2):
        put(half, AT_OUT, gout[half * (D // 2) : (half + 1) * (D // 2)])
        put(half, AT_SHORT, gshort[half * (D_IN // 2) : (half + 1) * (D_IN // 2)])
        put(half, AT_LINES, lines)
        put(half, AT_END, jnp.zeros((HALF_ROWS - AT_END, 128), FLOAT))
        ship(half, AT_OUT, HALF_ROWS)
    for copy in shipped + stores:
        copy.wait()


def forward_kernel(
    core_ref,
    gathered_ref,
    picks_ref,
    bn_scale_ref,
    bn_bias_ref,
    gain1_ref,
    shift1_ref,
    wqkv_ref,
    gain2_ref,
    shift2_ref,
    b1_ref,
    b2_ref,
    cells_hbm,
    bias_hbm,
    cot_hbm,
    w_short_hbm,
    w_out_hbm,
    w1_hbm,
    w2_hbm,
    coef_ref,
    x_hbm,
    qkv_hbm,
    probs_hbm,
    plain_hbm,
    result_hbm,
    dattn_hbm,
    dshort_hbm,
    shared_hbm,
    keep_hbm,
    send_hbm,
    s_ref,
    picked_ref,
    attn_ref,
    pooled_ref,
    bias_ref,
    cot_ref,
    w_short_ref,
    w_out_ref,
    w1_ref,
    w2_ref,
    result_ref,
    dattn_ref,
    dshort_ref,
    shared_ref,
    message_ref,
    first_ref,
    step_ref,
    load_sems,
    ship_sems,
    store_sems,
):
    pairs = (
        (cells_hbm.at[pl.ds(0, 1)], first_ref),
        (bias_hbm, bias_ref),
        (w_short_hbm, w_short_ref),
        (w_out_hbm, w_out_ref),
        (w1_hbm, w1_ref),
        (cot_hbm, cot_ref),
        (w2_hbm, w2_ref),
    )
    loads = [pltpu.make_async_copy(a, b, load_sems.at[k]) for k, (a, b) in enumerate(pairs)]
    for load in loads:
        load.start()
    mean, inv = batch_coefficients(gathered_ref[...])
    coef_ref[...] = jnp.zeros_like(coef_ref)
    coef_ref[0:1, :] = mean
    coef_ref[1:2, :] = inv
    loads[0].wait()
    select_cells(picks_ref, first_ref, picked_ref)
    loads[1].wait()

    step_ref[0] = 0

    def body(next_ref, x_ref, qkv_ref, probs_ref, plain_ref):
        crop = step_ref[0]
        step_ref[0] = crop + 1
        attend(
            crop,
            x_ref,
            next_ref,
            picks_ref,
            picked_ref,
            coef_ref,
            bn_scale_ref,
            bn_bias_ref,
            gain1_ref,
            shift1_ref,
            wqkv_ref,
            bias_ref,
            qkv_ref,
            probs_ref,
            attn_ref,
            pooled_ref,
            plain_ref,
            s_ref,
        )

    by_crop = lambda *shape: pl.BlockSpec((1,) + shape, lambda c: (c,) + (0,) * len(shape))
    pltpu.emit_pipeline(
        body,
        grid=(CROPS,),
        in_specs=[
            pl.BlockSpec((1, D_IN, CELLS), lambda c: (jnp.minimum(c + 1, CROPS - 1), 0, 0))
        ],
        out_specs=[
            by_crop(4 * TP, D_IN),
            by_crop(TP, 3 * D),
            by_crop(HEADS, TP, TP),
            by_crop(TP, D_IN),
        ],
    )(cells_hbm, x_hbm, qkv_hbm, probs_hbm, plain_hbm)
    for load in loads[2:]:
        load.wait()
    feed(
        core_ref[0],
        attn_ref,
        pooled_ref,
        cot_ref,
        w_short_ref,
        w_out_ref,
        gain2_ref,
        shift2_ref,
        w1_ref,
        b1_ref,
        w2_ref,
        b2_ref,
        result_ref,
        dattn_ref,
        dshort_ref,
        shared_ref,
        message_ref,
        result_hbm,
        dattn_hbm,
        dshort_hbm,
        shared_hbm,
        keep_hbm,
        send_hbm,
        ship_sems,
        store_sems,
    )


def forward(
    core,
    gathered,
    picks,
    cells,
    bn_scale,
    bn_bias,
    gain1,
    shift1,
    w_qkv,
    gain2,
    shift2,
    b1,
    b2,
    bias,
    cot,
    w_short,
    w_out,
    w1,
    w2,
):
    hbm = pl.BlockSpec(memory_space=pl.ANY)
    small = (gathered, picks, bn_scale, bn_bias, gain1, shift1, w_qkv, gain2, shift2, b1, b2)
    large = (cells, bias, cot, w_short, w_out, w1, w2)
    feed_shapes = [(ROWS, D), (3, ROWS_P, 128), (2, ROWS_P, 128), (ROWS_P, 128)]
    return pl.pallas_call(
        forward_kernel,
        in_specs=[pl.BlockSpec(memory_space=pltpu.SMEM)]
        + [whole(a.shape) for a in small]
        + [hbm] * len(large),
        out_specs=[whole((8, D_IN))] + [hbm] * 10,
        out_shape=[
            jax.ShapeDtypeStruct((8, D_IN), FLOAT),
            jax.ShapeDtypeStruct((CROPS, 4 * TP, D_IN), HALF),
            jax.ShapeDtypeStruct((CROPS, TP, 3 * D), HALF),
            jax.ShapeDtypeStruct((CROPS, HEADS, TP, TP), HALF),
            jax.ShapeDtypeStruct((CROPS, TP, D_IN), FLOAT),
        ]
        + [jax.ShapeDtypeStruct(shape, FLOAT) for shape in feed_shapes]
        + [jax.ShapeDtypeStruct((HALF_ROWS, 128), FLOAT)] * 2,
        scratch_shapes=[
            pltpu.VMEM((3, TP, TP), FLOAT),
            pltpu.VMEM((4 * TP, D_IN), HALF),
            pltpu.VMEM((3, ROWS_P, 128), FLOAT),
            pltpu.VMEM((2, ROWS_P, 128), FLOAT),
        ]
        + [pltpu.VMEM(a.shape, a.dtype) for a in (bias, cot, w_short, w_out, w1, w2)]
        + [pltpu.VMEM(shape, FLOAT) for shape in feed_shapes]
        + [
            pltpu.VMEM((2, HALF_ROWS, 128), FLOAT),
            pltpu.VMEM((1, D_IN, CELLS), HALF),
            pltpu.SMEM((1,), jnp.int32),
            pltpu.SemaphoreType.DMA((7,)),
            pltpu.SemaphoreType.DMA((8,)),
            pltpu.SemaphoreType.DMA((4,)),
        ],
        compiler_params=params(56 << 20),
        name="forward",
        cost_estimate=cost(1.6e10, 5e7, 8e6),
    )(core, *small, *large)


def second_message_kernel(pieces_ref, late_ref, out_ref):
    total = pieces_ref[0]
    for k in range(1, PIECES):
        total = total + pieces_ref[k]
    out_ref[:, :EARLY, :] = jnp.broadcast_to(total[None], (PIECES, EARLY, 128))
    out_ref[:, EARLY:, :] = late_ref[...]


def second_message(pieces, late):
    shape = (PIECES, ROWS_2, 128)
    return pl.pallas_call(
        second_message_kernel,
        in_specs=[whole(pieces.shape), whole(late.shape)],
        out_specs=whole(shape),
        out_shape=jax.ShapeDtypeStruct(shape, FLOAT),
        compiler_params=params(16 << 20),
        name="second_message",
        cost_estimate=cost(1e6, 7e6),
    )(pieces, late)


def late_sum_kernel(in_hbm, copies_ref, totals_ref, late_ref, sem):
    load = pltpu.make_async_copy(in_hbm.at[:, pl.ds(EARLY, LATE + SUMS)], late_ref, sem)
    load.start()
    load.wait()
    total = late_ref[0]
    for k in range(1, PIECES):
        total = total + late_ref[k]
    copies_ref[...] = jnp.broadcast_to(total[None, :LATE], copies_ref.shape)
    totals_ref[...] = total[LATE:]


def late_sum(arrived):
    shapes = [(2 * PIECES, LATE, 128), (SUMS, 128)]
    return pl.pallas_call(
        late_sum_kernel,
        in_specs=[pl.BlockSpec(memory_space=pl.ANY)],
        out_specs=[whole(shape) for shape in shapes],
        out_shape=[jax.ShapeDtypeStruct(shape, FLOAT) for shape in shapes],
        scratch_shapes=[
            pltpu.VMEM((PIECES, LATE + SUMS, 128), FLOAT),
            pltpu.SemaphoreType.DMA,
        ],
        compiler_params=params(8 << 20),
        name="late_sum",
        cost_estimate=cost(1e5, 2e6),
    )(arrived)


def touch_kernel(*refs):
    del refs


def pass_after(after, value):
    return pl.pallas_call(
        touch_kernel,
        in_specs=[pl.BlockSpec(memory_space=pl.ANY)] * 2,
        out_specs=pl.BlockSpec(memory_space=pl.ANY),
        out_shape=jax.ShapeDtypeStruct(value.shape, value.dtype),
        input_output_aliases={1: 0},
        compiler_params=params(4 << 20),
        name="pass_after",
        cost_estimate=cost(1, 1),
    )(after, value)


def unpack_kernel(which_ref, early_ref, *refs):
    g1_ref, g2_ref, gout_ref, gshort_ref = refs[-8:][:4]

    def read(at, count):
        pieces = []
        while count:
            piece, row = divmod(at, EARLY)
            n = min(count, EARLY - row)
            pieces.append(early_ref[piece, row : row + n, :])
            at, count = at + n, count - n
        return pieces[0] if len(pieces) == 1 else jnp.concatenate(pieces, axis=0)

    for k in range(FF // 128):
        g1_ref[:, k * 128 : (k + 1) * 128] = read(k * D // 2, D // 2)
    for k in range(FF // 256):
        g2_ref[k * 128 : (k + 1) * 128, :] = read(AT_G2 + k * D, D).T
    for k in range(3):
        cols = slice(k * 128, (k + 1) * 128)
        gout_ref[:, cols] = read(AT_OUT + k * D // 2, D // 2)
        gshort_ref[:, cols] = read(AT_SHORT + k * D_IN // 2, D_IN // 2)
    db1_ref, dgain2_ref, dshift2_ref, db2_ref = refs[-4:]
    lines = read(AT_LINES, 24)
    flat = jnp.concatenate([lines[k : k + 1, :] for k in range(21)], axis=1)
    db1_ref[...] = flat[:, :FF].reshape(FF)
    for k, target in enumerate((dgain2_ref, dshift2_ref, db2_ref)):
        target[...] = flat[:, FF + k * D : FF + (k + 1) * D].reshape(D)


def unpack(half, message, before=()):
    rows = [(D // 2, FF), (FF // 2, D), (D // 2, D), (D_IN // 2, D)]
    small = [(FF,), (D,), (D,), (D,)]
    shapes = [(2 * a, b) for a, b in rows] + small
    any_spec = pl.BlockSpec(memory_space=pl.ANY)
    return pl.pallas_call(
        unpack_kernel,
        grid_spec=pltpu.PrefetchScalarGridSpec(
            num_scalar_prefetch=1,
            grid=(1,),
            in_specs=[pl.BlockSpec(message.shape, lambda i, h: (0, 0, 0))]
            + [any_spec] * len(before),
            out_specs=[pl.BlockSpec(shape, lambda i, h: (h[0], 0)) for shape in rows]
            + [pl.BlockSpec(shape, lambda i, h: (0,)) for shape in small],
        ),
        out_shape=[jax.ShapeDtypeStruct(shape, FLOAT) for shape in shapes],
        input_output_aliases={2 + k: k for k in range(len(before))},
        compiler_params=params(24 << 20),
        name="unpack",
        cost_estimate=cost(1e6, 6e6),
    )(half, message, *before)


def unpack_late_kernel(after_ref, late_ref, gqkv_ref, table_ref, dgain_ref, dshift_ref):
    def read(half, at, count):
        pieces = [late_ref[2 * p + half] for p in range(at // LATE, (at + count) // LATE)]
        return jnp.concatenate(pieces, axis=0)

    for half in range(2):
        rows = slice(half * (D_IN // 2), (half + 1) * (D_IN // 2))
        for k in range(9):
            value = read(half, k * D_IN // 2, D_IN // 2)
            gqkv_ref[rows, k * 128 : (k + 1) * 128] = value
    lines = read(0, 9 * D_IN // 2, 80)
    per = TAB // 128
    columns = []
    for k in range(per):
        rows = [lines[h * per + k : h * per + k + 1, :] for h in range(HEADS)]
        columns.append(jnp.concatenate(rows, axis=0))
    table_ref[...] = jnp.concatenate(columns, axis=1)[:, : REL * REL]
    for k, target in enumerate((dgain_ref, dshift_ref)):
        at = HEADS * per + 2 * k
        both = jnp.concatenate([lines[at : at + 1, :], lines[at + 1 : at + 2, :]], axis=1)
        target[...] = both[:, :D_IN].reshape(D_IN)


def unpack_late(after, late):
    shapes = [(D_IN, 3 * D), (HEADS, REL * REL), (D_IN,), (D_IN,)]
    return pl.pallas_call(
        unpack_late_kernel,
        in_specs=[pl.BlockSpec(memory_space=pl.ANY), whole((2 * PIECES, LATE, 128))],
        out_specs=[whole(shape) for shape in shapes],
        out_shape=[jax.ShapeDtypeStruct(shape, FLOAT) for shape in shapes],
        compiler_params=params(12 << 20),
        name="unpack_late",
        cost_estimate=cost(1e5, 2e6),
    )(after, late)


def back_kernel(
    after_ref,
    coef_ref,
    x_ref,
    plain_ref,
    qkv_ref,
    probs_ref,
    dattn_ref,
    dshort_ref,
    shared_ref,
    bn_scale_ref,
    bn_bias_ref,
    gain_ref,
    shift_ref,
    w_ref,
    dbias_ref,
    gw_ref,
    sums_ref,
    dcells_ref,
    dp_ref,
    ds_ref,
):
    crop = pl.program_id(0)

    @pl.when(crop == 0)
    def _():
        dbias_ref[...] = jnp.zeros_like(dbias_ref)
        gw_ref[...] = jnp.zeros_like(gw_ref)
        sums_ref[...] = jnp.zeros_like(sums_ref)

    dattn = take_rows(dattn_ref, crop).astype(HALF)
    shared = shared_ref[pl.ds(crop, TP, stride=CROPS), :].T
    key_t = qkv_ref[0, :, D : 2 * D].astype(FLOAT).T.astype(HALF)
    masks = head_masks()
    dquery_t, dkeys, dvalues = [], [], []

    def start(head):
        group = head // 4
        grad = dattn[:, group * 128 : (group + 1) * 128] * masks[head % 4]
        value = qkv_ref[0, :, 2 * D + group * 128 : 2 * D + (group + 1) * 128]
        dp_ref[head % 3] = dot(value, grad, NT)
        dvalues.append(dot(probs_ref[0, head], grad))

    def finish(head):
        group = head // 4
        query = qkv_ref[0, :, group * 128 : (group + 1) * 128] * masks[head % 4]
        dscores = ds_ref[head % 2]
        dkeys.append(dot(dscores, query))
        dquery_t.append(dot(key_t[head * HEAD : (head + 1) * HEAD, :], dscores))

    start(0)
    for head in range(HEADS):
        if head + 1 < HEADS:
            start(head + 1)
        for cols in (slice(0, 128), slice(128, TP)):
            probs = probs_ref[0, head, :, cols].astype(FLOAT)
            dscores = probs * (dp_ref[head % 3, :, cols] - shared[head : head + 1, cols])
            dbias_ref[head, :, cols] += dscores
            ds_ref[head % 2, :, cols] = dscores.astype(HALF)
        if head > 0:
            finish(head - 1)
    finish(HEADS - 1)
    group_sum = lambda items, g: sum(items[4 * g + 1 : 4 * g + 4], items[4 * g])
    dquery = jnp.concatenate(dquery_t, axis=0).T * SCALE
    dqkv = jnp.concatenate(
        [dquery]
        + [group_sum(dkeys, g) * SCALE for g in range(3)]
        + [group_sum(dvalues, g) for g in range(3)],
        axis=1,
    ).astype(HALF)
    pooled = plain_ref[0]
    z, inverse = norm_rows(pooled)
    gain = line(gain_ref)
    first_t = (z * gain + line(shift_ref)).T.astype(HALF)
    gw_ref[...] += dot(first_t, dqkv)
    dfirst = dot(dqkv, w_ref[...], NT)
    dz = dfirst * gain
    dpooled = take_rows(dshort_ref, crop)[:, :D_IN] + inverse * (
        dz
        - jnp.mean(dz, axis=-1, keepdims=True)
        - z * jnp.mean(dz * z, axis=-1, keepdims=True)
    )
    sums_ref[0:1, :] += jnp.sum(dfirst * z, axis=0, keepdims=True)
    sums_ref[1:2, :] += jnp.sum(dfirst, axis=0, keepdims=True)
    level = pooled * LOG2E
    parts = bn_parts(x_ref, coef_ref, bn_scale_ref, bn_bias_ref)
    along = jnp.zeros((TP, D_IN), FLOAT)
    total = jnp.zeros((TP, D_IN), FLOAT)
    for part in range(4):
        dpart = dpooled * jnp.exp2(parts[part] - level)
        dcells_ref[0, part * TP : (part + 1) * TP, :] = dpart.astype(HALF)
        raw = x_ref[0, part * TP : (part + 1) * TP, :].astype(FLOAT)
        along = along + dpart * (raw - coef_ref[0:1, :])
        total = total + dpart
    sums_ref[2:3, :] += jnp.sum(along, axis=0, keepdims=True) * coef_ref[1:2, :]
    sums_ref[3:4, :] += jnp.sum(total, axis=0, keepdims=True)


def attention_back(
    after, coef, picked, plain, qkv, probs, dattn, dshort, shared, bn_scale, bn_bias, gain, shift, w_qkv
):
    return pl.pallas_call(
        back_kernel,
        grid=(CROPS,),
        in_specs=[
            pl.BlockSpec(memory_space=pl.ANY),
            whole((8, D_IN)),
            pl.BlockSpec((1, 4 * TP, D_IN), lambda c: (c, 0, 0)),
            pl.BlockSpec((1, TP, D_IN), lambda c: (c, 0, 0)),
            pl.BlockSpec((1, TP, 3 * D), lambda c: (c, 0, 0)),
            pl.BlockSpec((1, HEADS, TP, TP), lambda c: (c, 0, 0, 0)),
            whole((3, ROWS_P, 128)),
            whole((2, ROWS_P, 128)),
            whole((ROWS_P, 128)),
            whole((D_IN,)),
            whole((D_IN,)),
            whole((D_IN,)),
            whole((D_IN,)),
            whole((D_IN, 3 * D)),
        ],
        out_specs=[
            whole((HEADS, TP, TP)),
            whole((D_IN, 3 * D)),
            whole((8, D_IN)),
            pl.BlockSpec((1, 4 * TP, D_IN), lambda c: (c, 0, 0)),
        ],
        out_shape=[
            jax.ShapeDtypeStruct((HEADS, TP, TP), FLOAT),
            jax.ShapeDtypeStruct((D_IN, 3 * D), FLOAT),
            jax.ShapeDtypeStruct((8, D_IN), FLOAT),
            jax.ShapeDtypeStruct((CROPS, 4 * TP, D_IN), HALF),
        ],
        scratch_shapes=[pltpu.VMEM((3, TP, TP), FLOAT), pltpu.VMEM((2, TP, TP), HALF)],
        compiler_params=params(56 << 20),
        name="attention_back",
        cost_estimate=cost(6e9, 4e7, 2e6),
    )(after, coef, picked, plain, qkv, probs, dattn, dshort, shared, bn_scale, bn_bias, gain, shift, w_qkv)


def scatter_kernel(s_ref, d_ref, out_ref):
    for k in range(d_ref.shape[0]):
        for low, high, first, last in CELL_CHUNKS:
            value = None
            for part in range(4):
                rows = slice(part * TP + first, part * TP + last)
                term = dot(d_ref[k, rows, :], s_ref[rows, low:high], TN)
                value = term if value is None else value + term
            out_ref[k, :, low:high] = value.astype(HALF)


def scatter_cells(places, dcells):
    each = 2
    return pl.pallas_call(
        scatter_kernel,
        grid=(CROPS // each,),
        in_specs=[
            whole((4 * TP, CELLS)),
            pl.BlockSpec((each, 4 * TP, D_IN), lambda c: (c, 0, 0)),
        ],
        out_specs=pl.BlockSpec((each, D_IN, CELLS), lambda c: (c, 0, 0)),
        out_shape=jax.ShapeDtypeStruct((CROPS, D_IN, CELLS), HALF),
        compiler_params=params(16 << 20),
        name="scatter_cells",
        cost_estimate=cost(3e9, 8e6),
    )(places, dcells)


def column(row):
    return jnp.broadcast_to(row, (128, D_IN)).T[:, 0:1]


def cells_kernel(count, totals_ref, coef_ref, scale_ref, d_ref, x_ref, out_ref, dscale_ref, dshift_ref, cols_ref):
    @pl.when(pl.program_id(0) == 0)
    def _():
        rest = slice(0, D_IN - 128)
        along = jnp.concatenate([totals_ref[0:1, :], totals_ref[1:2, rest]], axis=1)
        plain = jnp.concatenate([totals_ref[2:3, :], totals_ref[3:4, rest]], axis=1)
        dscale_ref[...] = along.reshape(D_IN)
        dshift_ref[...] = plain.reshape(D_IN)
        mean = coef_ref[0:1, :]
        inv = coef_ref[1:2, :]
        factor = inv * line(scale_ref)
        share = 1.0 / float(count * CROPS * CELLS)
        slope = factor * along * inv * share
        cols_ref[:, 0:1] = column(factor)
        cols_ref[:, 1:2] = column(factor * plain * share)
        cols_ref[:, 2:3] = column(slope)
        cols_ref[:, 3:4] = column(mean)

    out_ref[0] = (
        d_ref[0].astype(FLOAT) * cols_ref[:, 0:1]
        - cols_ref[:, 1:2]
        - (x_ref[0].astype(FLOAT) - cols_ref[:, 3:4]) * cols_ref[:, 2:3]
    )


def cell_gradient(count, totals, coef, bn_scale, dcells, cells):
    crop_block = pl.BlockSpec((1, D_IN, CELLS), lambda c: (c, 0, 0))
    return pl.pallas_call(
        functools.partial(cells_kernel, count),
        grid=(CROPS,),
        in_specs=[
            whole((8, 128)),
            whole((8, D_IN)),
            whole((D_IN,)),
            crop_block,
            crop_block,
        ],
        out_specs=[crop_block, whole((D_IN,)), whole((D_IN,))],
        out_shape=[
            jax.ShapeDtypeStruct((CROPS, D_IN, CELLS), FLOAT),
            jax.ShapeDtypeStruct((D_IN,), FLOAT),
            jax.ShapeDtypeStruct((D_IN,), FLOAT),
        ],
        scratch_shapes=[pltpu.VMEM((D_IN, 128), FLOAT)],
        compiler_params=params(16 << 20),
        name="cell_gradient",
        cost_estimate=cost(1e7, 1.5e7),
    )(totals, coef, bn_scale, dcells, cells)


CHIPS = ("y", "x", "z")
ALL = ("y", "x", "z", "core")


def gather_rows(copies):
    if copies.shape[0] == 1:
        return copies
    return lax.all_to_all(copies, ALL, 0, 0)


def on_device(
    count,
    features,
    bn_scale,
    bn_bias,
    w_short,
    ln1_gain,
    ln1_bias,
    w_qkv,
    rel_table,
    w_out,
    ln2_gain,
    ln2_bias,
    w_fc1,
    fc1_bias,
    w_fc2,
    fc2_bias,
    cotangent,
):
    picks = jnp.asarray(select_matrix(), HALF)
    places = jnp.asarray(scatter_matrix(), HALF)
    spread = jnp.asarray(spread_matrix(), HALF)
    spread_back = jnp.asarray(spread_matrix().T, HALF)
    core = lax.axis_index("core").astype(jnp.int32).reshape(1)
    cells = features.transpose(0, 2, 1)
    cot = cotangent.transpose(1, 0, 2).reshape(ROWS, D)
    stats = gather_rows(local_stats(cells, count))
    bias = expand_bias(rel_table, spread)
    coef, picked, qkv, probs, plain, out, dattn, dshort, shared, keep, send = forward(
        core,
        stats,
        picks,
        cells,
        bn_scale,
        bn_bias,
        ln1_gain,
        ln1_bias,
        w_qkv,
        ln2_gain,
        ln2_bias,
        fc1_bias,
        fc2_bias,
        bias,
        cot,
        w_short,
        w_out,
        w_fc1,
        w_fc2,
    )
    swap = [(0, 1), (1, 0)]
    keep = keep.reshape(PIECES, EARLY, 128)
    send = send.reshape(PIECES, EARLY, 128)
    mine = keep
    if count > 1:
        mine = keep + lax.ppermute(send, "core", swap)
        pieces = lax.all_to_all(mine, CHIPS, 0, 0)
    dbias, gqkv, sums, dcells = attention_back(
        mine,
        coef,
        picked,
        plain,
        qkv,
        probs,
        dattn,
        dshort,
        shared,
        bn_scale,
        bn_bias,
        ln1_gain,
        ln1_bias,
        w_qkv,
    )
    late_keep, late_send = late_message(core, dbias, spread_back, gqkv, sums)
    scattered = scatter_cells(places, dcells)
    if count > 1:
        late = late_keep + lax.ppermute(late_send, "core", swap)
        own = lax.all_to_all(second_message(pieces, late), CHIPS, 0, 0)
        own = pass_after(scattered, own)
        copies, totals = late_sum(own)
        late = lax.all_to_all(copies, ALL, 0, 0)
        other = lax.ppermute(own, "core", swap)
    else:
        totals = late_keep[0, LATE:]
        own, other = keep, send
        late = jnp.stack([late_keep, late_send], axis=1)[:, :, :LATE].reshape(-1, LATE, 128)
    grad_cells, dscale, dshift = cell_gradient(count, totals, coef, bn_scale, scattered, cells)
    grads = unpack(core, own)
    g1, g2, gout, gshort = unpack(1 - core, other, grads[:4])[:4]
    db1, dgain2, dshift2, db2 = grads[4:]
    gqkv, table, dgain1, dshift1 = unpack_late(gshort, late)
    return (
        out.reshape(TOK, CROPS, D).transpose(1, 0, 2),
        grad_cells.transpose(0, 2, 1),
        dscale,
        dshift,
        gshort,
        dgain1,
        dshift1,
        gqkv,
        table,
        gout,
        dgain2,
        dshift2,
        g1,
        db1,
        g2,
        db2,
    )


def solution(mesh):
    count = mesh.size
    shape = (4, 4, 4, 2) if count == 128 else (1, 1, 1, 1)
    grid = jax.sharding.Mesh(mesh.devices.reshape(shape), ALL)
    split = P(ALL, None, None)
    same = P()
    in_specs = (split,) + (same,) * 14 + (split,)
    out_specs = (split, split) + (same,) * 14

    def run(*args):
        return on_device(count, *args)

    return jax.shard_map(run, mesh=grid, in_specs=in_specs, out_specs=out_specs, check_vma=False)
```

```python
import functools

import jax
import jax.numpy as jnp
import numpy as np
from jax import lax
from jax.experimental import pallas as pl
from jax.experimental.pallas import tpu as pltpu
from jax.sharding import PartitionSpec as P

HEADS = 12
HEAD = 32
SIDE = 14
TOK = 196
TP = 208
GRID2 = 2 * SIDE
CELLS = 784
D_IN = 192
D = 384
FF = 1536
CROPS = 8
ROWS = TOK * CROPS
ROWS_P = TP * CROPS
REL = 27
TAB = 768
SPREAD = 384

EPS = 1e-05
FLOAT = jnp.float32
HALF = jnp.bfloat16
LOG2E = 1.4426950408889634
LN2 = 0.6931471805599453
SCALE = HEAD ** (-0.5)
NN = (((1,), (0,)), ((), ()))
NT = (((1,), (1,)), ((), ()))
TN = (((0,), (0,)), ((), ()))
VMEM_LIMIT = 56 * 1024 * 1024


def dot(left, right, dims=NN):
    return lax.dot_general(left, right, dims, preferred_element_type=FLOAT)


def split2(value):
    hi = value.astype(HALF)
    return hi, (value - hi.astype(FLOAT)).astype(HALF)


def params(limit=VMEM_LIMIT):
    return pltpu.CompilerParams(vmem_limit_bytes=limit)


def cost(flops, bytes_accessed, transcendentals=0):
    return pl.CostEstimate(
        flops=int(flops), bytes_accessed=int(bytes_accessed), transcendentals=int(transcendentals)
    )


def whole(shape):
    return pl.BlockSpec(shape, lambda *_: (0,) * len(shape))


CHUNKS = (
    (0, 48, 0, 256),
    (48, 80, 0, 512),
    (80, 112, 256, 512),
    (112, 144, 256, 768),
    (144, 176, 512, 768),
    (176, TP, 512, CELLS),
)
CELL_CHUNKS = ((0, 256, 0, 80), (256, 512, 48, 144), (512, CELLS, 112, TP))


def cell_of(part, token):
    i, j = divmod(token, SIDE)
    a, b = divmod(part, 2)
    return (2 * i + a) * GRID2 + 2 * j + b


def select_matrix():
    rows = []
    for first, last, low, high in CHUNKS:
        for part in range(4):
            block = np.zeros((last - first, CELLS), np.float32)
            for t in range(first, min(last, TOK)):
                assert low <= cell_of(part, t) < high
                block[t - first, cell_of(part, t)] = 1.0
            rows.append(block)
    return np.concatenate(rows)


def scatter_matrix():
    table = np.zeros((4 * TP, CELLS), np.float32)
    for low, high, first, last in CELL_CHUNKS:
        for part in range(4):
            for t in range(TOK):
                if low <= cell_of(part, t) < high:
                    assert first <= t < last
                    table[part * TP + t, cell_of(part, t)] = 1.0
    return table


def spread_matrix():
    table = np.zeros((SPREAD, TP), np.float32)
    for t in range(TOK):
        i, j = divmod(t, SIDE)
        table[REL * i + j, t] = 1.0
    return table


def stats_kernel(x_ref, out_ref):
    pieces = []
    step = 32
    for block in range(D_IN // step):
        rows = slice(block * step, (block + 1) * step)
        total = x_ref[0, rows, :].astype(FLOAT)
        for crop in range(1, CROPS):
            total = total + x_ref[crop, rows, :].astype(FLOAT)
        total = jnp.sum(total, axis=1, keepdims=True)
        mean = total * (1.0 / (CROPS * CELLS))
        square = jnp.zeros((step, CELLS), FLOAT)
        for crop in range(CROPS):
            centre = x_ref[crop, rows, :].astype(FLOAT) - mean
            square = square + centre * centre
        square = jnp.sum(square, axis=1, keepdims=True)
        lane = lax.broadcasted_iota(jnp.int32, (step, 128), 1)
        pieces.append(jnp.where(lane == 0, mean, jnp.where(lane == 1, square, 0.0)))
    turned = jnp.concatenate(pieces, axis=0).T
    pad = jnp.zeros((1, 64), FLOAT)
    row = jnp.concatenate([turned[0:1], pad, turned[1:2], pad], axis=1)
    out_ref[...] = jnp.broadcast_to(row[None], out_ref.shape)


def local_stats(cells, copies):
    return pl.pallas_call(
        stats_kernel,
        out_shape=jax.ShapeDtypeStruct((copies, 1, 512), FLOAT),
        compiler_params=params(),
        name="stats",
        cost_estimate=cost(8e6, 2.8e6),
    )(cells)


def batch_coefficients(gathered):
    count = gathered.shape[0]
    means = gathered[:, 0, 0:D_IN]
    squares = gathered[:, 0, 256 : 256 + D_IN]
    mean = jnp.sum(means, axis=0, keepdims=True) * (1.0 / count)
    off = means - mean
    local = float(CROPS * CELLS)
    var = jnp.sum(squares, axis=0, keepdims=True) + local * jnp.sum(
        off * off, axis=0, keepdims=True
    )
    return mean, lax.rsqrt(var * (1.0 / (local * count)) + EPS)


def select_cells(s_ref, x_ref, out_ref):
    at = 0
    for first, last, low, high in CHUNKS:
        size = last - first
        picked = dot(s_ref[at : at + 4 * size, low:high], x_ref[0, :, low:high], NT).astype(HALF)
        for part in range(4):
            start = part * TP + first
            out_ref[start : start + size, :] = picked[part * size : (part + 1) * size]
        at += 4 * size


def bias_kernel(table_ref, spread_ref, picks_ref, cells_ref, out_ref, picked_ref, rows_ref):
    select_cells(picks_ref, cells_ref, picked_ref)
    row = lax.broadcasted_iota(jnp.int32, (TP, TP), 0)
    for head in range(HEADS):
        pad = jnp.zeros((1, TAB - REL * REL), FLOAT)
        table = jnp.concatenate([table_ref[head : head + 1, :] * LOG2E, pad], axis=1)
        base = pltpu.roll(jnp.broadcast_to(table, (16, TAB)), 0, 1, stride=1, stride_axis=0)
        for r in range(SIDE):
            rolled = pltpu.roll(base, (TAB - 364 + REL * r) % TAB, 1)
            rows_ref[head, SIDE * r : SIDE * (r + 1), :] = rolled[:SIDE, :SPREAD]
        rows_ref[head, TOK:, :] = jnp.zeros((TP - TOK, SPREAD), FLOAT)
        hi, lo = split2(rows_ref[head])
        value = dot(hi, spread_ref[...]) + dot(lo, spread_ref[...])
        out_ref[head] = jnp.where(row < TOK, value, -1e30)


def expand_bias(rel_table, spread, picks, cells):
    first = pl.BlockSpec((1, D_IN, CELLS), lambda i: (0, 0, 0))
    return pl.pallas_call(
        bias_kernel,
        grid=(1,),
        in_specs=[whole(rel_table.shape), whole(spread.shape), whole(picks.shape), first],
        out_specs=[whole((HEADS, TP, TP)), whole((4 * TP, D_IN))],
        out_shape=[
            jax.ShapeDtypeStruct((HEADS, TP, TP), FLOAT),
            jax.ShapeDtypeStruct((4 * TP, D_IN), HALF),
        ],
        scratch_shapes=[pltpu.VMEM((HEADS, TP, SPREAD), FLOAT)],
        compiler_params=params(24 << 20),
        name="expand_bias",
        cost_estimate=cost(2e9, 3e6),
    )(rel_table, spread, picks, cells)


def reduce_bias(dbias_ref, spread_ref, rows_ref):
    row = lax.broadcasted_iota(jnp.int32, (16, TAB), 0)
    lines = []
    for head in range(HEADS):
        hi, lo = split2(dbias_ref[head])
        rows_ref[head, :, :SPREAD] = dot(hi, spread_ref[...]) + dot(lo, spread_ref[...])
        rows_ref[head, :, SPREAD:] = jnp.zeros((TP, TAB - SPREAD), FLOAT)
        total = rows_ref[head, 0:16, :]
        for r in range(1, SIDE):
            piece = rows_ref[head, SIDE * r : SIDE * r + 16, :]
            total = total + pltpu.roll(piece, TAB - REL * r, 1)
        total = jnp.where(row < SIDE, total, 0.0)
        total = jnp.concatenate([total[c : c + 1, :] for c in range(15, -1, -1)], axis=0)
        total = pltpu.roll(total, 0, 1, stride=1, stride_axis=0)
        total = jnp.sum(total, axis=0, keepdims=True)
        total = pltpu.roll(total, 364 - 15, 1)
        lines += [total[:, k * 128 : (k + 1) * 128] for k in range(TAB // 128)]
    return lines


def line(ref):
    return ref[...].reshape(1, ref.shape[0])


def bn_parts(x_ref, coef_ref, scale_ref, bias_ref):
    mean = coef_ref[0:1, :]
    factor = coef_ref[1:2, :] * line(scale_ref) * LOG2E
    shift = line(bias_ref) * LOG2E
    return [
        (x_ref[0, part * TP : (part + 1) * TP, :].astype(FLOAT) - mean) * factor + shift
        for part in range(4)
    ]


def norm_rows(value):
    centre = value - jnp.mean(value, axis=-1, keepdims=True)
    inverse = lax.rsqrt(jnp.mean(centre * centre, axis=-1, keepdims=True) + EPS)
    return centre * inverse, inverse


def put_rows(ref, crop, value):
    for group in range(ref.shape[0]):
        piece = value[:, group * 128 : (group + 1) * 128]
        if piece.shape[1] < 128:
            rest = jnp.zeros((piece.shape[0], 128 - piece.shape[1]), piece.dtype)
            piece = jnp.concatenate([piece, rest], axis=1)
        ref[group, pl.ds(crop, TP, stride=CROPS), :] = piece


def take_rows(ref, crop):
    pieces = [ref[group, pl.ds(crop, TP, stride=CROPS), :] for group in range(ref.shape[0])]
    return jnp.concatenate(pieces, axis=1)


def head_masks():
    lane = lax.broadcasted_iota(jnp.int32, (1, 128), 1)
    return [(lane // HEAD == k).astype(HALF) for k in range(4)]


def attend(
    crop,
    x_ref,
    next_ref,
    picks_ref,
    picked_ref,
    coef_ref,
    bn_scale_ref,
    bn_bias_ref,
    gain_ref,
    shift_ref,
    w_ref,
    bias_ref,
    qkv_ref,
    probs_ref,
    attn_ref,
    pooled_ref,
    plain_ref,
    s_ref,
):
    x_ref[0] = picked_ref[...]
    parts = bn_parts(x_ref, coef_ref, bn_scale_ref, bn_bias_ref)
    top = jnp.maximum(jnp.maximum(parts[0], parts[1]), jnp.maximum(parts[2], parts[3]))
    total = jnp.exp2(parts[0] - top)
    for part in range(1, 4):
        total = total + jnp.exp2(parts[part] - top)
    pooled = top * LN2 + jnp.log(total)
    put_rows(pooled_ref, crop, pooled)
    plain_ref[0] = pooled
    z, _ = norm_rows(pooled)
    first = (z * line(gain_ref) + line(shift_ref)).astype(HALF)
    qkv_ref[0] = dot(first, w_ref[...]).astype(HALF)
    value_t = qkv_ref[0, :, 2 * D :].astype(FLOAT).T.astype(HALF)
    masks = head_masks()

    def start(head):
        group = head // 4
        query = qkv_ref[0, :, group * 128 : (group + 1) * 128] * masks[head % 4]
        key = qkv_ref[0, :, D + group * 128 : D + (group + 1) * 128]
        s_ref[head % 4] = dot(key, query, NT)

    def finish(head):
        rows = slice(head * HEAD, (head + 1) * HEAD)
        return dot(value_t[rows, :], probs_ref[0, head])

    heads = []
    for head in range(3):
        start(head)
    for head in range(HEADS):
        if head + 3 < HEADS:
            start(head + 3)
        if head == 2:
            select_cells(picks_ref, next_ref, picked_ref)
        for cols in (slice(0, 128), slice(128, TP)):
            scores = s_ref[head % 4, :, cols] * (SCALE * LOG2E) + bias_ref[head, :, cols]
            weight = jnp.exp2(scores - jnp.max(scores, axis=0, keepdims=True))
            weight = weight * (1.0 / jnp.sum(weight, axis=0, keepdims=True))
            probs_ref[0, head, :, cols] = weight.astype(HALF)
        if head >= 3:
            heads.append(finish(head - 3))
    for head in range(HEADS - 3, HEADS):
        heads.append(finish(head))
    put_rows(attn_ref, crop, jnp.concatenate(heads, axis=0).T)


def normal_parts(u):
    cdf = lax.erf(u * np.float32(np.sqrt(0.5))) * 0.5 + 0.5
    return cdf, jnp.exp2(u * u * (-0.5 * LOG2E)) * (u * np.float32(1.0 / np.sqrt(2 * np.pi)))


PIECES = 64
EARLY = 72
LATE = 32
DATA = 29
AT_G2 = FF // 128 * (D // 2)
HALF_ROWS = PIECES * EARLY
ROWS_2 = EARLY + LATE
AT_SHORT = 3 * D // 2
AT_LINES = AT_SHORT + 3 * D_IN // 2
TAIL = AT_LINES + 24
AT_TABLE = TAIL + 9 * D_IN // 2
FLAT = PIECES * DATA
assert AT_G2 + FF // 2 // 128 * D == HALF_ROWS and AT_TABLE + 80 <= FLAT

FC_COLS = 768


def feed(
    core,
    attn_ref,
    pooled_ref,
    cot_ref,
    w_short_ref,
    w_out_ref,
    gain_ref,
    shift_ref,
    w1_ref,
    b1_ref,
    w2_ref,
    b2_ref,
    result_ref,
    dattn_ref,
    dshort_ref,
    shared_ref,
    tail_ref,
    message_ref,
    result_hbm,
    dattn_hbm,
    dshort_hbm,
    shared_hbm,
    tail_hbm,
    keep_ref,
    send_ref,
    sems,
    store_sems,
):
    stores = []

    def store(source, target):
        stores.append(pltpu.make_async_copy(source, target, store_sems.at[len(stores)]))
        stores[-1].start()

    def put(half, at, value):
        count = value.shape[0]
        for k in range(value.shape[1] // 128):
            message_ref[half, at + k * count : at + (k + 1) * count, :] = value[
                :, k * 128 : (k + 1) * 128
            ]

    shipped = []

    def ship(half, at, end):
        sem = sems.at[len(shipped)]
        rows = pl.ds(at, end - at)
        to_keep = pltpu.make_async_copy(message_ref.at[half, rows], keep_ref.at[rows], sem)
        to_send = pltpu.make_async_copy(message_ref.at[half, rows], send_ref.at[rows], sem)

        @pl.when(core == half)
        def _():
            to_keep.start()

        @pl.when(core != half)
        def _():
            to_send.start()

        shipped.append(to_keep)

    def attn_all():
        return jnp.concatenate([attn_ref[k, :ROWS] for k in range(3)], axis=1)

    def pooled_all():
        return jnp.concatenate([pooled_ref[k, :ROWS] for k in range(2)], axis=1)[:, :D_IN]

    y1 = dot(pooled_all().astype(HALF), w_short_ref[...]) + dot(
        attn_all().astype(HALF), w_out_ref[...]
    )
    z, inverse = norm_rows(y1)
    gain = line(gain_ref)
    second = (z * gain + line(shift_ref)).astype(HALF)
    result_ref[...] = y1 + line(b2_ref)
    b1 = line(b1_ref)
    back = jnp.zeros((ROWS, D), FLOAT)
    second_t = second.astype(FLOAT).T.astype(HALF)
    cot = cot_ref[...]
    cot_t = cot.astype(FLOAT).T.astype(HALF)
    sums1 = []
    for block in range(FF // FC_COLS):
        cols = slice(block * FC_COLS, (block + 1) * FC_COLS)
        u = dot(second, w1_ref[:, cols]) + b1[:, cols]
        cdf, slope = normal_parts(u)
        hidden = (u * cdf).astype(HALF)
        dhidden = dot(cot, w2_ref[cols, :], NT)
        du = dhidden * (cdf + slope)
        sums1.append(jnp.sum(du, axis=0, keepdims=True))
        du = du.astype(HALF)
        result_ref[...] += dot(hidden, w2_ref[cols, :])
        back = back + dot(du, w1_ref[:, cols], NT)
        g1 = dot(second_t, du)
        at = block * (FC_COLS // 128) * (D // 2)
        for half in range(2):
            put(half, at, g1[half * (D // 2) : (half + 1) * (D // 2)])
            ship(half, at, at + FC_COLS // 128 * (D // 2))
        put(block, AT_G2, dot(cot_t, hidden))
        ship(block, AT_G2, HALF_ROWS)
    store(result_ref, result_hbm)
    dz = back * gain
    dy1 = cot_ref[...].astype(FLOAT) + inverse * (
        dz
        - jnp.mean(dz, axis=-1, keepdims=True)
        - z * jnp.mean(dz * z, axis=-1, keepdims=True)
    )
    low = dy1.astype(HALF)
    dattn = dot(low, w_out_ref[...], NT).astype(HALF).astype(FLOAT)
    for k in range(3):
        dattn_ref[k, :ROWS, :] = dattn[:, k * 128 : (k + 1) * 128]
    dattn_ref[:, ROWS:, :] = jnp.zeros((3, ROWS_P - ROWS, 128), FLOAT)
    store(dattn_ref, dattn_hbm)
    dshort = dot(low, w_short_ref[...], NT)
    dshort_ref[0, :ROWS, :] = dshort[:, :128]
    dshort_ref[1, :ROWS, :] = jnp.concatenate(
        [dshort[:, 128:], jnp.zeros((ROWS, 256 - D_IN), FLOAT)], axis=1
    )
    dshort_ref[:, ROWS:, :] = jnp.zeros((2, ROWS_P - ROWS, 128), FLOAT)
    store(dshort_ref, dshort_hbm)
    lane = lax.broadcasted_iota(jnp.int32, (D, 128), 0) // HEAD
    column = lax.broadcasted_iota(jnp.int32, (D, 128), 1)
    ones = (lane == column).astype(HALF)
    product = attn_all() * dattn
    high = product.astype(HALF)
    rest = (product - high.astype(FLOAT)).astype(HALF)
    shared_ref[:ROWS, :] = dot(high, ones) + dot(rest, ones)
    shared_ref[ROWS:, :] = jnp.zeros((ROWS_P - ROWS, 128), FLOAT)
    store(shared_ref, shared_hbm)
    gout = dot(attn_all().T.astype(HALF), low)
    gshort = dot(pooled_all().T.astype(HALF), low)
    lines = [
        jnp.sum(back * z, axis=0, keepdims=True),
        jnp.sum(back, axis=0, keepdims=True),
        jnp.sum(cot_ref[...].astype(FLOAT), axis=0, keepdims=True),
    ]
    flat = jnp.concatenate(sums1 + lines, axis=1)
    pieces = [flat[:, k * 128 : (k + 1) * 128] for k in range((FF + 3 * D) // 128)]
    pieces.append(jnp.zeros((3, 128), FLOAT))
    lines = jnp.concatenate(pieces, axis=0)
    for half in range(2):
        rows = slice(half * (D // 2), (half + 1) * (D // 2))
        rows_in = slice(half * (D_IN // 2), (half + 1) * (D_IN // 2))
        for k in range(3):
            cols = slice(k * 128, (k + 1) * 128)
            tail_ref[half, k * (D // 2) : (k + 1) * (D // 2), :] = gout[rows, cols]
            at = AT_SHORT + k * (D_IN // 2)
            tail_ref[half, at : at + D_IN // 2, :] = gshort[rows_in, cols]
        tail_ref[half, AT_LINES:TAIL, :] = lines
    store(tail_ref, tail_hbm)
    for copy in shipped + stores:
        copy.wait()


def forward_kernel(
    core_ref,
    gathered_ref,
    picks_ref,
    bn_scale_ref,
    bn_bias_ref,
    gain1_ref,
    shift1_ref,
    wqkv_ref,
    gain2_ref,
    shift2_ref,
    b1_ref,
    b2_ref,
    cells_hbm,
    first_hbm,
    bias_hbm,
    cot_hbm,
    w_short_hbm,
    w_out_hbm,
    w1_hbm,
    w2_hbm,
    coef_ref,
    x_hbm,
    qkv_hbm,
    probs_hbm,
    plain_hbm,
    result_hbm,
    dattn_hbm,
    dshort_hbm,
    shared_hbm,
    tail_hbm,
    keep_hbm,
    send_hbm,
    s_ref,
    picked_ref,
    attn_ref,
    pooled_ref,
    bias_ref,
    cot_ref,
    w_short_ref,
    w_out_ref,
    w1_ref,
    w2_ref,
    result_ref,
    dattn_ref,
    dshort_ref,
    shared_ref,
    tail_ref,
    message_ref,
    step_ref,
    load_sems,
    ship_sems,
    store_sems,
):
    pairs = (
        (first_hbm, picked_ref),
        (bias_hbm, bias_ref),
        (w_short_hbm, w_short_ref),
        (w_out_hbm, w_out_ref),
        (w1_hbm, w1_ref),
        (cot_hbm, cot_ref),
        (w2_hbm, w2_ref),
    )
    loads = [pltpu.make_async_copy(a, b, load_sems.at[k]) for k, (a, b) in enumerate(pairs)]
    for load in loads:
        load.start()
    mean, inv = batch_coefficients(gathered_ref[...])
    coef_ref[...] = jnp.zeros_like(coef_ref)
    coef_ref[0:1, :] = mean
    coef_ref[1:2, :] = inv
    loads[0].wait()
    loads[1].wait()

    step_ref[0] = 0

    def body(next_ref, x_ref, qkv_ref, probs_ref, plain_ref):
        crop = step_ref[0]
        step_ref[0] = crop + 1
        attend(
            crop,
            x_ref,
            next_ref,
            picks_ref,
            picked_ref,
            coef_ref,
            bn_scale_ref,
            bn_bias_ref,
            gain1_ref,
            shift1_ref,
            wqkv_ref,
            bias_ref,
            qkv_ref,
            probs_ref,
            attn_ref,
            pooled_ref,
            plain_ref,
            s_ref,
        )

    by_crop = lambda *shape: pl.BlockSpec((1,) + shape, lambda c: (c,) + (0,) * len(shape))
    pltpu.emit_pipeline(
        body,
        grid=(CROPS,),
        in_specs=[
            pl.BlockSpec((1, D_IN, CELLS), lambda c: (jnp.minimum(c + 1, CROPS - 1), 0, 0))
        ],
        out_specs=[
            by_crop(4 * TP, D_IN),
            by_crop(TP, 3 * D),
            by_crop(HEADS, TP, TP),
            by_crop(TP, D_IN),
        ],
    )(cells_hbm, x_hbm, qkv_hbm, probs_hbm, plain_hbm)
    for load in loads[2:]:
        load.wait()
    feed(
        core_ref[0],
        attn_ref,
        pooled_ref,
        cot_ref,
        w_short_ref,
        w_out_ref,
        gain2_ref,
        shift2_ref,
        w1_ref,
        b1_ref,
        w2_ref,
        b2_ref,
        result_ref,
        dattn_ref,
        dshort_ref,
        shared_ref,
        tail_ref,
        message_ref,
        result_hbm,
        dattn_hbm,
        dshort_hbm,
        shared_hbm,
        tail_hbm,
        keep_hbm,
        send_hbm,
        ship_sems,
        store_sems,
    )


def forward(
    core,
    gathered,
    picks,
    cells,
    first,
    bn_scale,
    bn_bias,
    gain1,
    shift1,
    w_qkv,
    gain2,
    shift2,
    b1,
    b2,
    bias,
    cot,
    w_short,
    w_out,
    w1,
    w2,
):
    hbm = pl.BlockSpec(memory_space=pl.ANY)
    small = (gathered, picks, bn_scale, bn_bias, gain1, shift1, w_qkv, gain2, shift2, b1, b2)
    large = (cells, first, bias, cot, w_short, w_out, w1, w2)
    feed_shapes = [
        (ROWS, D),
        (3, ROWS_P, 128),
        (2, ROWS_P, 128),
        (ROWS_P, 128),
        (2, TAIL, 128),
    ]
    return pl.pallas_call(
        forward_kernel,
        in_specs=[pl.BlockSpec(memory_space=pltpu.SMEM)]
        + [whole(a.shape) for a in small]
        + [hbm] * len(large),
        out_specs=[whole((8, D_IN))] + [hbm] * 11,
        out_shape=[
            jax.ShapeDtypeStruct((8, D_IN), FLOAT),
            jax.ShapeDtypeStruct((CROPS, 4 * TP, D_IN), HALF),
            jax.ShapeDtypeStruct((CROPS, TP, 3 * D), HALF),
            jax.ShapeDtypeStruct((CROPS, HEADS, TP, TP), HALF),
            jax.ShapeDtypeStruct((CROPS, TP, D_IN), FLOAT),
        ]
        + [jax.ShapeDtypeStruct(shape, FLOAT) for shape in feed_shapes]
        + [jax.ShapeDtypeStruct((HALF_ROWS, 128), FLOAT)] * 2,
        scratch_shapes=[
            pltpu.VMEM((4, TP, TP), FLOAT),
            pltpu.VMEM((4 * TP, D_IN), HALF),
            pltpu.VMEM((3, ROWS_P, 128), FLOAT),
            pltpu.VMEM((2, ROWS_P, 128), FLOAT),
        ]
        + [pltpu.VMEM(a.shape, a.dtype) for a in (bias, cot, w_short, w_out, w1, w2)]
        + [pltpu.VMEM(shape, FLOAT) for shape in feed_shapes]
        + [
            pltpu.VMEM((2, HALF_ROWS, 128), FLOAT),
            pltpu.SMEM((1,), jnp.int32),
            pltpu.SemaphoreType.DMA((7,)),
            pltpu.SemaphoreType.DMA((6,)),
            pltpu.SemaphoreType.DMA((5,)),
        ],
        compiler_params=params(),
        name="forward",
        cost_estimate=cost(1.6e10, 5e7, 8e6),
    )(core, *small, *large)


def second_message_kernel(pieces_ref, keep_ref, other_ref, out_ref):
    total = pieces_ref[0]
    for k in range(1, PIECES):
        total = total + pieces_ref[k]
    out_ref[:, :EARLY, :] = jnp.broadcast_to(total[None], (PIECES, EARLY, 128))
    out_ref[:, EARLY:, :] = keep_ref[...] + other_ref[...]


def second_message(pieces, keep, other):
    shape = (PIECES, ROWS_2, 128)
    return pl.pallas_call(
        second_message_kernel,
        in_specs=[whole(a.shape) for a in (pieces, keep, other)],
        out_specs=whole(shape),
        out_shape=jax.ShapeDtypeStruct(shape, FLOAT),
        compiler_params=params(),
        name="second_message",
        cost_estimate=cost(1e6, 7e6),
    )(pieces, keep, other)


def late_sum_kernel(in_hbm, copies_ref, totals_ref, late_ref, sem):
    load = pltpu.make_async_copy(in_hbm.at[:, pl.ds(EARLY, LATE)], late_ref, sem)
    load.start()
    load.wait()
    total = late_ref[0]
    for k in range(1, PIECES):
        total = total + late_ref[k]
    copies_ref[...] = jnp.broadcast_to(total[None], copies_ref.shape)
    totals_ref[...] = total[24:]


def late_sum(arrived):
    shapes = [(PIECES, LATE, 128), (8, 128)]
    return pl.pallas_call(
        late_sum_kernel,
        in_specs=[pl.BlockSpec(memory_space=pl.ANY)],
        out_specs=[whole(shape) for shape in shapes],
        out_shape=[jax.ShapeDtypeStruct(shape, FLOAT) for shape in shapes],
        scratch_shapes=[pltpu.VMEM((PIECES, LATE, 128), FLOAT), pltpu.SemaphoreType.DMA],
        compiler_params=params(),
        name="late_sum",
        cost_estimate=cost(1e5, 2e6),
    )(arrived)


def touch_kernel(*refs):
    del refs


def pass_after(after, value):
    return pl.pallas_call(
        touch_kernel,
        in_specs=[pl.BlockSpec(memory_space=pl.ANY)] * (len(after) + 1),
        out_specs=pl.BlockSpec(memory_space=pl.ANY),
        out_shape=jax.ShapeDtypeStruct(value.shape, value.dtype),
        input_output_aliases={len(after): 0},
        compiler_params=params(),
        name="pass_after",
        cost_estimate=cost(1, 1),
    )(*after, value)


def unpack_kernel(which_ref, early_ref, *refs):
    g1_ref, g2_ref = refs[-2:]

    def read(at, count):
        pieces = []
        while count:
            piece, row = divmod(at, EARLY)
            n = min(count, EARLY - row)
            pieces.append(early_ref[piece, row : row + n, :])
            at, count = at + n, count - n
        return pieces[0] if len(pieces) == 1 else jnp.concatenate(pieces, axis=0)

    for k in range(FF // 128):
        g1_ref[:, k * 128 : (k + 1) * 128] = read(k * D // 2, D // 2)
    for k in range(FF // 256):
        g2_ref[k * 128 : (k + 1) * 128, :] = read(AT_G2 + k * D, D).T


def unpack_late_kernel(which_ref, late_ref, *refs):
    gout_ref, gshort_ref, gqkv_ref = refs[-11:-8]
    db1_ref, dgain2_ref, dshift2_ref, db2_ref, table_ref, dgain1_ref, dshift1_ref = refs[-8:-1]
    flat_ref = refs[-1]
    for piece in range(PIECES):
        flat_ref[piece * DATA : (piece + 1) * DATA, :] = late_ref[piece, :DATA, :]
    for k in range(9):
        cols = slice(k * 128, (k + 1) * 128)
        at = TAIL + k * D_IN // 2
        gqkv_ref[:, cols] = flat_ref[at : at + D_IN // 2, :]
        if k < 3:
            gout_ref[:, cols] = flat_ref[k * D // 2 : (k + 1) * D // 2, :]
            at = AT_SHORT + k * D_IN // 2
            gshort_ref[:, cols] = flat_ref[at : at + D_IN // 2, :]
    lines = flat_ref[AT_LINES:TAIL, :]
    flat = jnp.concatenate([lines[k : k + 1, :] for k in range(21)], axis=1)
    db1_ref[...] = flat[:, :FF].reshape(FF)
    for k, target in enumerate((dgain2_ref, dshift2_ref, db2_ref)):
        target[...] = flat[:, FF + k * D : FF + (k + 1) * D].reshape(D)
    lines = flat_ref[AT_TABLE : AT_TABLE + 80, :]
    per = TAB // 128
    columns = []
    for k in range(per):
        rows = [lines[h * per + k : h * per + k + 1, :] for h in range(HEADS)]
        columns.append(jnp.concatenate(rows, axis=0))
    table_ref[...] = jnp.concatenate(columns, axis=1)[:, : REL * REL]
    for k, target in enumerate((dgain1_ref, dshift1_ref)):
        at = HEADS * per + 2 * k
        both = jnp.concatenate([lines[at : at + 1, :], lines[at + 1 : at + 2, :]], axis=1)
        target[...] = both[:, :D_IN].reshape(D_IN)


def fill(kernel, name, rows, small, scratch, half, message, before):
    shapes = [(2 * a, b) for a, b in rows] + small
    any_spec = pl.BlockSpec(memory_space=pl.ANY)
    return pl.pallas_call(
        kernel,
        grid_spec=pltpu.PrefetchScalarGridSpec(
            num_scalar_prefetch=1,
            grid=(1,),
            in_specs=[pl.BlockSpec(message.shape, lambda i, h: (0, 0, 0))]
            + [any_spec] * len(before),
            out_specs=[pl.BlockSpec(shape, lambda i, h: (h[0], 0)) for shape in rows]
            + [pl.BlockSpec(shape, lambda i, h, n=len(shape): (0,) * n) for shape in small],
            scratch_shapes=scratch,
        ),
        out_shape=[jax.ShapeDtypeStruct(shape, FLOAT) for shape in shapes],
        input_output_aliases={2 + k: k for k in range(len(before))},
        compiler_params=params(20 << 20),
        name=name,
        cost_estimate=cost(1e6, 6e6),
    )(half, message, *before)


def unpack(half, message, before=()):
    rows = [(D // 2, FF), (FF // 2, D)]
    return fill(unpack_kernel, "unpack", rows, [], [], half, message, before)


def unpack_late(half, message, before=()):
    rows = [(D // 2, D), (D_IN // 2, D), (D_IN // 2, 3 * D)]
    small = [(FF,), (D,), (D,), (D,), (HEADS, REL * REL), (D_IN,), (D_IN,)]
    scratch = [pltpu.VMEM((FLAT, 128), FLOAT)]
    return fill(unpack_late_kernel, "unpack_late", rows, small, scratch, half, message, before)


def back_crop(
    crop,
    coef_ref,
    x_ref,
    plain_ref,
    qkv_ref,
    probs_ref,
    dattn_ref,
    dshort_ref,
    shared_ref,
    bn_scale_ref,
    bn_bias_ref,
    gain_ref,
    shift_ref,
    w_ref,
    dbias_ref,
    gw_ref,
    sums_ref,
    dcells_ref,
    dp_ref,
    ds_ref,
):
    dattn = take_rows(dattn_ref, crop).astype(HALF)
    shared = shared_ref[pl.ds(crop, TP, stride=CROPS), :].T
    key_t = qkv_ref[0, :, D : 2 * D].astype(FLOAT).T.astype(HALF)
    masks = head_masks()
    dquery_t, dkeys, dvalues = [], [], []

    def start(head):
        group = head // 4
        grad = dattn[:, group * 128 : (group + 1) * 128] * masks[head % 4]
        value = qkv_ref[0, :, 2 * D + group * 128 : 2 * D + (group + 1) * 128]
        dp_ref[head % 3] = dot(value, grad, NT)
        dvalues.append(dot(probs_ref[0, head], grad))

    def finish(head):
        group = head // 4
        query = qkv_ref[0, :, group * 128 : (group + 1) * 128] * masks[head % 4]
        dscores = ds_ref[head % 3]
        dkeys.append(dot(dscores, query))
        dquery_t.append(dot(key_t[head * HEAD : (head + 1) * HEAD, :], dscores))

    for head in range(2):
        start(head)
    for head in range(HEADS):
        if head + 2 < HEADS:
            start(head + 2)
        for cols in (slice(0, 128), slice(128, TP)):
            probs = probs_ref[0, head, :, cols].astype(FLOAT)
            dscores = probs * (dp_ref[head % 3, :, cols] - shared[head : head + 1, cols])
            dbias_ref[head, :, cols] += dscores
            ds_ref[head % 3, :, cols] = dscores.astype(HALF)
        if head >= 2:
            finish(head - 2)
    for head in range(HEADS - 2, HEADS):
        finish(head)
    group_sum = lambda items, g: sum(items[4 * g + 1 : 4 * g + 4], items[4 * g])
    dquery = jnp.concatenate(dquery_t, axis=0).T * SCALE
    dqkv = jnp.concatenate(
        [dquery]
        + [group_sum(dkeys, g) * SCALE for g in range(3)]
        + [group_sum(dvalues, g) for g in range(3)],
        axis=1,
    ).astype(HALF)
    pooled = plain_ref[0]
    z, inverse = norm_rows(pooled)
    gain = line(gain_ref)
    first_t = (z * gain + line(shift_ref)).T.astype(HALF)
    gw_ref[...] += dot(first_t, dqkv)
    dfirst = dot(dqkv, w_ref[...], NT)
    dz = dfirst * gain
    dpooled = take_rows(dshort_ref, crop)[:, :D_IN] + inverse * (
        dz
        - jnp.mean(dz, axis=-1, keepdims=True)
        - z * jnp.mean(dz * z, axis=-1, keepdims=True)
    )
    sums_ref[0:1, :] += jnp.sum(dfirst * z, axis=0, keepdims=True)
    sums_ref[1:2, :] += jnp.sum(dfirst, axis=0, keepdims=True)
    level = pooled * LOG2E
    parts = bn_parts(x_ref, coef_ref, bn_scale_ref, bn_bias_ref)
    along = jnp.zeros((TP, D_IN), FLOAT)
    total = jnp.zeros((TP, D_IN), FLOAT)
    for part in range(4):
        dpart = dpooled * jnp.exp2(parts[part] - level)
        dcells_ref[0, part * TP : (part + 1) * TP, :] = dpart.astype(HALF)
        raw = x_ref[0, part * TP : (part + 1) * TP, :].astype(FLOAT)
        along = along + dpart * (raw - coef_ref[0:1, :])
        total = total + dpart
    sums_ref[2:3, :] += jnp.sum(along, axis=0, keepdims=True) * coef_ref[1:2, :]
    sums_ref[3:4, :] += jnp.sum(total, axis=0, keepdims=True)


def back_kernel(
    core_ref,
    after_ref,
    coef_ref,
    bn_scale_ref,
    bn_bias_ref,
    gain_ref,
    shift_ref,
    w_ref,
    spread_ref,
    x_hbm,
    plain_hbm,
    qkv_hbm,
    probs_hbm,
    dattn_hbm,
    dshort_hbm,
    shared_hbm,
    tail_hbm,
    keep_ref,
    send_ref,
    dcells_hbm,
    dattn_ref,
    dshort_ref,
    shared_ref,
    tail_ref,
    dbias_ref,
    gw_ref,
    sums_ref,
    dp_ref,
    ds_ref,
    rows_ref,
    flat_ref,
    step_ref,
    load_sems,
):
    pairs = (
        (dattn_hbm, dattn_ref),
        (dshort_hbm, dshort_ref),
        (shared_hbm, shared_ref),
        (tail_hbm, tail_ref),
    )
    loads = [pltpu.make_async_copy(a, b, load_sems.at[k]) for k, (a, b) in enumerate(pairs)]
    for load in loads:
        load.start()
    dbias_ref[...] = jnp.zeros_like(dbias_ref)
    gw_ref[...] = jnp.zeros_like(gw_ref)
    sums_ref[...] = jnp.zeros_like(sums_ref)
    step_ref[0] = 0
    for load in loads:
        load.wait()

    def body(x_ref, plain_ref, qkv_ref, probs_ref, dcells_ref):
        crop = step_ref[0]
        step_ref[0] = crop + 1
        back_crop(
            crop,
            coef_ref,
            x_ref,
            plain_ref,
            qkv_ref,
            probs_ref,
            dattn_ref,
            dshort_ref,
            shared_ref,
            bn_scale_ref,
            bn_bias_ref,
            gain_ref,
            shift_ref,
            w_ref,
            dbias_ref,
            gw_ref,
            sums_ref,
            dcells_ref,
            dp_ref,
            ds_ref,
        )

    by_crop = lambda *shape: pl.BlockSpec((1,) + shape, lambda c: (c,) + (0,) * len(shape))
    pltpu.emit_pipeline(
        body,
        grid=(CROPS,),
        in_specs=[
            by_crop(4 * TP, D_IN),
            by_crop(TP, D_IN),
            by_crop(TP, 3 * D),
            by_crop(HEADS, TP, TP),
        ],
        out_specs=[by_crop(4 * TP, D_IN)],
    )(x_hbm, plain_hbm, qkv_hbm, probs_hbm, dcells_hbm)

    lines = reduce_bias(dbias_ref, spread_ref, rows_ref)
    pad = jnp.zeros((1, 256 - D_IN), FLOAT)
    for k in range(2):
        value = jnp.concatenate([sums_ref[k : k + 1, :], pad], axis=1)
        lines += [value[:, :128], value[:, 128:]]
    lines.append(jnp.zeros((FLAT - AT_TABLE - len(lines), 128), FLOAT))
    flat_ref[AT_TABLE:, :] = jnp.concatenate(lines, axis=0)
    totals = jnp.concatenate([sums_ref[2:3, :], sums_ref[3:4, :]], axis=1)
    totals = jnp.concatenate([totals[:, k * 128 : (k + 1) * 128] for k in range(3)], axis=0)

    def write(ref, half):
        flat_ref[:TAIL, :] = tail_ref[half]
        for k in range(9):
            at = TAIL + k * D_IN // 2
            flat_ref[at : at + D_IN // 2, :] = gw_ref[
                half * (D_IN // 2) : (half + 1) * (D_IN // 2), k * 128 : (k + 1) * 128
            ]
        for piece in range(PIECES):
            ref[piece, :DATA, :] = flat_ref[piece * DATA : (piece + 1) * DATA, :]
            ref[piece, DATA:, :] = totals

    @pl.when(core_ref[0] == 0)
    def _():
        write(keep_ref, 0)
        write(send_ref, 1)

    @pl.when(core_ref[0] != 0)
    def _():
        write(keep_ref, 1)
        write(send_ref, 0)


def attention_back(
    core,
    after,
    coef,
    bn_scale,
    bn_bias,
    gain,
    shift,
    w_qkv,
    spread,
    picked,
    plain,
    qkv,
    probs,
    dattn,
    dshort,
    shared,
    tail,
):
    hbm = pl.BlockSpec(memory_space=pl.ANY)
    small = (coef, bn_scale, bn_bias, gain, shift, w_qkv, spread)
    large = (picked, plain, qkv, probs, dattn, dshort, shared, tail)
    message = (PIECES, LATE, 128)
    return pl.pallas_call(
        back_kernel,
        in_specs=[pl.BlockSpec(memory_space=pltpu.SMEM), hbm]
        + [whole(a.shape) for a in small]
        + [hbm] * len(large),
        out_specs=[whole(message), whole(message), hbm],
        out_shape=[
            jax.ShapeDtypeStruct(message, FLOAT),
            jax.ShapeDtypeStruct(message, FLOAT),
            jax.ShapeDtypeStruct((CROPS, 4 * TP, D_IN), HALF),
        ],
        scratch_shapes=[pltpu.VMEM(a.shape, FLOAT) for a in (dattn, dshort, shared, tail)]
        + [
            pltpu.VMEM((HEADS, TP, TP), FLOAT),
            pltpu.VMEM((D_IN, 3 * D), FLOAT),
            pltpu.VMEM((8, D_IN), FLOAT),
            pltpu.VMEM((3, TP, TP), FLOAT),
            pltpu.VMEM((3, TP, TP), HALF),
            pltpu.VMEM((HEADS, TP, TAB), FLOAT),
            pltpu.VMEM((FLAT, 128), FLOAT),
            pltpu.SMEM((1,), jnp.int32),
            pltpu.SemaphoreType.DMA((4,)),
        ],
        compiler_params=params(),
        name="attention_back",
        cost_estimate=cost(8e9, 4e7, 2e6),
    )(core, after, *small, *large)


def scatter_kernel(s_ref, d_ref, out_ref):
    for k in range(d_ref.shape[0]):
        for low, high, first, last in CELL_CHUNKS:
            value = None
            for part in range(4):
                rows = slice(part * TP + first, part * TP + last)
                term = dot(d_ref[k, rows, :], s_ref[rows, low:high], TN)
                value = term if value is None else value + term
            out_ref[k, :, low:high] = value.astype(HALF)


def scatter_cells(places, dcells):
    each = 2
    return pl.pallas_call(
        scatter_kernel,
        grid=(CROPS // each,),
        in_specs=[
            whole((4 * TP, CELLS)),
            pl.BlockSpec((each, 4 * TP, D_IN), lambda c: (c, 0, 0)),
        ],
        out_specs=pl.BlockSpec((each, D_IN, CELLS), lambda c: (c, 0, 0)),
        out_shape=jax.ShapeDtypeStruct((CROPS, D_IN, CELLS), HALF),
        compiler_params=params(16 << 20),
        name="scatter_cells",
        cost_estimate=cost(3e9, 8e6),
    )(places, dcells)


def column(row):
    return jnp.broadcast_to(row, (128, D_IN)).T[:, 0:1]


def cells_kernel(count, totals_ref, coef_ref, scale_ref, d_ref, x_ref, out_ref, dscale_ref, dshift_ref, cols_ref):
    @pl.when(pl.program_id(0) == 0)
    def _():
        rows = [totals_ref[k : k + 1, :] for k in range(8 - (LATE - DATA), 8)]
        totals = jnp.concatenate(rows, axis=1)
        along = totals[:, :D_IN]
        plain = totals[:, D_IN:]
        dscale_ref[...] = along.reshape(D_IN)
        dshift_ref[...] = plain.reshape(D_IN)
        mean = coef_ref[0:1, :]
        inv = coef_ref[1:2, :]
        factor = inv * line(scale_ref)
        share = 1.0 / float(count * CROPS * CELLS)
        slope = factor * along * inv * share
        cols_ref[:, 0:1] = column(factor)
        cols_ref[:, 1:2] = column(factor * plain * share)
        cols_ref[:, 2:3] = column(slope)
        cols_ref[:, 3:4] = column(mean)

    out_ref[0] = (
        d_ref[0].astype(FLOAT) * cols_ref[:, 0:1]
        - cols_ref[:, 1:2]
        - (x_ref[0].astype(FLOAT) - cols_ref[:, 3:4]) * cols_ref[:, 2:3]
    )


def cell_gradient(count, totals, coef, bn_scale, dcells, cells):
    crop_block = pl.BlockSpec((1, D_IN, CELLS), lambda c: (c, 0, 0))
    return pl.pallas_call(
        functools.partial(cells_kernel, count),
        grid=(CROPS,),
        in_specs=[
            whole((8, 128)),
            whole((8, D_IN)),
            whole((D_IN,)),
            crop_block,
            crop_block,
        ],
        out_specs=[crop_block, whole((D_IN,)), whole((D_IN,))],
        out_shape=[
            jax.ShapeDtypeStruct((CROPS, D_IN, CELLS), FLOAT),
            jax.ShapeDtypeStruct((D_IN,), FLOAT),
            jax.ShapeDtypeStruct((D_IN,), FLOAT),
        ],
        scratch_shapes=[pltpu.VMEM((D_IN, 128), FLOAT)],
        compiler_params=params(16 << 20),
        name="cell_gradient",
        cost_estimate=cost(1e7, 1.5e7),
    )(totals, coef, bn_scale, dcells, cells)


CHIPS = ("y", "x", "z")
ALL = ("y", "x", "z", "core")


def gather_rows(copies):
    if copies.shape[0] == 1:
        return copies
    return lax.all_to_all(copies, ALL, 0, 0)


def on_device(
    count,
    features,
    bn_scale,
    bn_bias,
    w_short,
    ln1_gain,
    ln1_bias,
    w_qkv,
    rel_table,
    w_out,
    ln2_gain,
    ln2_bias,
    w_fc1,
    fc1_bias,
    w_fc2,
    fc2_bias,
    cotangent,
):
    picks = jnp.asarray(select_matrix(), HALF)
    places = jnp.asarray(scatter_matrix(), HALF)
    spread = jnp.asarray(spread_matrix(), HALF)
    spread_back = jnp.asarray(spread_matrix().T, HALF)
    core = lax.axis_index("core").astype(jnp.int32).reshape(1)
    cells = features.transpose(0, 2, 1)
    cot = cotangent.transpose(1, 0, 2).reshape(ROWS, D)
    stats = gather_rows(local_stats(cells, count))
    bias, first = expand_bias(rel_table, spread, picks, cells)
    coef, picked, qkv, probs, plain, out, dattn, dshort, shared, tail, keep, send = forward(
        core,
        stats,
        picks,
        cells,
        first,
        bn_scale,
        bn_bias,
        ln1_gain,
        ln1_bias,
        w_qkv,
        ln2_gain,
        ln2_bias,
        fc1_bias,
        fc2_bias,
        bias,
        cot,
        w_short,
        w_out,
        w_fc1,
        w_fc2,
    )
    swap = [(0, 1), (1, 0)]
    keep = keep.reshape(PIECES, EARLY, 128)
    send = send.reshape(PIECES, EARLY, 128)
    mine = keep
    if count > 1:
        mine = keep + lax.ppermute(send, "core", swap)
        pieces = lax.all_to_all(mine, CHIPS, 0, 0)
    late_keep, late_send, dcells = attention_back(
        core,
        mine,
        coef,
        bn_scale,
        bn_bias,
        ln1_gain,
        ln1_bias,
        w_qkv,
        spread_back,
        picked,
        plain,
        qkv,
        probs,
        dattn,
        dshort,
        shared,
        tail,
    )
    scattered = scatter_cells(places, dcells)
    if count > 1:
        late = lax.ppermute(late_send, "core", swap)
        own = lax.all_to_all(second_message(pieces, late_keep, late), CHIPS, 0, 0)
        own = pass_after((scattered,), own)
        copies, totals = late_sum(own)
        own_late = lax.all_to_all(copies, CHIPS, 0, 0)
        other = lax.ppermute(own, "core", swap)
    else:
        totals = late_keep[0, 24:]
        own, other = keep, send
        own_late, other_late = late_keep, late_send
    grad_cells, dscale, dshift = cell_gradient(count, totals, coef, bn_scale, scattered, cells)
    g1, g2 = unpack(1 - core, other, unpack(core, own))
    if count > 1:
        own_late = pass_after((g1, grad_cells), own_late)
        other_late = lax.ppermute(own_late, "core", swap)
    grads = unpack_late(core, own_late)
    gout, gshort, gqkv = unpack_late(1 - core, other_late, grads[:3])[:3]
    db1, dgain2, dshift2, db2, table, dgain1, dshift1 = grads[3:]
    return (
        out.reshape(TOK, CROPS, D).transpose(1, 0, 2),
        grad_cells.transpose(0, 2, 1),
        dscale,
        dshift,
        gshort,
        dgain1,
        dshift1,
        gqkv,
        table,
        gout,
        dgain2,
        dshift2,
        g1,
        db1,
        g2,
        db2,
    )


def solution(mesh):
    count = mesh.size
    shape = (4, 4, 4, 2) if count == 128 else (1, 1, 1, 1)
    grid = jax.sharding.Mesh(mesh.devices.reshape(shape), ALL)
    split = P(ALL, None, None)
    same = P()
    in_specs = (split,) + (same,) * 14 + (split,)
    out_specs = (split, split) + (same,) * 14

    def run(*args):
        return on_device(count, *args)

    return jax.shard_map(run, mesh=grid, in_specs=in_specs, out_specs=out_specs, check_vma=False)
```

```python
import functools

import jax
import jax.numpy as jnp
import numpy as np
from jax import lax
from jax.experimental import pallas as pl
from jax.experimental.pallas import tpu as pltpu
from jax.sharding import PartitionSpec as P

HEADS = 12
HEAD = 32
SIDE = 14
TOK = 196
TP = 208
GRID2 = 2 * SIDE
CELLS = 784
D_IN = 192
D = 384
FF = 1536
CROPS = 8
ROWS = TOK * CROPS
ROWS_P = TP * CROPS
REL = 27
TAB = 768
SPREAD = 384

EPS = 1e-05
FLOAT = jnp.float32
HALF = jnp.bfloat16
LOG2E = 1.4426950408889634
LN2 = 0.6931471805599453
SCALE = HEAD ** (-0.5)
NN = (((1,), (0,)), ((), ()))
NT = (((1,), (1,)), ((), ()))
TN = (((0,), (0,)), ((), ()))
VMEM_LIMIT = 56 * 1024 * 1024


def dot(left, right, dims=NN):
    return lax.dot_general(left, right, dims, preferred_element_type=FLOAT)


def split2(value):
    hi = value.astype(HALF)
    return hi, (value - hi.astype(FLOAT)).astype(HALF)


def params(limit=VMEM_LIMIT):
    return pltpu.CompilerParams(vmem_limit_bytes=limit)


def cost(flops, bytes_accessed, transcendentals=0):
    return pl.CostEstimate(
        flops=int(flops), bytes_accessed=int(bytes_accessed), transcendentals=int(transcendentals)
    )


def whole(shape):
    return pl.BlockSpec(shape, lambda *_: (0,) * len(shape))


CHUNKS = (
    (0, 48, 0, 256),
    (48, 80, 0, 512),
    (80, 112, 256, 512),
    (112, 144, 256, 768),
    (144, 176, 512, 768),
    (176, TP, 512, CELLS),
)
CELL_CHUNKS = ((0, 256, 0, 80), (256, 512, 48, 144), (512, CELLS, 112, TP))


def cell_of(part, token):
    i, j = divmod(token, SIDE)
    a, b = divmod(part, 2)
    return (2 * i + a) * GRID2 + 2 * j + b


def select_matrix():
    rows = []
    for first, last, low, high in CHUNKS:
        for part in range(4):
            block = np.zeros((last - first, CELLS), np.float32)
            for t in range(first, min(last, TOK)):
                assert low <= cell_of(part, t) < high
                block[t - first, cell_of(part, t)] = 1.0
            rows.append(block)
    return np.concatenate(rows)


def scatter_matrix():
    table = np.zeros((4 * TP, CELLS), np.float32)
    for low, high, first, last in CELL_CHUNKS:
        for part in range(4):
            for t in range(TOK):
                if low <= cell_of(part, t) < high:
                    assert first <= t < last
                    table[part * TP + t, cell_of(part, t)] = 1.0
    return table


def spread_matrix():
    table = np.zeros((SPREAD, TP), np.float32)
    for t in range(TOK):
        i, j = divmod(t, SIDE)
        table[REL * i + j, t] = 1.0
    return table


def stats_kernel(x_ref, out_ref):
    pieces = []
    step = 32
    for block in range(D_IN // step):
        rows = slice(block * step, (block + 1) * step)
        total = x_ref[0, rows, :].astype(FLOAT)
        for crop in range(1, CROPS):
            total = total + x_ref[crop, rows, :].astype(FLOAT)
        total = jnp.sum(total, axis=1, keepdims=True)
        mean = total * (1.0 / (CROPS * CELLS))
        square = jnp.zeros((step, CELLS), FLOAT)
        for crop in range(CROPS):
            centre = x_ref[crop, rows, :].astype(FLOAT) - mean
            square = square + centre * centre
        square = jnp.sum(square, axis=1, keepdims=True)
        lane = lax.broadcasted_iota(jnp.int32, (step, 128), 1)
        pieces.append(jnp.where(lane == 0, mean, jnp.where(lane == 1, square, 0.0)))
    turned = jnp.concatenate(pieces, axis=0).T
    pad = jnp.zeros((1, 64), FLOAT)
    row = jnp.concatenate([turned[0:1], pad, turned[1:2], pad], axis=1)
    out_ref[...] = jnp.broadcast_to(row[None], out_ref.shape)


def local_stats(cells, copies):
    return pl.pallas_call(
        stats_kernel,
        out_shape=jax.ShapeDtypeStruct((copies, 1, 512), FLOAT),
        compiler_params=params(),
        name="stats",
        cost_estimate=cost(8e6, 2.8e6),
    )(cells)


def batch_coefficients(gathered):
    count = gathered.shape[0]
    means = gathered[:, 0, 0:D_IN]
    squares = gathered[:, 0, 256 : 256 + D_IN]
    mean = jnp.sum(means, axis=0, keepdims=True) * (1.0 / count)
    off = means - mean
    local = float(CROPS * CELLS)
    var = jnp.sum(squares, axis=0, keepdims=True) + local * jnp.sum(
        off * off, axis=0, keepdims=True
    )
    return mean, lax.rsqrt(var * (1.0 / (local * count)) + EPS)


def select_cells(s_ref, x_ref, out_ref):
    at = 0
    for first, last, low, high in CHUNKS:
        size = last - first
        picked = dot(s_ref[at : at + 4 * size, low:high], x_ref[0, :, low:high], NT).astype(HALF)
        for part in range(4):
            start = part * TP + first
            out_ref[start : start + size, :] = picked[part * size : (part + 1) * size]
        at += 4 * size


def bias_kernel(table_ref, spread_ref, picks_ref, cells_ref, out_ref, picked_ref, rows_ref):
    select_cells(picks_ref, cells_ref, picked_ref)
    row = lax.broadcasted_iota(jnp.int32, (TP, TP), 0)
    for head in range(HEADS):
        pad = jnp.zeros((1, TAB - REL * REL), FLOAT)
        table = jnp.concatenate([table_ref[head : head + 1, :] * LOG2E, pad], axis=1)
        base = pltpu.roll(jnp.broadcast_to(table, (16, TAB)), 0, 1, stride=1, stride_axis=0)
        for r in range(SIDE):
            rolled = pltpu.roll(base, (TAB - 364 + REL * r) % TAB, 1)
            rows_ref[head, SIDE * r : SIDE * (r + 1), :] = rolled[:SIDE, :SPREAD]
        rows_ref[head, TOK:, :] = jnp.zeros((TP - TOK, SPREAD), FLOAT)
        hi, lo = split2(rows_ref[head])
        value = dot(hi, spread_ref[...]) + dot(lo, spread_ref[...])
        out_ref[head] = jnp.where(row < TOK, value, -1e30)


def expand_bias(rel_table, spread, picks, cells):
    first = pl.BlockSpec((1, D_IN, CELLS), lambda i: (0, 0, 0))
    return pl.pallas_call(
        bias_kernel,
        grid=(1,),
        in_specs=[whole(rel_table.shape), whole(spread.shape), whole(picks.shape), first],
        out_specs=[whole((HEADS, TP, TP)), whole((4 * TP, D_IN))],
        out_shape=[
            jax.ShapeDtypeStruct((HEADS, TP, TP), FLOAT),
            jax.ShapeDtypeStruct((4 * TP, D_IN), HALF),
        ],
        scratch_shapes=[pltpu.VMEM((HEADS, TP, SPREAD), FLOAT)],
        compiler_params=params(24 << 20),
        name="expand_bias",
        cost_estimate=cost(2e9, 3e6),
    )(rel_table, spread, picks, cells)


def reduce_bias(dbias_ref, spread_ref, rows_ref):
    row = lax.broadcasted_iota(jnp.int32, (16, TAB), 0)
    lines = []
    for head in range(HEADS):
        hi, lo = split2(dbias_ref[head])
        rows_ref[head, :, :SPREAD] = dot(hi, spread_ref[...]) + dot(lo, spread_ref[...])
        rows_ref[head, :, SPREAD:] = jnp.zeros((TP, TAB - SPREAD), FLOAT)
        total = rows_ref[head, 0:16, :]
        for r in range(1, SIDE):
            piece = rows_ref[head, SIDE * r : SIDE * r + 16, :]
            total = total + pltpu.roll(piece, TAB - REL * r, 1)
        total = jnp.where(row < SIDE, total, 0.0)
        total = jnp.concatenate([total[c : c + 1, :] for c in range(15, -1, -1)], axis=0)
        total = pltpu.roll(total, 0, 1, stride=1, stride_axis=0)
        total = jnp.sum(total, axis=0, keepdims=True)
        total = pltpu.roll(total, 364 - 15, 1)
        lines += [total[:, k * 128 : (k + 1) * 128] for k in range(TAB // 128)]
    return lines


def line(ref):
    return ref[...].reshape(1, ref.shape[0])


def bn_parts(x_ref, coef_ref, scale_ref, bias_ref):
    mean = coef_ref[0:1, :]
    factor = coef_ref[1:2, :] * line(scale_ref) * LOG2E
    shift = line(bias_ref) * LOG2E
    return [
        (x_ref[0, part * TP : (part + 1) * TP, :].astype(FLOAT) - mean) * factor + shift
        for part in range(4)
    ]


def norm_rows(value):
    centre = value - jnp.mean(value, axis=-1, keepdims=True)
    inverse = lax.rsqrt(jnp.mean(centre * centre, axis=-1, keepdims=True) + EPS)
    return centre * inverse, inverse


def put_rows(ref, crop, value):
    for group in range(ref.shape[0]):
        piece = value[:, group * 128 : (group + 1) * 128]
        if piece.shape[1] < 128:
            rest = jnp.zeros((piece.shape[0], 128 - piece.shape[1]), piece.dtype)
            piece = jnp.concatenate([piece, rest], axis=1)
        ref[group, pl.ds(crop, TP, stride=CROPS), :] = piece


def take_rows(ref, crop):
    pieces = [ref[group, pl.ds(crop, TP, stride=CROPS), :] for group in range(ref.shape[0])]
    return jnp.concatenate(pieces, axis=1)


def head_masks():
    lane = lax.broadcasted_iota(jnp.int32, (1, 128), 1)
    return [(lane // HEAD == k).astype(HALF) for k in range(4)]


def attend(
    crop,
    x_ref,
    next_ref,
    picks_ref,
    picked_ref,
    coef_ref,
    bn_scale_ref,
    bn_bias_ref,
    gain_ref,
    shift_ref,
    w_ref,
    bias_ref,
    qkv_ref,
    probs_ref,
    attn_ref,
    pooled_ref,
    plain_ref,
    s_ref,
):
    x_ref[0] = picked_ref[...]
    parts = bn_parts(x_ref, coef_ref, bn_scale_ref, bn_bias_ref)
    top = jnp.maximum(jnp.maximum(parts[0], parts[1]), jnp.maximum(parts[2], parts[3]))
    total = jnp.exp2(parts[0] - top)
    for part in range(1, 4):
        total = total + jnp.exp2(parts[part] - top)
    pooled = top * LN2 + jnp.log(total)
    put_rows(pooled_ref, crop, pooled)
    plain_ref[0] = pooled
    z, _ = norm_rows(pooled)
    first = (z * line(gain_ref) + line(shift_ref)).astype(HALF)
    qkv_ref[0] = dot(first, w_ref[...]).astype(HALF)
    value_t = qkv_ref[0, :, 2 * D :].astype(FLOAT).T.astype(HALF)
    masks = head_masks()

    def start(head):
        group = head // 4
        query = qkv_ref[0, :, group * 128 : (group + 1) * 128] * masks[head % 4]
        key = qkv_ref[0, :, D + group * 128 : D + (group + 1) * 128]
        s_ref[head % 4] = dot(key, query, NT)

    def finish(head):
        rows = slice(head * HEAD, (head + 1) * HEAD)
        return dot(value_t[rows, :], probs_ref[0, head])

    heads = []
    for head in range(3):
        start(head)
    for head in range(HEADS):
        if head + 3 < HEADS:
            start(head + 3)
        if head == 2:
            select_cells(picks_ref, next_ref, picked_ref)
        for cols in (slice(0, 128), slice(128, TP)):
            scores = s_ref[head % 4, :, cols] * (SCALE * LOG2E) + bias_ref[head, :, cols]
            weight = jnp.exp2(scores - jnp.max(scores, axis=0, keepdims=True))
            weight = weight * (1.0 / jnp.sum(weight, axis=0, keepdims=True))
            probs_ref[0, head, :, cols] = weight.astype(HALF)
        if head >= 3:
            heads.append(finish(head - 3))
    for head in range(HEADS - 3, HEADS):
        heads.append(finish(head))
    put_rows(attn_ref, crop, jnp.concatenate(heads, axis=0).T)


def normal_parts(u):
    cdf = lax.erf(u * np.float32(np.sqrt(0.5))) * 0.5 + 0.5
    return cdf, jnp.exp2(u * u * (-0.5 * LOG2E)) * (u * np.float32(1.0 / np.sqrt(2 * np.pi)))


PIECES = 64
EARLY = 72
LATE = 32
DATA = 29
AT_G2 = FF // 128 * (D // 2)
HALF_ROWS = PIECES * EARLY
ROWS_2 = EARLY + LATE
AT_SHORT = 3 * D // 2
AT_LINES = AT_SHORT + 3 * D_IN // 2
TAIL = AT_LINES + 24
AT_TABLE = TAIL + 9 * D_IN // 2
FLAT = PIECES * DATA
assert AT_G2 + FF // 2 // 128 * D == HALF_ROWS and AT_TABLE + 80 <= FLAT

FC_COLS = 768


def feed(
    core,
    attn_ref,
    pooled_ref,
    cot_ref,
    w_short_ref,
    w_out_ref,
    gain_ref,
    shift_ref,
    w1_ref,
    b1_ref,
    w2_ref,
    b2_ref,
    result_ref,
    dattn_ref,
    dshort_ref,
    shared_ref,
    tail_ref,
    message_ref,
    result_hbm,
    dattn_hbm,
    dshort_hbm,
    shared_hbm,
    tail_hbm,
    keep_ref,
    send_ref,
    sems,
    store_sems,
):
    stores = []

    def store(source, target):
        stores.append(pltpu.make_async_copy(source, target, store_sems.at[len(stores)]))
        stores[-1].start()

    def put(half, at, value):
        count = value.shape[0]
        for k in range(value.shape[1] // 128):
            message_ref[half, at + k * count : at + (k + 1) * count, :] = value[
                :, k * 128 : (k + 1) * 128
            ]

    shipped = []

    def ship(half, at, end):
        sem = sems.at[len(shipped)]
        rows = pl.ds(at, end - at)
        to_keep = pltpu.make_async_copy(message_ref.at[half, rows], keep_ref.at[rows], sem)
        to_send = pltpu.make_async_copy(message_ref.at[half, rows], send_ref.at[rows], sem)

        @pl.when(core == half)
        def _():
            to_keep.start()

        @pl.when(core != half)
        def _():
            to_send.start()

        shipped.append(to_keep)

    def attn_all():
        return jnp.concatenate([attn_ref[k, :ROWS] for k in range(3)], axis=1)

    def pooled_all():
        return jnp.concatenate([pooled_ref[k, :ROWS] for k in range(2)], axis=1)[:, :D_IN]

    y1 = dot(pooled_all().astype(HALF), w_short_ref[...]) + dot(
        attn_all().astype(HALF), w_out_ref[...]
    )
    z, inverse = norm_rows(y1)
    gain = line(gain_ref)
    second = (z * gain + line(shift_ref)).astype(HALF)
    result_ref[...] = y1 + line(b2_ref)
    b1 = line(b1_ref)
    back = jnp.zeros((ROWS, D), FLOAT)
    second_t = second.astype(FLOAT).T.astype(HALF)
    cot = cot_ref[...]
    cot_t = cot.astype(FLOAT).T.astype(HALF)
    sums1 = []
    for block in range(FF // FC_COLS):
        cols = slice(block * FC_COLS, (block + 1) * FC_COLS)
        u = dot(second, w1_ref[:, cols]) + b1[:, cols]
        cdf, slope = normal_parts(u)
        hidden = (u * cdf).astype(HALF)
        dhidden = dot(cot, w2_ref[cols, :], NT)
        du = dhidden * (cdf + slope)
        sums1.append(jnp.sum(du, axis=0, keepdims=True))
        du = du.astype(HALF)
        result_ref[...] += dot(hidden, w2_ref[cols, :])
        back = back + dot(du, w1_ref[:, cols], NT)
        g1 = dot(second_t, du)
        at = block * (FC_COLS // 128) * (D // 2)
        for half in range(2):
            put(half, at, g1[half * (D // 2) : (half + 1) * (D // 2)])
            ship(half, at, at + FC_COLS // 128 * (D // 2))
        put(block, AT_G2, dot(cot_t, hidden))
        ship(block, AT_G2, HALF_ROWS)
    store(result_ref, result_hbm)
    dz = back * gain
    dy1 = cot_ref[...].astype(FLOAT) + inverse * (
        dz
        - jnp.mean(dz, axis=-1, keepdims=True)
        - z * jnp.mean(dz * z, axis=-1, keepdims=True)
    )
    low = dy1.astype(HALF)
    dattn = dot(low, w_out_ref[...], NT).astype(HALF).astype(FLOAT)
    for k in range(3):
        dattn_ref[k, :ROWS, :] = dattn[:, k * 128 : (k + 1) * 128]
    dattn_ref[:, ROWS:, :] = jnp.zeros((3, ROWS_P - ROWS, 128), FLOAT)
    store(dattn_ref, dattn_hbm)
    dshort = dot(low, w_short_ref[...], NT)
    dshort_ref[0, :ROWS, :] = dshort[:, :128]
    dshort_ref[1, :ROWS, :] = jnp.concatenate(
        [dshort[:, 128:], jnp.zeros((ROWS, 256 - D_IN), FLOAT)], axis=1
    )
    dshort_ref[:, ROWS:, :] = jnp.zeros((2, ROWS_P - ROWS, 128), FLOAT)
    store(dshort_ref, dshort_hbm)
    lane = lax.broadcasted_iota(jnp.int32, (D, 128), 0) // HEAD
    column = lax.broadcasted_iota(jnp.int32, (D, 128), 1)
    ones = (lane == column).astype(HALF)
    product = attn_all() * dattn
    high = product.astype(HALF)
    rest = (product - high.astype(FLOAT)).astype(HALF)
    shared_ref[:ROWS, :] = dot(high, ones) + dot(rest, ones)
    shared_ref[ROWS:, :] = jnp.zeros((ROWS_P - ROWS, 128), FLOAT)
    store(shared_ref, shared_hbm)
    gout = dot(attn_all().T.astype(HALF), low)
    gshort = dot(pooled_all().T.astype(HALF), low)
    lines = [
        jnp.sum(back * z, axis=0, keepdims=True),
        jnp.sum(back, axis=0, keepdims=True),
        jnp.sum(cot_ref[...].astype(FLOAT), axis=0, keepdims=True),
    ]
    flat = jnp.concatenate(sums1 + lines, axis=1)
    pieces = [flat[:, k * 128 : (k + 1) * 128] for k in range((FF + 3 * D) // 128)]
    pieces.append(jnp.zeros((3, 128), FLOAT))
    lines = jnp.concatenate(pieces, axis=0)
    for half in range(2):
        rows = slice(half * (D // 2), (half + 1) * (D // 2))
        rows_in = slice(half * (D_IN // 2), (half + 1) * (D_IN // 2))
        for k in range(3):
            cols = slice(k * 128, (k + 1) * 128)
            tail_ref[half, k * (D // 2) : (k + 1) * (D // 2), :] = gout[rows, cols]
            at = AT_SHORT + k * (D_IN // 2)
            tail_ref[half, at : at + D_IN // 2, :] = gshort[rows_in, cols]
        tail_ref[half, AT_LINES:TAIL, :] = lines
    store(tail_ref, tail_hbm)
    for copy in shipped + stores:
        copy.wait()


def forward_kernel(
    core_ref,
    gathered_ref,
    picks_ref,
    bn_scale_ref,
    bn_bias_ref,
    gain1_ref,
    shift1_ref,
    wqkv_ref,
    gain2_ref,
    shift2_ref,
    b1_ref,
    b2_ref,
    cells_hbm,
    first_hbm,
    bias_hbm,
    cot_hbm,
    w_short_hbm,
    w_out_hbm,
    w1_hbm,
    w2_hbm,
    coef_ref,
    x_hbm,
    qkv_hbm,
    probs_hbm,
    plain_hbm,
    result_hbm,
    dattn_hbm,
    dshort_hbm,
    shared_hbm,
    tail_hbm,
    keep_hbm,
    send_hbm,
    s_ref,
    picked_ref,
    attn_ref,
    pooled_ref,
    bias_ref,
    cot_ref,
    w_short_ref,
    w_out_ref,
    w1_ref,
    w2_ref,
    result_ref,
    dattn_ref,
    dshort_ref,
    shared_ref,
    tail_ref,
    message_ref,
    step_ref,
    load_sems,
    ship_sems,
    store_sems,
):
    pairs = (
        (first_hbm, picked_ref),
        (bias_hbm, bias_ref),
        (w_short_hbm, w_short_ref),
        (w_out_hbm, w_out_ref),
        (w1_hbm, w1_ref),
        (cot_hbm, cot_ref),
        (w2_hbm, w2_ref),
    )
    loads = [pltpu.make_async_copy(a, b, load_sems.at[k]) for k, (a, b) in enumerate(pairs)]
    for load in loads:
        load.start()
    mean, inv = batch_coefficients(gathered_ref[...])
    coef_ref[...] = jnp.zeros_like(coef_ref)
    coef_ref[0:1, :] = mean
    coef_ref[1:2, :] = inv
    loads[0].wait()
    loads[1].wait()

    step_ref[0] = 0

    def body(next_ref, x_ref, qkv_ref, probs_ref, plain_ref):
        crop = step_ref[0]
        step_ref[0] = crop + 1
        attend(
            crop,
            x_ref,
            next_ref,
            picks_ref,
            picked_ref,
            coef_ref,
            bn_scale_ref,
            bn_bias_ref,
            gain1_ref,
            shift1_ref,
            wqkv_ref,
            bias_ref,
            qkv_ref,
            probs_ref,
            attn_ref,
            pooled_ref,
            plain_ref,
            s_ref,
        )

    by_crop = lambda *shape: pl.BlockSpec((1,) + shape, lambda c: (c,) + (0,) * len(shape))
    pltpu.emit_pipeline(
        body,
        grid=(CROPS,),
        in_specs=[
            pl.BlockSpec((1, D_IN, CELLS), lambda c: (jnp.minimum(c + 1, CROPS - 1), 0, 0))
        ],
        out_specs=[
            by_crop(4 * TP, D_IN),
            by_crop(TP, 3 * D),
            by_crop(HEADS, TP, TP),
            by_crop(TP, D_IN),
        ],
    )(cells_hbm, x_hbm, qkv_hbm, probs_hbm, plain_hbm)
    for load in loads[2:]:
        load.wait()
    feed(
        core_ref[0],
        attn_ref,
        pooled_ref,
        cot_ref,
        w_short_ref,
        w_out_ref,
        gain2_ref,
        shift2_ref,
        w1_ref,
        b1_ref,
        w2_ref,
        b2_ref,
        result_ref,
        dattn_ref,
        dshort_ref,
        shared_ref,
        tail_ref,
        message_ref,
        result_hbm,
        dattn_hbm,
        dshort_hbm,
        shared_hbm,
        tail_hbm,
        keep_hbm,
        send_hbm,
        ship_sems,
        store_sems,
    )


def forward(
    core,
    gathered,
    picks,
    cells,
    first,
    bn_scale,
    bn_bias,
    gain1,
    shift1,
    w_qkv,
    gain2,
    shift2,
    b1,
    b2,
    bias,
    cot,
    w_short,
    w_out,
    w1,
    w2,
):
    hbm = pl.BlockSpec(memory_space=pl.ANY)
    small = (gathered, picks, bn_scale, bn_bias, gain1, shift1, w_qkv, gain2, shift2, b1, b2)
    large = (cells, first, bias, cot, w_short, w_out, w1, w2)
    feed_shapes = [
        (ROWS, D),
        (3, ROWS_P, 128),
        (2, ROWS_P, 128),
        (ROWS_P, 128),
        (2, TAIL, 128),
    ]
    return pl.pallas_call(
        forward_kernel,
        in_specs=[pl.BlockSpec(memory_space=pltpu.SMEM)]
        + [whole(a.shape) for a in small]
        + [hbm] * len(large),
        out_specs=[whole((8, D_IN))] + [hbm] * 11,
        out_shape=[
            jax.ShapeDtypeStruct((8, D_IN), FLOAT),
            jax.ShapeDtypeStruct((CROPS, 4 * TP, D_IN), HALF),
            jax.ShapeDtypeStruct((CROPS, TP, 3 * D), HALF),
            jax.ShapeDtypeStruct((CROPS, HEADS, TP, TP), HALF),
            jax.ShapeDtypeStruct((CROPS, TP, D_IN), FLOAT),
        ]
        + [jax.ShapeDtypeStruct(shape, FLOAT) for shape in feed_shapes]
        + [jax.ShapeDtypeStruct((HALF_ROWS, 128), FLOAT)] * 2,
        scratch_shapes=[
            pltpu.VMEM((4, TP, TP), FLOAT),
            pltpu.VMEM((4 * TP, D_IN), HALF),
            pltpu.VMEM((3, ROWS_P, 128), FLOAT),
            pltpu.VMEM((2, ROWS_P, 128), FLOAT),
        ]
        + [pltpu.VMEM(a.shape, a.dtype) for a in (bias, cot, w_short, w_out, w1, w2)]
        + [pltpu.VMEM(shape, FLOAT) for shape in feed_shapes]
        + [
            pltpu.VMEM((2, HALF_ROWS, 128), FLOAT),
            pltpu.SMEM((1,), jnp.int32),
            pltpu.SemaphoreType.DMA((7,)),
            pltpu.SemaphoreType.DMA((6,)),
            pltpu.SemaphoreType.DMA((5,)),
        ],
        compiler_params=params(),
        name="forward",
        cost_estimate=cost(1.6e10, 5e7, 8e6),
    )(core, *small, *large)


def second_message_kernel(pieces_ref, keep_ref, other_ref, out_ref):
    total = pieces_ref[0]
    for k in range(1, PIECES):
        total = total + pieces_ref[k]
    out_ref[:, :EARLY, :] = jnp.broadcast_to(total[None], (PIECES, EARLY, 128))
    out_ref[:, EARLY:, :] = keep_ref[...] + other_ref[...]


def second_message(pieces, keep, other):
    shape = (PIECES, ROWS_2, 128)
    return pl.pallas_call(
        second_message_kernel,
        in_specs=[whole(a.shape) for a in (pieces, keep, other)],
        out_specs=whole(shape),
        out_shape=jax.ShapeDtypeStruct(shape, FLOAT),
        compiler_params=params(20 << 20),
        name="second_message",
        cost_estimate=cost(1e6, 7e6),
    )(pieces, keep, other)


def late_sum_kernel(in_hbm, copies_ref, totals_ref, late_ref, sem):
    load = pltpu.make_async_copy(in_hbm.at[:, pl.ds(EARLY, LATE)], late_ref, sem)
    load.start()
    load.wait()
    total = late_ref[0]
    for k in range(1, PIECES):
        total = total + late_ref[k]
    copies_ref[...] = jnp.broadcast_to(total[None], copies_ref.shape)
    totals_ref[...] = total[24:]


def late_sum(arrived):
    shapes = [(PIECES, LATE, 128), (8, 128)]
    return pl.pallas_call(
        late_sum_kernel,
        in_specs=[pl.BlockSpec(memory_space=pl.ANY)],
        out_specs=[whole(shape) for shape in shapes],
        out_shape=[jax.ShapeDtypeStruct(shape, FLOAT) for shape in shapes],
        scratch_shapes=[pltpu.VMEM((PIECES, LATE, 128), FLOAT), pltpu.SemaphoreType.DMA],
        compiler_params=params(),
        name="late_sum",
        cost_estimate=cost(1e5, 2e6),
    )(arrived)


def touch_kernel(*refs):
    del refs


def pass_after(after, value):
    return pl.pallas_call(
        touch_kernel,
        in_specs=[pl.BlockSpec(memory_space=pl.ANY)] * (len(after) + 1),
        out_specs=pl.BlockSpec(memory_space=pl.ANY),
        out_shape=jax.ShapeDtypeStruct(value.shape, value.dtype),
        input_output_aliases={len(after): 0},
        compiler_params=params(),
        name="pass_after",
        cost_estimate=cost(1, 1),
    )(*after, value)


def unpack_kernel(which_ref, early_ref, *refs):
    g1_ref, g2_ref = refs[-2:]

    def read(at, count):
        pieces = []
        while count:
            piece, row = divmod(at, EARLY)
            n = min(count, EARLY - row)
            pieces.append(early_ref[piece, row : row + n, :])
            at, count = at + n, count - n
        return pieces[0] if len(pieces) == 1 else jnp.concatenate(pieces, axis=0)

    for k in range(FF // 128):
        g1_ref[:, k * 128 : (k + 1) * 128] = read(k * D // 2, D // 2)
    for k in range(FF // 256):
        g2_ref[k * 128 : (k + 1) * 128, :] = read(AT_G2 + k * D, D).T


def unpack_late_kernel(which_ref, late_ref, *refs):
    gout_ref, gshort_ref, gqkv_ref = refs[-11:-8]
    db1_ref, dgain2_ref, dshift2_ref, db2_ref, table_ref, dgain1_ref, dshift1_ref = refs[-8:-1]
    flat_ref = refs[-1]
    for piece in range(PIECES):
        flat_ref[piece * DATA : (piece + 1) * DATA, :] = late_ref[piece, :DATA, :]
    for k in range(9):
        cols = slice(k * 128, (k + 1) * 128)
        at = TAIL + k * D_IN // 2
        gqkv_ref[:, cols] = flat_ref[at : at + D_IN // 2, :]
        if k < 3:
            gout_ref[:, cols] = flat_ref[k * D // 2 : (k + 1) * D // 2, :]
            at = AT_SHORT + k * D_IN // 2
            gshort_ref[:, cols] = flat_ref[at : at + D_IN // 2, :]
    lines = flat_ref[AT_LINES:TAIL, :]
    flat = jnp.concatenate([lines[k : k + 1, :] for k in range(21)], axis=1)
    db1_ref[...] = flat[:, :FF].reshape(FF)
    for k, target in enumerate((dgain2_ref, dshift2_ref, db2_ref)):
        target[...] = flat[:, FF + k * D : FF + (k + 1) * D].reshape(D)
    lines = flat_ref[AT_TABLE : AT_TABLE + 80, :]
    per = TAB // 128
    columns = []
    for k in range(per):
        rows = [lines[h * per + k : h * per + k + 1, :] for h in range(HEADS)]
        columns.append(jnp.concatenate(rows, axis=0))
    table_ref[...] = jnp.concatenate(columns, axis=1)[:, : REL * REL]
    for k, target in enumerate((dgain1_ref, dshift1_ref)):
        at = HEADS * per + 2 * k
        both = jnp.concatenate([lines[at : at + 1, :], lines[at + 1 : at + 2, :]], axis=1)
        target[...] = both[:, :D_IN].reshape(D_IN)


def fill(kernel, name, rows, small, scratch, half, message, before):
    shapes = [(2 * a, b) for a, b in rows] + small
    any_spec = pl.BlockSpec(memory_space=pl.ANY)
    return pl.pallas_call(
        kernel,
        grid_spec=pltpu.PrefetchScalarGridSpec(
            num_scalar_prefetch=1,
            grid=(1,),
            in_specs=[pl.BlockSpec(message.shape, lambda i, h: (0, 0, 0))]
            + [any_spec] * len(before),
            out_specs=[pl.BlockSpec(shape, lambda i, h: (h[0], 0)) for shape in rows]
            + [pl.BlockSpec(shape, lambda i, h, n=len(shape): (0,) * n) for shape in small],
            scratch_shapes=scratch,
        ),
        out_shape=[jax.ShapeDtypeStruct(shape, FLOAT) for shape in shapes],
        input_output_aliases={2 + k: k for k in range(len(before))},
        compiler_params=params(20 << 20),
        name=name,
        cost_estimate=cost(1e6, 6e6),
    )(half, message, *before)


def unpack(half, message, before=()):
    rows = [(D // 2, FF), (FF // 2, D)]
    return fill(unpack_kernel, "unpack", rows, [], [], half, message, before)


def unpack_late(half, message, before=()):
    rows = [(D // 2, D), (D_IN // 2, D), (D_IN // 2, 3 * D)]
    small = [(FF,), (D,), (D,), (D,), (HEADS, REL * REL), (D_IN,), (D_IN,)]
    scratch = [pltpu.VMEM((FLAT, 128), FLOAT)]
    return fill(unpack_late_kernel, "unpack_late", rows, small, scratch, half, message, before)


def back_crop(
    crop,
    coef_ref,
    x_ref,
    plain_ref,
    qkv_ref,
    probs_ref,
    dattn_ref,
    dshort_ref,
    shared_ref,
    bn_scale_ref,
    bn_bias_ref,
    gain_ref,
    shift_ref,
    w_ref,
    dbias_ref,
    gw_ref,
    sums_ref,
    dcells_ref,
    dp_ref,
    ds_ref,
):
    dattn = take_rows(dattn_ref, crop).astype(HALF)
    shared = shared_ref[pl.ds(crop, TP, stride=CROPS), :].T
    key_t = qkv_ref[0, :, D : 2 * D].astype(FLOAT).T.astype(HALF)
    masks = head_masks()
    dquery_t, dkeys, dvalues = [], [], []

    def start(head):
        group = head // 4
        grad = dattn[:, group * 128 : (group + 1) * 128] * masks[head % 4]
        value = qkv_ref[0, :, 2 * D + group * 128 : 2 * D + (group + 1) * 128]
        dp_ref[head % 3] = dot(value, grad, NT)
        dvalues.append(dot(probs_ref[0, head], grad))

    def finish(head):
        group = head // 4
        query = qkv_ref[0, :, group * 128 : (group + 1) * 128] * masks[head % 4]
        dscores = ds_ref[head % 3]
        dkeys.append(dot(dscores, query))
        dquery_t.append(dot(key_t[head * HEAD : (head + 1) * HEAD, :], dscores))

    for head in range(2):
        start(head)
    for head in range(HEADS):
        if head + 2 < HEADS:
            start(head + 2)
        for cols in (slice(0, 128), slice(128, TP)):
            probs = probs_ref[0, head, :, cols].astype(FLOAT)
            dscores = probs * (dp_ref[head % 3, :, cols] - shared[head : head + 1, cols])
            dbias_ref[head, :, cols] += dscores
            ds_ref[head % 3, :, cols] = dscores.astype(HALF)
        if head >= 2:
            finish(head - 2)
    for head in range(HEADS - 2, HEADS):
        finish(head)
    group_sum = lambda items, g: sum(items[4 * g + 1 : 4 * g + 4], items[4 * g])
    dquery = jnp.concatenate(dquery_t, axis=0).T * SCALE
    dqkv = jnp.concatenate(
        [dquery]
        + [group_sum(dkeys, g) * SCALE for g in range(3)]
        + [group_sum(dvalues, g) for g in range(3)],
        axis=1,
    ).astype(HALF)
    pooled = plain_ref[0]
    z, inverse = norm_rows(pooled)
    gain = line(gain_ref)
    first_t = (z * gain + line(shift_ref)).T.astype(HALF)
    gw_ref[...] += dot(first_t, dqkv)
    dfirst = dot(dqkv, w_ref[...], NT)
    dz = dfirst * gain
    dpooled = take_rows(dshort_ref, crop)[:, :D_IN] + inverse * (
        dz
        - jnp.mean(dz, axis=-1, keepdims=True)
        - z * jnp.mean(dz * z, axis=-1, keepdims=True)
    )
    sums_ref[0:1, :] += jnp.sum(dfirst * z, axis=0, keepdims=True)
    sums_ref[1:2, :] += jnp.sum(dfirst, axis=0, keepdims=True)
    level = pooled * LOG2E
    parts = bn_parts(x_ref, coef_ref, bn_scale_ref, bn_bias_ref)
    along = jnp.zeros((TP, D_IN), FLOAT)
    total = jnp.zeros((TP, D_IN), FLOAT)
    for part in range(4):
        dpart = dpooled * jnp.exp2(parts[part] - level)
        dcells_ref[0, part * TP : (part + 1) * TP, :] = dpart.astype(HALF)
        raw = x_ref[0, part * TP : (part + 1) * TP, :].astype(FLOAT)
        along = along + dpart * (raw - coef_ref[0:1, :])
        total = total + dpart
    sums_ref[2:3, :] += jnp.sum(along, axis=0, keepdims=True) * coef_ref[1:2, :]
    sums_ref[3:4, :] += jnp.sum(total, axis=0, keepdims=True)


def back_kernel(
    core_ref,
    after_ref,
    coef_ref,
    bn_scale_ref,
    bn_bias_ref,
    gain_ref,
    shift_ref,
    w_ref,
    spread_ref,
    x_hbm,
    plain_hbm,
    qkv_hbm,
    probs_hbm,
    dattn_hbm,
    dshort_hbm,
    shared_hbm,
    tail_hbm,
    keep_ref,
    send_ref,
    dcells_hbm,
    dattn_ref,
    dshort_ref,
    shared_ref,
    tail_ref,
    dbias_ref,
    gw_ref,
    sums_ref,
    dp_ref,
    ds_ref,
    rows_ref,
    flat_ref,
    step_ref,
    load_sems,
):
    pairs = (
        (dattn_hbm, dattn_ref),
        (dshort_hbm, dshort_ref),
        (shared_hbm, shared_ref),
        (tail_hbm, tail_ref),
    )
    loads = [pltpu.make_async_copy(a, b, load_sems.at[k]) for k, (a, b) in enumerate(pairs)]
    for load in loads:
        load.start()
    dbias_ref[...] = jnp.zeros_like(dbias_ref)
    gw_ref[...] = jnp.zeros_like(gw_ref)
    sums_ref[...] = jnp.zeros_like(sums_ref)
    step_ref[0] = 0
    for load in loads:
        load.wait()

    def body(x_ref, plain_ref, qkv_ref, probs_ref, dcells_ref):
        crop = step_ref[0]
        step_ref[0] = crop + 1
        back_crop(
            crop,
            coef_ref,
            x_ref,
            plain_ref,
            qkv_ref,
            probs_ref,
            dattn_ref,
            dshort_ref,
            shared_ref,
            bn_scale_ref,
            bn_bias_ref,
            gain_ref,
            shift_ref,
            w_ref,
            dbias_ref,
            gw_ref,
            sums_ref,
            dcells_ref,
            dp_ref,
            ds_ref,
        )

    by_crop = lambda *shape: pl.BlockSpec((1,) + shape, lambda c: (c,) + (0,) * len(shape))
    pltpu.emit_pipeline(
        body,
        grid=(CROPS,),
        in_specs=[
            by_crop(4 * TP, D_IN),
            by_crop(TP, D_IN),
            by_crop(TP, 3 * D),
            by_crop(HEADS, TP, TP),
        ],
        out_specs=[by_crop(4 * TP, D_IN)],
    )(x_hbm, plain_hbm, qkv_hbm, probs_hbm, dcells_hbm)

    lines = reduce_bias(dbias_ref, spread_ref, rows_ref)
    pad = jnp.zeros((1, 256 - D_IN), FLOAT)
    for k in range(2):
        value = jnp.concatenate([sums_ref[k : k + 1, :], pad], axis=1)
        lines += [value[:, :128], value[:, 128:]]
    lines.append(jnp.zeros((FLAT - AT_TABLE - len(lines), 128), FLOAT))
    flat_ref[AT_TABLE:, :] = jnp.concatenate(lines, axis=0)
    totals = jnp.concatenate([sums_ref[2:3, :], sums_ref[3:4, :]], axis=1)
    totals = jnp.concatenate([totals[:, k * 128 : (k + 1) * 128] for k in range(3)], axis=0)

    def write(ref, half):
        flat_ref[:TAIL, :] = tail_ref[half]
        for k in range(9):
            at = TAIL + k * D_IN // 2
            flat_ref[at : at + D_IN // 2, :] = gw_ref[
                half * (D_IN // 2) : (half + 1) * (D_IN // 2), k * 128 : (k + 1) * 128
            ]
        for piece in range(PIECES):
            ref[piece, :DATA, :] = flat_ref[piece * DATA : (piece + 1) * DATA, :]
            ref[piece, DATA:, :] = totals

    @pl.when(core_ref[0] == 0)
    def _():
        write(keep_ref, 0)
        write(send_ref, 1)

    @pl.when(core_ref[0] != 0)
    def _():
        write(keep_ref, 1)
        write(send_ref, 0)


def attention_back(
    core,
    after,
    coef,
    bn_scale,
    bn_bias,
    gain,
    shift,
    w_qkv,
    spread,
    picked,
    plain,
    qkv,
    probs,
    dattn,
    dshort,
    shared,
    tail,
):
    hbm = pl.BlockSpec(memory_space=pl.ANY)
    small = (coef, bn_scale, bn_bias, gain, shift, w_qkv, spread)
    large = (picked, plain, qkv, probs, dattn, dshort, shared, tail)
    message = (PIECES, LATE, 128)
    return pl.pallas_call(
        back_kernel,
        in_specs=[pl.BlockSpec(memory_space=pltpu.SMEM), hbm]
        + [whole(a.shape) for a in small]
        + [hbm] * len(large),
        out_specs=[whole(message), whole(message), hbm],
        out_shape=[
            jax.ShapeDtypeStruct(message, FLOAT),
            jax.ShapeDtypeStruct(message, FLOAT),
            jax.ShapeDtypeStruct((CROPS, 4 * TP, D_IN), HALF),
        ],
        scratch_shapes=[pltpu.VMEM(a.shape, FLOAT) for a in (dattn, dshort, shared, tail)]
        + [
            pltpu.VMEM((HEADS, TP, TP), FLOAT),
            pltpu.VMEM((D_IN, 3 * D), FLOAT),
            pltpu.VMEM((8, D_IN), FLOAT),
            pltpu.VMEM((3, TP, TP), FLOAT),
            pltpu.VMEM((3, TP, TP), HALF),
            pltpu.VMEM((HEADS, TP, TAB), FLOAT),
            pltpu.VMEM((FLAT, 128), FLOAT),
            pltpu.SMEM((1,), jnp.int32),
            pltpu.SemaphoreType.DMA((4,)),
        ],
        compiler_params=params(),
        name="attention_back",
        cost_estimate=cost(8e9, 4e7, 2e6),
    )(core, after, *small, *large)


def scatter_kernel(s_ref, d_ref, out_ref):
    for k in range(d_ref.shape[0]):
        for low, high, first, last in CELL_CHUNKS:
            value = None
            for part in range(4):
                rows = slice(part * TP + first, part * TP + last)
                term = dot(d_ref[k, rows, :], s_ref[rows, low:high], TN)
                value = term if value is None else value + term
            out_ref[k, :, low:high] = value.astype(HALF)


def scatter_cells(places, dcells):
    each = 2
    return pl.pallas_call(
        scatter_kernel,
        grid=(CROPS // each,),
        in_specs=[
            whole((4 * TP, CELLS)),
            pl.BlockSpec((each, 4 * TP, D_IN), lambda c: (c, 0, 0)),
        ],
        out_specs=pl.BlockSpec((each, D_IN, CELLS), lambda c: (c, 0, 0)),
        out_shape=jax.ShapeDtypeStruct((CROPS, D_IN, CELLS), HALF),
        compiler_params=params(16 << 20),
        name="scatter_cells",
        cost_estimate=cost(3e9, 8e6),
    )(places, dcells)


def column(row):
    return jnp.broadcast_to(row, (128, D_IN)).T[:, 0:1]


def cells_kernel(count, totals_ref, coef_ref, scale_ref, d_ref, x_ref, out_ref, dscale_ref, dshift_ref, cols_ref):
    @pl.when(pl.program_id(0) == 0)
    def _():
        rows = [totals_ref[k : k + 1, :] for k in range(8 - (LATE - DATA), 8)]
        totals = jnp.concatenate(rows, axis=1)
        along = totals[:, :D_IN]
        plain = totals[:, D_IN:]
        dscale_ref[...] = along.reshape(D_IN)
        dshift_ref[...] = plain.reshape(D_IN)
        mean = coef_ref[0:1, :]
        inv = coef_ref[1:2, :]
        factor = inv * line(scale_ref)
        share = 1.0 / float(count * CROPS * CELLS)
        slope = factor * along * inv * share
        cols_ref[:, 0:1] = column(factor)
        cols_ref[:, 1:2] = column(factor * plain * share)
        cols_ref[:, 2:3] = column(slope)
        cols_ref[:, 3:4] = column(mean)

    out_ref[0] = (
        d_ref[0].astype(FLOAT) * cols_ref[:, 0:1]
        - cols_ref[:, 1:2]
        - (x_ref[0].astype(FLOAT) - cols_ref[:, 3:4]) * cols_ref[:, 2:3]
    )


def cell_gradient(count, totals, coef, bn_scale, dcells, cells):
    crop_block = pl.BlockSpec((1, D_IN, CELLS), lambda c: (c, 0, 0))
    return pl.pallas_call(
        functools.partial(cells_kernel, count),
        grid=(CROPS,),
        in_specs=[
            whole((8, 128)),
            whole((8, D_IN)),
            whole((D_IN,)),
            crop_block,
            crop_block,
        ],
        out_specs=[crop_block, whole((D_IN,)), whole((D_IN,))],
        out_shape=[
            jax.ShapeDtypeStruct((CROPS, D_IN, CELLS), FLOAT),
            jax.ShapeDtypeStruct((D_IN,), FLOAT),
            jax.ShapeDtypeStruct((D_IN,), FLOAT),
        ],
        scratch_shapes=[pltpu.VMEM((D_IN, 128), FLOAT)],
        compiler_params=params(16 << 20),
        name="cell_gradient",
        cost_estimate=cost(1e7, 1.5e7),
    )(totals, coef, bn_scale, dcells, cells)


CHIPS = ("y", "x", "z")
ALL = ("y", "x", "z", "core")


def gather_rows(copies):
    if copies.shape[0] == 1:
        return copies
    return lax.all_to_all(copies, ALL, 0, 0)


def on_device(
    count,
    features,
    bn_scale,
    bn_bias,
    w_short,
    ln1_gain,
    ln1_bias,
    w_qkv,
    rel_table,
    w_out,
    ln2_gain,
    ln2_bias,
    w_fc1,
    fc1_bias,
    w_fc2,
    fc2_bias,
    cotangent,
):
    picks = jnp.asarray(select_matrix(), HALF)
    places = jnp.asarray(scatter_matrix(), HALF)
    spread = jnp.asarray(spread_matrix(), HALF)
    spread_back = jnp.asarray(spread_matrix().T, HALF)
    core = lax.axis_index("core").astype(jnp.int32).reshape(1)
    cells = features.transpose(0, 2, 1)
    cot = cotangent.transpose(1, 0, 2).reshape(ROWS, D)
    stats = gather_rows(local_stats(cells, count))
    bias, first = expand_bias(rel_table, spread, picks, cells)
    coef, picked, qkv, probs, plain, out, dattn, dshort, shared, tail, keep, send = forward(
        core,
        stats,
        picks,
        cells,
        first,
        bn_scale,
        bn_bias,
        ln1_gain,
        ln1_bias,
        w_qkv,
        ln2_gain,
        ln2_bias,
        fc1_bias,
        fc2_bias,
        bias,
        cot,
        w_short,
        w_out,
        w_fc1,
        w_fc2,
    )
    swap = [(0, 1), (1, 0)]
    keep = keep.reshape(PIECES, EARLY, 128)
    send = send.reshape(PIECES, EARLY, 128)
    mine = keep
    if count > 1:
        mine = keep + lax.ppermute(send, "core", swap)
        pieces = lax.all_to_all(mine, CHIPS, 0, 0)
    late_keep, late_send, dcells = attention_back(
        core,
        mine,
        coef,
        bn_scale,
        bn_bias,
        ln1_gain,
        ln1_bias,
        w_qkv,
        spread_back,
        picked,
        plain,
        qkv,
        probs,
        dattn,
        dshort,
        shared,
        tail,
    )
    scattered = scatter_cells(places, dcells)
    if count > 1:
        late = lax.ppermute(late_send, "core", swap)
        own = lax.all_to_all(second_message(pieces, late_keep, late), CHIPS, 0, 0)
        own = pass_after((scattered,), own)
        copies, totals = late_sum(own)
        own_late = lax.all_to_all(copies, CHIPS, 0, 0)
        other = lax.ppermute(own, "core", swap)
    else:
        totals = late_keep[0, 24:]
        own, other = keep, send
        own_late, other_late = late_keep, late_send
    grad_cells, dscale, dshift = cell_gradient(count, totals, coef, bn_scale, scattered, cells)
    g1, g2 = unpack(1 - core, other, unpack(core, own))
    if count > 1:
        own_late = pass_after((g1, grad_cells), own_late)
        other_late = lax.ppermute(own_late, "core", swap)
    grads = unpack_late(core, own_late)
    gout, gshort, gqkv = unpack_late(1 - core, other_late, grads[:3])[:3]
    db1, dgain2, dshift2, db2, table, dgain1, dshift1 = grads[3:]
    return (
        out.reshape(TOK, CROPS, D).transpose(1, 0, 2),
        grad_cells.transpose(0, 2, 1),
        dscale,
        dshift,
        gshort,
        dgain1,
        dshift1,
        gqkv,
        table,
        gout,
        dgain2,
        dshift2,
        g1,
        db1,
        g2,
        db2,
    )


def solution(mesh):
    count = mesh.size
    shape = (4, 4, 4, 2) if count == 128 else (1, 1, 1, 1)
    grid = jax.sharding.Mesh(mesh.devices.reshape(shape), ALL)
    split = P(ALL, None, None)
    same = P()
    in_specs = (split,) + (same,) * 14 + (split,)
    out_specs = (split, split) + (same,) * 14

    def run(*args):
        return on_device(count, *args)

    return jax.shard_map(run, mesh=grid, in_specs=in_specs, out_specs=out_specs, check_vma=False)
```

```python
import functools

import jax
import jax.numpy as jnp
import numpy as np
from jax import lax
from jax.experimental import pallas as pl
from jax.experimental.pallas import tpu as pltpu
from jax.sharding import PartitionSpec as P

HEADS = 12
HEAD = 32
SIDE = 14
TOK = 196
TP = 208
GRID2 = 2 * SIDE
CELLS = 784
D_IN = 192
D = 384
FF = 1536
CROPS = 8
ROWS = TOK * CROPS
ROWS_P = TP * CROPS
REL = 27
TAB = 768
SPREAD = 384

EPS = 1e-05
FLOAT = jnp.float32
HALF = jnp.bfloat16
LOG2E = 1.4426950408889634
LN2 = 0.6931471805599453
SCALE = HEAD ** (-0.5)
NN = (((1,), (0,)), ((), ()))
NT = (((1,), (1,)), ((), ()))
TN = (((0,), (0,)), ((), ()))
VMEM_LIMIT = 56 * 1024 * 1024


def dot(left, right, dims=NN):
    return lax.dot_general(left, right, dims, preferred_element_type=FLOAT)


def split2(value):
    hi = value.astype(HALF)
    return hi, (value - hi.astype(FLOAT)).astype(HALF)


def params(limit=VMEM_LIMIT):
    return pltpu.CompilerParams(vmem_limit_bytes=limit)


def cost(flops, bytes_accessed, transcendentals=0):
    return pl.CostEstimate(
        flops=int(flops), bytes_accessed=int(bytes_accessed), transcendentals=int(transcendentals)
    )


def whole(shape):
    return pl.BlockSpec(shape, lambda *_: (0,) * len(shape))


CHUNKS = (
    (0, 48, 0, 256),
    (48, 80, 0, 512),
    (80, 112, 256, 512),
    (112, 144, 256, 768),
    (144, 176, 512, 768),
    (176, TP, 512, CELLS),
)
CELL_CHUNKS = ((0, 256, 0, 80), (256, 512, 48, 144), (512, CELLS, 112, TP))


def cell_of(part, token):
    i, j = divmod(token, SIDE)
    a, b = divmod(part, 2)
    return (2 * i + a) * GRID2 + 2 * j + b


def select_matrix():
    rows = []
    for first, last, low, high in CHUNKS:
        for part in range(4):
            block = np.zeros((last - first, CELLS), np.float32)
            for t in range(first, min(last, TOK)):
                assert low <= cell_of(part, t) < high
                block[t - first, cell_of(part, t)] = 1.0
            rows.append(block)
    return np.concatenate(rows)


def scatter_matrix():
    table = np.zeros((4 * TP, CELLS), np.float32)
    for low, high, first, last in CELL_CHUNKS:
        for part in range(4):
            for t in range(TOK):
                if low <= cell_of(part, t) < high:
                    assert first <= t < last
                    table[part * TP + t, cell_of(part, t)] = 1.0
    return table


def spread_matrix():
    table = np.zeros((SPREAD, TP), np.float32)
    for t in range(TOK):
        i, j = divmod(t, SIDE)
        table[REL * i + j, t] = 1.0
    return table


def stats_kernel(x_hbm, out_ref, x_ref, sems):
    pieces = []
    step = 32
    loads = []
    for block in range(D_IN // step):
        rows = pl.ds(block * step, step)
        loads.append(
            pltpu.make_async_copy(x_hbm.at[:, rows], x_ref.at[:, rows], sems.at[block])
        )
        loads[-1].start()
    for block in range(D_IN // step):
        loads[block].wait()
        rows = slice(block * step, (block + 1) * step)
        total = x_ref[0, rows, :].astype(FLOAT)
        for crop in range(1, CROPS):
            total = total + x_ref[crop, rows, :].astype(FLOAT)
        total = jnp.sum(total, axis=1, keepdims=True)
        mean = total * (1.0 / (CROPS * CELLS))
        square = jnp.zeros((step, CELLS), FLOAT)
        for crop in range(CROPS):
            centre = x_ref[crop, rows, :].astype(FLOAT) - mean
            square = square + centre * centre
        square = jnp.sum(square, axis=1, keepdims=True)
        lane = lax.broadcasted_iota(jnp.int32, (step, 128), 1)
        pieces.append(jnp.where(lane == 0, mean, jnp.where(lane == 1, square, 0.0)))
    turned = jnp.concatenate(pieces, axis=0).T
    pad = jnp.zeros((1, 64), FLOAT)
    row = jnp.concatenate([turned[0:1], pad, turned[1:2], pad], axis=1)
    out_ref[...] = jnp.broadcast_to(row[None], out_ref.shape)


def local_stats(cells, copies):
    return pl.pallas_call(
        stats_kernel,
        in_specs=[pl.BlockSpec(memory_space=pl.ANY)],
        out_specs=whole((copies, 1, 512)),
        out_shape=jax.ShapeDtypeStruct((copies, 1, 512), FLOAT),
        scratch_shapes=[
            pltpu.VMEM((CROPS, D_IN, CELLS), HALF),
            pltpu.SemaphoreType.DMA((D_IN // 32,)),
        ],
        compiler_params=params(),
        name="stats",
        cost_estimate=cost(8e6, 2.8e6),
    )(cells)


def batch_coefficients(gathered):
    count = gathered.shape[0]
    means = gathered[:, 0, 0:D_IN]
    squares = gathered[:, 0, 256 : 256 + D_IN]
    mean = jnp.sum(means, axis=0, keepdims=True) * (1.0 / count)
    off = means - mean
    local = float(CROPS * CELLS)
    var = jnp.sum(squares, axis=0, keepdims=True) + local * jnp.sum(
        off * off, axis=0, keepdims=True
    )
    return mean, lax.rsqrt(var * (1.0 / (local * count)) + EPS)


def select_cells(s_ref, x_ref, out_ref):
    at = 0
    for first, last, low, high in CHUNKS:
        size = last - first
        picked = dot(s_ref[at : at + 4 * size, low:high], x_ref[0, :, low:high], NT).astype(HALF)
        for part in range(4):
            start = part * TP + first
            out_ref[start : start + size, :] = picked[part * size : (part + 1) * size]
        at += 4 * size


def bias_kernel(table_ref, spread_ref, picks_ref, cells_ref, out_ref, picked_ref, rows_ref):
    select_cells(picks_ref, cells_ref, picked_ref)
    row = lax.broadcasted_iota(jnp.int32, (TP, TP), 0)
    for head in range(HEADS):
        pad = jnp.zeros((1, TAB - REL * REL), FLOAT)
        table = jnp.concatenate([table_ref[head : head + 1, :] * LOG2E, pad], axis=1)
        base = pltpu.roll(jnp.broadcast_to(table, (16, TAB)), 0, 1, stride=1, stride_axis=0)
        for r in range(SIDE):
            rolled = pltpu.roll(base, (TAB - 364 + REL * r) % TAB, 1)
            rows_ref[head, SIDE * r : SIDE * (r + 1), :] = rolled[:SIDE, :SPREAD]
        rows_ref[head, TOK:, :] = jnp.zeros((TP - TOK, SPREAD), FLOAT)
        hi, lo = split2(rows_ref[head])
        value = dot(hi, spread_ref[...]) + dot(lo, spread_ref[...])
        out_ref[head] = jnp.where(row < TOK, value, -1e30)


def expand_bias(rel_table, spread, picks, cells):
    first = pl.BlockSpec((1, D_IN, CELLS), lambda i: (0, 0, 0))
    return pl.pallas_call(
        bias_kernel,
        grid=(1,),
        in_specs=[whole(rel_table.shape), whole(spread.shape), whole(picks.shape), first],
        out_specs=[whole((HEADS, TP, TP)), whole((4 * TP, D_IN))],
        out_shape=[
            jax.ShapeDtypeStruct((HEADS, TP, TP), FLOAT),
            jax.ShapeDtypeStruct((4 * TP, D_IN), HALF),
        ],
        scratch_shapes=[pltpu.VMEM((HEADS, TP, SPREAD), FLOAT)],
        compiler_params=params(24 << 20),
        name="expand_bias",
        cost_estimate=cost(2e9, 3e6),
    )(rel_table, spread, picks, cells)


def reduce_bias(dbias_ref, spread_ref, rows_ref):
    row = lax.broadcasted_iota(jnp.int32, (16, TAB), 0)
    lines = []
    for head in range(HEADS):
        hi, lo = split2(dbias_ref[head])
        rows_ref[head, :, :SPREAD] = dot(hi, spread_ref[...]) + dot(lo, spread_ref[...])
        rows_ref[head, :, SPREAD:] = jnp.zeros((TP, TAB - SPREAD), FLOAT)
        total = rows_ref[head, 0:16, :]
        for r in range(1, SIDE):
            piece = rows_ref[head, SIDE * r : SIDE * r + 16, :]
            total = total + pltpu.roll(piece, TAB - REL * r, 1)
        total = jnp.where(row < SIDE, total, 0.0)
        total = jnp.concatenate([total[c : c + 1, :] for c in range(15, -1, -1)], axis=0)
        total = pltpu.roll(total, 0, 1, stride=1, stride_axis=0)
        total = jnp.sum(total, axis=0, keepdims=True)
        total = pltpu.roll(total, 364 - 15, 1)
        lines += [total[:, k * 128 : (k + 1) * 128] for k in range(TAB // 128)]
    return lines


def line(ref):
    return ref[...].reshape(1, ref.shape[0])


def bn_parts(x_ref, coef_ref, scale_ref, bias_ref):
    mean = coef_ref[0:1, :]
    factor = coef_ref[1:2, :] * line(scale_ref) * LOG2E
    shift = line(bias_ref) * LOG2E
    return [
        (x_ref[0, part * TP : (part + 1) * TP, :].astype(FLOAT) - mean) * factor + shift
        for part in range(4)
    ]


def norm_rows(value):
    centre = value - jnp.mean(value, axis=-1, keepdims=True)
    inverse = lax.rsqrt(jnp.mean(centre * centre, axis=-1, keepdims=True) + EPS)
    return centre * inverse, inverse


def put_rows(ref, crop, value):
    for group in range(ref.shape[0]):
        piece = value[:, group * 128 : (group + 1) * 128]
        if piece.shape[1] < 128:
            rest = jnp.zeros((piece.shape[0], 128 - piece.shape[1]), piece.dtype)
            piece = jnp.concatenate([piece, rest], axis=1)
        ref[group, pl.ds(crop, TP, stride=CROPS), :] = piece


def take_rows(ref, crop):
    pieces = [ref[group, pl.ds(crop, TP, stride=CROPS), :] for group in range(ref.shape[0])]
    return jnp.concatenate(pieces, axis=1)


def head_masks():
    lane = lax.broadcasted_iota(jnp.int32, (1, 128), 1)
    return [(lane // HEAD == k).astype(HALF) for k in range(4)]


def attend(
    crop,
    x_ref,
    next_ref,
    picks_ref,
    picked_ref,
    coef_ref,
    bn_scale_ref,
    bn_bias_ref,
    gain_ref,
    shift_ref,
    w_ref,
    bias_ref,
    qkv_ref,
    probs_ref,
    attn_ref,
    pooled_ref,
    plain_ref,
    s_ref,
):
    x_ref[0] = picked_ref[...]
    parts = bn_parts(x_ref, coef_ref, bn_scale_ref, bn_bias_ref)
    top = jnp.maximum(jnp.maximum(parts[0], parts[1]), jnp.maximum(parts[2], parts[3]))
    total = jnp.exp2(parts[0] - top)
    for part in range(1, 4):
        total = total + jnp.exp2(parts[part] - top)
    pooled = top * LN2 + jnp.log(total)
    put_rows(pooled_ref, crop, pooled)
    plain_ref[0] = pooled
    z, _ = norm_rows(pooled)
    first = (z * line(gain_ref) + line(shift_ref)).astype(HALF)
    qkv_ref[0] = dot(first, w_ref[...]).astype(HALF)
    value_t = qkv_ref[0, :, 2 * D :].astype(FLOAT).T.astype(HALF)
    masks = head_masks()

    def start(head):
        group = head // 4
        query = qkv_ref[0, :, group * 128 : (group + 1) * 128] * masks[head % 4]
        key = qkv_ref[0, :, D + group * 128 : D + (group + 1) * 128]
        s_ref[head % 4] = dot(key, query, NT)

    def finish(head):
        rows = slice(head * HEAD, (head + 1) * HEAD)
        return dot(value_t[rows, :], probs_ref[0, head])

    heads = []
    for head in range(3):
        start(head)
    for head in range(HEADS):
        if head + 3 < HEADS:
            start(head + 3)
        if head == 2:
            select_cells(picks_ref, next_ref, picked_ref)
        for cols in (slice(0, 128), slice(128, TP)):
            scores = s_ref[head % 4, :, cols] * (SCALE * LOG2E) + bias_ref[head, :, cols]
            weight = jnp.exp2(scores - jnp.max(scores, axis=0, keepdims=True))
            weight = weight * (1.0 / jnp.sum(weight, axis=0, keepdims=True))
            probs_ref[0, head, :, cols] = weight.astype(HALF)
        if head >= 3:
            heads.append(finish(head - 3))
    for head in range(HEADS - 3, HEADS):
        heads.append(finish(head))
    put_rows(attn_ref, crop, jnp.concatenate(heads, axis=0).T)


def normal_parts(u):
    cdf = lax.erf(u * np.float32(np.sqrt(0.5))) * 0.5 + 0.5
    return cdf, jnp.exp2(u * u * (-0.5 * LOG2E)) * (u * np.float32(1.0 / np.sqrt(2 * np.pi)))


PIECES = 64
EARLY = 72
LATE = 32
DATA = 29
AT_G2 = FF // 128 * (D // 2)
HALF_ROWS = PIECES * EARLY
ROWS_2 = EARLY + LATE
AT_SHORT = 3 * D // 2
AT_LINES = AT_SHORT + 3 * D_IN // 2
TAIL = AT_LINES + 24
AT_TABLE = TAIL + 9 * D_IN // 2
FLAT = PIECES * DATA
assert AT_G2 + FF // 2 // 128 * D == HALF_ROWS and AT_TABLE + 80 <= FLAT

FC_COLS = 768


def feed(
    core,
    attn_ref,
    pooled_ref,
    cot_ref,
    w_short_ref,
    w_out_ref,
    gain_ref,
    shift_ref,
    w1_ref,
    b1_ref,
    w2_ref,
    b2_ref,
    result_ref,
    dattn_ref,
    dshort_ref,
    shared_ref,
    tail_ref,
    message_ref,
    result_hbm,
    dattn_hbm,
    dshort_hbm,
    shared_hbm,
    tail_hbm,
    keep_ref,
    send_ref,
    sems,
    store_sems,
):
    stores = []

    def store(source, target):
        stores.append(pltpu.make_async_copy(source, target, store_sems.at[len(stores)]))
        stores[-1].start()

    def put(half, at, value):
        count = value.shape[0]
        for k in range(value.shape[1] // 128):
            message_ref[half, at + k * count : at + (k + 1) * count, :] = value[
                :, k * 128 : (k + 1) * 128
            ]

    shipped = []

    def ship(half, at, end):
        sem = sems.at[len(shipped)]
        rows = pl.ds(at, end - at)
        to_keep = pltpu.make_async_copy(message_ref.at[half, rows], keep_ref.at[rows], sem)
        to_send = pltpu.make_async_copy(message_ref.at[half, rows], send_ref.at[rows], sem)

        @pl.when(core == half)
        def _():
            to_keep.start()

        @pl.when(core != half)
        def _():
            to_send.start()

        shipped.append(to_keep)

    def attn_all():
        return jnp.concatenate([attn_ref[k, :ROWS] for k in range(3)], axis=1)

    def pooled_all():
        return jnp.concatenate([pooled_ref[k, :ROWS] for k in range(2)], axis=1)[:, :D_IN]

    y1 = dot(pooled_all().astype(HALF), w_short_ref[...]) + dot(
        attn_all().astype(HALF), w_out_ref[...]
    )
    z, inverse = norm_rows(y1)
    gain = line(gain_ref)
    second = (z * gain + line(shift_ref)).astype(HALF)
    result_ref[...] = y1 + line(b2_ref)
    b1 = line(b1_ref)
    back = jnp.zeros((ROWS, D), FLOAT)
    second_t = second.astype(FLOAT).T.astype(HALF)
    cot = cot_ref[...]
    cot_t = cot.astype(FLOAT).T.astype(HALF)
    sums1 = []
    for block in range(FF // FC_COLS):
        cols = slice(block * FC_COLS, (block + 1) * FC_COLS)
        u = dot(second, w1_ref[:, cols]) + b1[:, cols]
        cdf, slope = normal_parts(u)
        hidden = (u * cdf).astype(HALF)
        dhidden = dot(cot, w2_ref[cols, :], NT)
        du = dhidden * (cdf + slope)
        sums1.append(jnp.sum(du, axis=0, keepdims=True))
        du = du.astype(HALF)
        result_ref[...] += dot(hidden, w2_ref[cols, :])
        back = back + dot(du, w1_ref[:, cols], NT)
        g1 = dot(second_t, du)
        at = block * (FC_COLS // 128) * (D // 2)
        for half in range(2):
            put(half, at, g1[half * (D // 2) : (half + 1) * (D // 2)])
            ship(half, at, at + FC_COLS // 128 * (D // 2))
        put(block, AT_G2, dot(cot_t, hidden))
        ship(block, AT_G2, HALF_ROWS)
    store(result_ref, result_hbm)
    dz = back * gain
    dy1 = cot_ref[...].astype(FLOAT) + inverse * (
        dz
        - jnp.mean(dz, axis=-1, keepdims=True)
        - z * jnp.mean(dz * z, axis=-1, keepdims=True)
    )
    low = dy1.astype(HALF)
    dattn = dot(low, w_out_ref[...], NT).astype(HALF).astype(FLOAT)
    for k in range(3):
        dattn_ref[k, :ROWS, :] = dattn[:, k * 128 : (k + 1) * 128]
    dattn_ref[:, ROWS:, :] = jnp.zeros((3, ROWS_P - ROWS, 128), FLOAT)
    store(dattn_ref, dattn_hbm)
    dshort = dot(low, w_short_ref[...], NT)
    dshort_ref[0, :ROWS, :] = dshort[:, :128]
    dshort_ref[1, :ROWS, :] = jnp.concatenate(
        [dshort[:, 128:], jnp.zeros((ROWS, 256 - D_IN), FLOAT)], axis=1
    )
    dshort_ref[:, ROWS:, :] = jnp.zeros((2, ROWS_P - ROWS, 128), FLOAT)
    store(dshort_ref, dshort_hbm)
    lane = lax.broadcasted_iota(jnp.int32, (D, 128), 0) // HEAD
    column = lax.broadcasted_iota(jnp.int32, (D, 128), 1)
    ones = (lane == column).astype(HALF)
    product = attn_all() * dattn
    high = product.astype(HALF)
    rest = (product - high.astype(FLOAT)).astype(HALF)
    shared_ref[:ROWS, :] = dot(high, ones) + dot(rest, ones)
    shared_ref[ROWS:, :] = jnp.zeros((ROWS_P - ROWS, 128), FLOAT)
    store(shared_ref, shared_hbm)
    gout = dot(attn_all().T.astype(HALF), low)
    gshort = dot(pooled_all().T.astype(HALF), low)
    lines = [
        jnp.sum(back * z, axis=0, keepdims=True),
        jnp.sum(back, axis=0, keepdims=True),
        jnp.sum(cot_ref[...].astype(FLOAT), axis=0, keepdims=True),
    ]
    flat = jnp.concatenate(sums1 + lines, axis=1)
    pieces = [flat[:, k * 128 : (k + 1) * 128] for k in range((FF + 3 * D) // 128)]
    pieces.append(jnp.zeros((3, 128), FLOAT))
    lines = jnp.concatenate(pieces, axis=0)
    for half in range(2):
        rows = slice(half * (D // 2), (half + 1) * (D // 2))
        rows_in = slice(half * (D_IN // 2), (half + 1) * (D_IN // 2))
        for k in range(3):
            cols = slice(k * 128, (k + 1) * 128)
            tail_ref[half, k * (D // 2) : (k + 1) * (D // 2), :] = gout[rows, cols]
            at = AT_SHORT + k * (D_IN // 2)
            tail_ref[half, at : at + D_IN // 2, :] = gshort[rows_in, cols]
        tail_ref[half, AT_LINES:TAIL, :] = lines
    store(tail_ref, tail_hbm)
    for copy in shipped + stores:
        copy.wait()


def forward_kernel(
    core_ref,
    gathered_ref,
    picks_ref,
    bn_scale_ref,
    bn_bias_ref,
    gain1_ref,
    shift1_ref,
    wqkv_ref,
    gain2_ref,
    shift2_ref,
    b1_ref,
    b2_ref,
    cells_hbm,
    first_hbm,
    bias_hbm,
    cot_hbm,
    w_short_hbm,
    w_out_hbm,
    w1_hbm,
    w2_hbm,
    coef_ref,
    x_hbm,
    qkv_hbm,
    probs_hbm,
    plain_hbm,
    result_hbm,
    dattn_hbm,
    dshort_hbm,
    shared_hbm,
    tail_hbm,
    keep_hbm,
    send_hbm,
    s_ref,
    picked_ref,
    attn_ref,
    pooled_ref,
    bias_ref,
    cot_ref,
    w_short_ref,
    w_out_ref,
    w1_ref,
    w2_ref,
    result_ref,
    dattn_ref,
    dshort_ref,
    shared_ref,
    tail_ref,
    message_ref,
    step_ref,
    load_sems,
    ship_sems,
    store_sems,
):
    pairs = (
        (first_hbm, picked_ref),
        (bias_hbm, bias_ref),
        (w_short_hbm, w_short_ref),
        (w_out_hbm, w_out_ref),
        (w1_hbm, w1_ref),
        (cot_hbm, cot_ref),
        (w2_hbm, w2_ref),
    )
    loads = [pltpu.make_async_copy(a, b, load_sems.at[k]) for k, (a, b) in enumerate(pairs)]
    for load in loads:
        load.start()
    mean, inv = batch_coefficients(gathered_ref[...])
    coef_ref[...] = jnp.zeros_like(coef_ref)
    coef_ref[0:1, :] = mean
    coef_ref[1:2, :] = inv
    loads[0].wait()
    loads[1].wait()

    step_ref[0] = 0

    def body(next_ref, x_ref, qkv_ref, probs_ref, plain_ref):
        crop = step_ref[0]
        step_ref[0] = crop + 1
        attend(
            crop,
            x_ref,
            next_ref,
            picks_ref,
            picked_ref,
            coef_ref,
            bn_scale_ref,
            bn_bias_ref,
            gain1_ref,
            shift1_ref,
            wqkv_ref,
            bias_ref,
            qkv_ref,
            probs_ref,
            attn_ref,
            pooled_ref,
            plain_ref,
            s_ref,
        )

    by_crop = lambda *shape: pl.BlockSpec((1,) + shape, lambda c: (c,) + (0,) * len(shape))
    pltpu.emit_pipeline(
        body,
        grid=(CROPS,),
        in_specs=[
            pl.BlockSpec((1, D_IN, CELLS), lambda c: (jnp.minimum(c + 1, CROPS - 1), 0, 0))
        ],
        out_specs=[
            by_crop(4 * TP, D_IN),
            by_crop(TP, 3 * D),
            by_crop(HEADS, TP, TP),
            by_crop(TP, D_IN),
        ],
    )(cells_hbm, x_hbm, qkv_hbm, probs_hbm, plain_hbm)
    for load in loads[2:]:
        load.wait()
    feed(
        core_ref[0],
        attn_ref,
        pooled_ref,
        cot_ref,
        w_short_ref,
        w_out_ref,
        gain2_ref,
        shift2_ref,
        w1_ref,
        b1_ref,
        w2_ref,
        b2_ref,
        result_ref,
        dattn_ref,
        dshort_ref,
        shared_ref,
        tail_ref,
        message_ref,
        result_hbm,
        dattn_hbm,
        dshort_hbm,
        shared_hbm,
        tail_hbm,
        keep_hbm,
        send_hbm,
        ship_sems,
        store_sems,
    )


def forward(
    core,
    gathered,
    picks,
    cells,
    first,
    bn_scale,
    bn_bias,
    gain1,
    shift1,
    w_qkv,
    gain2,
    shift2,
    b1,
    b2,
    bias,
    cot,
    w_short,
    w_out,
    w1,
    w2,
):
    hbm = pl.BlockSpec(memory_space=pl.ANY)
    small = (gathered, picks, bn_scale, bn_bias, gain1, shift1, w_qkv, gain2, shift2, b1, b2)
    large = (cells, first, bias, cot, w_short, w_out, w1, w2)
    feed_shapes = [
        (ROWS, D),
        (3, ROWS_P, 128),
        (2, ROWS_P, 128),
        (ROWS_P, 128),
        (2, TAIL, 128),
    ]
    return pl.pallas_call(
        forward_kernel,
        in_specs=[pl.BlockSpec(memory_space=pltpu.SMEM)]
        + [whole(a.shape) for a in small]
        + [hbm] * len(large),
        out_specs=[whole((8, D_IN))] + [hbm] * 11,
        out_shape=[
            jax.ShapeDtypeStruct((8, D_IN), FLOAT),
            jax.ShapeDtypeStruct((CROPS, 4 * TP, D_IN), HALF),
            jax.ShapeDtypeStruct((CROPS, TP, 3 * D), HALF),
            jax.ShapeDtypeStruct((CROPS, HEADS, TP, TP), HALF),
            jax.ShapeDtypeStruct((CROPS, TP, D_IN), FLOAT),
        ]
        + [jax.ShapeDtypeStruct(shape, FLOAT) for shape in feed_shapes]
        + [jax.ShapeDtypeStruct((HALF_ROWS, 128), FLOAT)] * 2,
        scratch_shapes=[
            pltpu.VMEM((4, TP, TP), FLOAT),
            pltpu.VMEM((4 * TP, D_IN), HALF),
            pltpu.VMEM((3, ROWS_P, 128), FLOAT),
            pltpu.VMEM((2, ROWS_P, 128), FLOAT),
        ]
        + [pltpu.VMEM(a.shape, a.dtype) for a in (bias, cot, w_short, w_out, w1, w2)]
        + [pltpu.VMEM(shape, FLOAT) for shape in feed_shapes]
        + [
            pltpu.VMEM((2, HALF_ROWS, 128), FLOAT),
            pltpu.SMEM((1,), jnp.int32),
            pltpu.SemaphoreType.DMA((7,)),
            pltpu.SemaphoreType.DMA((6,)),
            pltpu.SemaphoreType.DMA((5,)),
        ],
        compiler_params=params(),
        name="forward",
        cost_estimate=cost(1.6e10, 5e7, 8e6),
    )(core, *small, *large)


def second_message_kernel(pieces_ref, keep_ref, other_ref, out_ref):
    total = pieces_ref[0]
    for k in range(1, PIECES):
        total = total + pieces_ref[k]
    out_ref[:, :EARLY, :] = jnp.broadcast_to(total[None], (PIECES, EARLY, 128))
    out_ref[:, EARLY:, :] = keep_ref[...] + other_ref[...]


def second_message(pieces, keep, other):
    shape = (PIECES, ROWS_2, 128)
    return pl.pallas_call(
        second_message_kernel,
        in_specs=[whole(a.shape) for a in (pieces, keep, other)],
        out_specs=whole(shape),
        out_shape=jax.ShapeDtypeStruct(shape, FLOAT),
        compiler_params=params(20 << 20),
        name="second_message",
        cost_estimate=cost(1e6, 7e6),
    )(pieces, keep, other)


def late_sum_kernel(in_hbm, copies_ref, totals_ref, late_ref, sem):
    load = pltpu.make_async_copy(in_hbm.at[:, pl.ds(EARLY, LATE)], late_ref, sem)
    load.start()
    load.wait()
    total = late_ref[0]
    for k in range(1, PIECES):
        total = total + late_ref[k]
    copies_ref[...] = jnp.broadcast_to(total[None], copies_ref.shape)
    totals_ref[...] = total[24:]


def late_sum(arrived):
    shapes = [(PIECES, LATE, 128), (8, 128)]
    return pl.pallas_call(
        late_sum_kernel,
        in_specs=[pl.BlockSpec(memory_space=pl.ANY)],
        out_specs=[whole(shape) for shape in shapes],
        out_shape=[jax.ShapeDtypeStruct(shape, FLOAT) for shape in shapes],
        scratch_shapes=[pltpu.VMEM((PIECES, LATE, 128), FLOAT), pltpu.SemaphoreType.DMA],
        compiler_params=params(),
        name="late_sum",
        cost_estimate=cost(1e5, 2e6),
    )(arrived)


def touch_kernel(*refs):
    del refs


def pass_after(after, value):
    return pl.pallas_call(
        touch_kernel,
        in_specs=[pl.BlockSpec(memory_space=pl.ANY)] * (len(after) + 1),
        out_specs=pl.BlockSpec(memory_space=pl.ANY),
        out_shape=jax.ShapeDtypeStruct(value.shape, value.dtype),
        input_output_aliases={len(after): 0},
        compiler_params=params(),
        name="pass_after",
        cost_estimate=cost(1, 1),
    )(*after, value)


def unpack_kernel(which_ref, early_ref, *refs):
    g1_ref, g2_ref = refs[-2:]

    def read(at, count):
        pieces = []
        while count:
            piece, row = divmod(at, EARLY)
            n = min(count, EARLY - row)
            pieces.append(early_ref[piece, row : row + n, :])
            at, count = at + n, count - n
        return pieces[0] if len(pieces) == 1 else jnp.concatenate(pieces, axis=0)

    for k in range(FF // 128):
        g1_ref[:, k * 128 : (k + 1) * 128] = read(k * D // 2, D // 2)
    for k in range(FF // 256):
        g2_ref[k * 128 : (k + 1) * 128, :] = read(AT_G2 + k * D, D).T


def unpack_late_kernel(which_ref, late_ref, *refs):
    gout_ref, gshort_ref, gqkv_ref = refs[-11:-8]
    db1_ref, dgain2_ref, dshift2_ref, db2_ref, table_ref, dgain1_ref, dshift1_ref = refs[-8:-1]
    flat_ref = refs[-1]
    for piece in range(PIECES):
        flat_ref[piece * DATA : (piece + 1) * DATA, :] = late_ref[piece, :DATA, :]
    for k in range(9):
        cols = slice(k * 128, (k + 1) * 128)
        at = TAIL + k * D_IN // 2
        gqkv_ref[:, cols] = flat_ref[at : at + D_IN // 2, :]
        if k < 3:
            gout_ref[:, cols] = flat_ref[k * D // 2 : (k + 1) * D // 2, :]
            at = AT_SHORT + k * D_IN // 2
            gshort_ref[:, cols] = flat_ref[at : at + D_IN // 2, :]
    lines = flat_ref[AT_LINES:TAIL, :]
    flat = jnp.concatenate([lines[k : k + 1, :] for k in range(21)], axis=1)
    db1_ref[...] = flat[:, :FF].reshape(FF)
    for k, target in enumerate((dgain2_ref, dshift2_ref, db2_ref)):
        target[...] = flat[:, FF + k * D : FF + (k + 1) * D].reshape(D)
    lines = flat_ref[AT_TABLE : AT_TABLE + 80, :]
    per = TAB // 128
    columns = []
    for k in range(per):
        rows = [lines[h * per + k : h * per + k + 1, :] for h in range(HEADS)]
        columns.append(jnp.concatenate(rows, axis=0))
    table_ref[...] = jnp.concatenate(columns, axis=1)[:, : REL * REL]
    for k, target in enumerate((dgain1_ref, dshift1_ref)):
        at = HEADS * per + 2 * k
        both = jnp.concatenate([lines[at : at + 1, :], lines[at + 1 : at + 2, :]], axis=1)
        target[...] = both[:, :D_IN].reshape(D_IN)


def fill(kernel, name, rows, small, scratch, half, message, before):
    shapes = [(2 * a, b) for a, b in rows] + small
    any_spec = pl.BlockSpec(memory_space=pl.ANY)
    return pl.pallas_call(
        kernel,
        grid_spec=pltpu.PrefetchScalarGridSpec(
            num_scalar_prefetch=1,
            grid=(1,),
            in_specs=[pl.BlockSpec(message.shape, lambda i, h: (0, 0, 0))]
            + [any_spec] * len(before),
            out_specs=[pl.BlockSpec(shape, lambda i, h: (h[0], 0)) for shape in rows]
            + [pl.BlockSpec(shape, lambda i, h, n=len(shape): (0,) * n) for shape in small],
            scratch_shapes=scratch,
        ),
        out_shape=[jax.ShapeDtypeStruct(shape, FLOAT) for shape in shapes],
        input_output_aliases={2 + k: k for k in range(len(before))},
        compiler_params=params(20 << 20),
        name=name,
        cost_estimate=cost(1e6, 6e6),
    )(half, message, *before)


def unpack(half, message, before=()):
    rows = [(D // 2, FF), (FF // 2, D)]
    return fill(unpack_kernel, "unpack", rows, [], [], half, message, before)


def unpack_late(half, message, before=()):
    rows = [(D // 2, D), (D_IN // 2, D), (D_IN // 2, 3 * D)]
    small = [(FF,), (D,), (D,), (D,), (HEADS, REL * REL), (D_IN,), (D_IN,)]
    scratch = [pltpu.VMEM((FLAT, 128), FLOAT)]
    return fill(unpack_late_kernel, "unpack_late", rows, small, scratch, half, message, before)


def back_crop(
    crop,
    coef_ref,
    x_ref,
    plain_ref,
    qkv_ref,
    probs_ref,
    dattn_ref,
    dshort_ref,
    shared_ref,
    bn_scale_ref,
    bn_bias_ref,
    gain_ref,
    shift_ref,
    w_ref,
    dbias_ref,
    gw_ref,
    sums_ref,
    dcells_ref,
    dp_ref,
    ds_ref,
):
    dattn = take_rows(dattn_ref, crop).astype(HALF)
    shared = shared_ref[pl.ds(crop, TP, stride=CROPS), :].T
    key_t = qkv_ref[0, :, D : 2 * D].astype(FLOAT).T.astype(HALF)
    masks = head_masks()
    dquery_t, dkeys, dvalues = [], [], []

    def start(head):
        group = head // 4
        grad = dattn[:, group * 128 : (group + 1) * 128] * masks[head % 4]
        value = qkv_ref[0, :, 2 * D + group * 128 : 2 * D + (group + 1) * 128]
        dp_ref[head % 3] = dot(value, grad, NT)
        dvalues.append(dot(probs_ref[0, head], grad))

    def finish(head):
        group = head // 4
        query = qkv_ref[0, :, group * 128 : (group + 1) * 128] * masks[head % 4]
        dscores = ds_ref[head % 3]
        dkeys.append(dot(dscores, query))
        dquery_t.append(dot(key_t[head * HEAD : (head + 1) * HEAD, :], dscores))

    for head in range(2):
        start(head)
    for head in range(HEADS):
        if head + 2 < HEADS:
            start(head + 2)
        for cols in (slice(0, 128), slice(128, TP)):
            probs = probs_ref[0, head, :, cols].astype(FLOAT)
            dscores = probs * (dp_ref[head % 3, :, cols] - shared[head : head + 1, cols])
            dbias_ref[head, :, cols] += dscores
            ds_ref[head % 3, :, cols] = dscores.astype(HALF)
        if head >= 2:
            finish(head - 2)
    for head in range(HEADS - 2, HEADS):
        finish(head)
    group_sum = lambda items, g: sum(items[4 * g + 1 : 4 * g + 4], items[4 * g])
    dquery = jnp.concatenate(dquery_t, axis=0).T * SCALE
    dqkv = jnp.concatenate(
        [dquery]
        + [group_sum(dkeys, g) * SCALE for g in range(3)]
        + [group_sum(dvalues, g) for g in range(3)],
        axis=1,
    ).astype(HALF)
    pooled = plain_ref[0]
    z, inverse = norm_rows(pooled)
    gain = line(gain_ref)
    first_t = (z * gain + line(shift_ref)).T.astype(HALF)
    gw_ref[...] += dot(first_t, dqkv)
    dfirst = dot(dqkv, w_ref[...], NT)
    dz = dfirst * gain
    dpooled = take_rows(dshort_ref, crop)[:, :D_IN] + inverse * (
        dz
        - jnp.mean(dz, axis=-1, keepdims=True)
        - z * jnp.mean(dz * z, axis=-1, keepdims=True)
    )
    sums_ref[0:1, :] += jnp.sum(dfirst * z, axis=0, keepdims=True)
    sums_ref[1:2, :] += jnp.sum(dfirst, axis=0, keepdims=True)
    level = pooled * LOG2E
    parts = bn_parts(x_ref, coef_ref, bn_scale_ref, bn_bias_ref)
    along = jnp.zeros((TP, D_IN), FLOAT)
    total = jnp.zeros((TP, D_IN), FLOAT)
    for part in range(4):
        dpart = dpooled * jnp.exp2(parts[part] - level)
        dcells_ref[0, part * TP : (part + 1) * TP, :] = dpart.astype(HALF)
        raw = x_ref[0, part * TP : (part + 1) * TP, :].astype(FLOAT)
        along = along + dpart * (raw - coef_ref[0:1, :])
        total = total + dpart
    sums_ref[2:3, :] += jnp.sum(along, axis=0, keepdims=True) * coef_ref[1:2, :]
    sums_ref[3:4, :] += jnp.sum(total, axis=0, keepdims=True)


def back_kernel(
    core_ref,
    after_ref,
    coef_ref,
    bn_scale_ref,
    bn_bias_ref,
    gain_ref,
    shift_ref,
    w_ref,
    spread_ref,
    x_hbm,
    plain_hbm,
    qkv_hbm,
    probs_hbm,
    dattn_hbm,
    dshort_hbm,
    shared_hbm,
    tail_hbm,
    keep_ref,
    send_ref,
    dcells_hbm,
    dattn_ref,
    dshort_ref,
    shared_ref,
    tail_ref,
    dbias_ref,
    gw_ref,
    sums_ref,
    dp_ref,
    ds_ref,
    rows_ref,
    flat_ref,
    step_ref,
    load_sems,
):
    pairs = (
        (dattn_hbm, dattn_ref),
        (dshort_hbm, dshort_ref),
        (shared_hbm, shared_ref),
        (tail_hbm, tail_ref),
    )
    loads = [pltpu.make_async_copy(a, b, load_sems.at[k]) for k, (a, b) in enumerate(pairs)]
    for load in loads:
        load.start()
    dbias_ref[...] = jnp.zeros_like(dbias_ref)
    gw_ref[...] = jnp.zeros_like(gw_ref)
    sums_ref[...] = jnp.zeros_like(sums_ref)
    step_ref[0] = 0
    for load in loads:
        load.wait()

    def body(x_ref, plain_ref, qkv_ref, probs_ref, dcells_ref):
        crop = step_ref[0]
        step_ref[0] = crop + 1
        back_crop(
            crop,
            coef_ref,
            x_ref,
            plain_ref,
            qkv_ref,
            probs_ref,
            dattn_ref,
            dshort_ref,
            shared_ref,
            bn_scale_ref,
            bn_bias_ref,
            gain_ref,
            shift_ref,
            w_ref,
            dbias_ref,
            gw_ref,
            sums_ref,
            dcells_ref,
            dp_ref,
            ds_ref,
        )

    by_crop = lambda *shape: pl.BlockSpec((1,) + shape, lambda c: (c,) + (0,) * len(shape))
    pltpu.emit_pipeline(
        body,
        grid=(CROPS,),
        in_specs=[
            by_crop(4 * TP, D_IN),
            by_crop(TP, D_IN),
            by_crop(TP, 3 * D),
            by_crop(HEADS, TP, TP),
        ],
        out_specs=[by_crop(4 * TP, D_IN)],
    )(x_hbm, plain_hbm, qkv_hbm, probs_hbm, dcells_hbm)

    lines = reduce_bias(dbias_ref, spread_ref, rows_ref)
    pad = jnp.zeros((1, 256 - D_IN), FLOAT)
    for k in range(2):
        value = jnp.concatenate([sums_ref[k : k + 1, :], pad], axis=1)
        lines += [value[:, :128], value[:, 128:]]
    lines.append(jnp.zeros((FLAT - AT_TABLE - len(lines), 128), FLOAT))
    flat_ref[AT_TABLE:, :] = jnp.concatenate(lines, axis=0)
    totals = jnp.concatenate([sums_ref[2:3, :], sums_ref[3:4, :]], axis=1)
    totals = jnp.concatenate([totals[:, k * 128 : (k + 1) * 128] for k in range(3)], axis=0)

    def write(ref, half):
        flat_ref[:TAIL, :] = tail_ref[half]
        for k in range(9):
            at = TAIL + k * D_IN // 2
            flat_ref[at : at + D_IN // 2, :] = gw_ref[
                half * (D_IN // 2) : (half + 1) * (D_IN // 2), k * 128 : (k + 1) * 128
            ]
        for piece in range(PIECES):
            ref[piece, :DATA, :] = flat_ref[piece * DATA : (piece + 1) * DATA, :]
            ref[piece, DATA:, :] = totals

    @pl.when(core_ref[0] == 0)
    def _():
        write(keep_ref, 0)
        write(send_ref, 1)

    @pl.when(core_ref[0] != 0)
    def _():
        write(keep_ref, 1)
        write(send_ref, 0)


def attention_back(
    core,
    after,
    coef,
    bn_scale,
    bn_bias,
    gain,
    shift,
    w_qkv,
    spread,
    picked,
    plain,
    qkv,
    probs,
    dattn,
    dshort,
    shared,
    tail,
):
    hbm = pl.BlockSpec(memory_space=pl.ANY)
    small = (coef, bn_scale, bn_bias, gain, shift, w_qkv, spread)
    large = (picked, plain, qkv, probs, dattn, dshort, shared, tail)
    message = (PIECES, LATE, 128)
    return pl.pallas_call(
        back_kernel,
        in_specs=[pl.BlockSpec(memory_space=pltpu.SMEM), hbm]
        + [whole(a.shape) for a in small]
        + [hbm] * len(large),
        out_specs=[whole(message), whole(message), hbm],
        out_shape=[
            jax.ShapeDtypeStruct(message, FLOAT),
            jax.ShapeDtypeStruct(message, FLOAT),
            jax.ShapeDtypeStruct((CROPS, 4 * TP, D_IN), HALF),
        ],
        scratch_shapes=[pltpu.VMEM(a.shape, FLOAT) for a in (dattn, dshort, shared, tail)]
        + [
            pltpu.VMEM((HEADS, TP, TP), FLOAT),
            pltpu.VMEM((D_IN, 3 * D), FLOAT),
            pltpu.VMEM((8, D_IN), FLOAT),
            pltpu.VMEM((3, TP, TP), FLOAT),
            pltpu.VMEM((3, TP, TP), HALF),
            pltpu.VMEM((HEADS, TP, TAB), FLOAT),
            pltpu.VMEM((FLAT, 128), FLOAT),
            pltpu.SMEM((1,), jnp.int32),
            pltpu.SemaphoreType.DMA((4,)),
        ],
        compiler_params=params(),
        name="attention_back",
        cost_estimate=cost(8e9, 4e7, 2e6),
    )(core, after, *small, *large)


def scatter_kernel(s_ref, d_ref, out_ref):
    for k in range(d_ref.shape[0]):
        for low, high, first, last in CELL_CHUNKS:
            value = None
            for part in range(4):
                rows = slice(part * TP + first, part * TP + last)
                term = dot(d_ref[k, rows, :], s_ref[rows, low:high], TN)
                value = term if value is None else value + term
            out_ref[k, :, low:high] = value.astype(HALF)


def scatter_cells(places, dcells):
    each = 2
    return pl.pallas_call(
        scatter_kernel,
        grid=(CROPS // each,),
        in_specs=[
            whole((4 * TP, CELLS)),
            pl.BlockSpec((each, 4 * TP, D_IN), lambda c: (c, 0, 0)),
        ],
        out_specs=pl.BlockSpec((each, D_IN, CELLS), lambda c: (c, 0, 0)),
        out_shape=jax.ShapeDtypeStruct((CROPS, D_IN, CELLS), HALF),
        compiler_params=params(16 << 20),
        name="scatter_cells",
        cost_estimate=cost(3e9, 8e6),
    )(places, dcells)


def column(row):
    return jnp.broadcast_to(row, (128, D_IN)).T[:, 0:1]


def cells_kernel(count, totals_ref, coef_ref, scale_ref, d_ref, x_ref, out_ref, dscale_ref, dshift_ref, cols_ref):
    @pl.when(pl.program_id(0) == 0)
    def _():
        rows = [totals_ref[k : k + 1, :] for k in range(8 - (LATE - DATA), 8)]
        totals = jnp.concatenate(rows, axis=1)
        along = totals[:, :D_IN]
        plain = totals[:, D_IN:]
        dscale_ref[...] = along.reshape(D_IN)
        dshift_ref[...] = plain.reshape(D_IN)
        mean = coef_ref[0:1, :]
        inv = coef_ref[1:2, :]
        factor = inv * line(scale_ref)
        share = 1.0 / float(count * CROPS * CELLS)
        slope = factor * along * inv * share
        cols_ref[:, 0:1] = column(factor)
        cols_ref[:, 1:2] = column(factor * plain * share)
        cols_ref[:, 2:3] = column(slope)
        cols_ref[:, 3:4] = column(mean)

    out_ref[0] = (
        d_ref[0].astype(FLOAT) * cols_ref[:, 0:1]
        - cols_ref[:, 1:2]
        - (x_ref[0].astype(FLOAT) - cols_ref[:, 3:4]) * cols_ref[:, 2:3]
    )


def cell_gradient(count, totals, coef, bn_scale, dcells, cells):
    crop_block = pl.BlockSpec((1, D_IN, CELLS), lambda c: (c, 0, 0))
    return pl.pallas_call(
        functools.partial(cells_kernel, count),
        grid=(CROPS,),
        in_specs=[
            whole((8, 128)),
            whole((8, D_IN)),
            whole((D_IN,)),
            crop_block,
            crop_block,
        ],
        out_specs=[crop_block, whole((D_IN,)), whole((D_IN,))],
        out_shape=[
            jax.ShapeDtypeStruct((CROPS, D_IN, CELLS), FLOAT),
            jax.ShapeDtypeStruct((D_IN,), FLOAT),
            jax.ShapeDtypeStruct((D_IN,), FLOAT),
        ],
        scratch_shapes=[pltpu.VMEM((D_IN, 128), FLOAT)],
        compiler_params=params(16 << 20),
        name="cell_gradient",
        cost_estimate=cost(1e7, 1.5e7),
    )(totals, coef, bn_scale, dcells, cells)


CHIPS = ("y", "x", "z")
ALL = ("y", "x", "z", "core")


def gather_rows(copies):
    if copies.shape[0] == 1:
        return copies
    return lax.all_to_all(copies, ALL, 0, 0)


def on_device(
    count,
    features,
    bn_scale,
    bn_bias,
    w_short,
    ln1_gain,
    ln1_bias,
    w_qkv,
    rel_table,
    w_out,
    ln2_gain,
    ln2_bias,
    w_fc1,
    fc1_bias,
    w_fc2,
    fc2_bias,
    cotangent,
):
    picks = jnp.asarray(select_matrix(), HALF)
    places = jnp.asarray(scatter_matrix(), HALF)
    spread = jnp.asarray(spread_matrix(), HALF)
    spread_back = jnp.asarray(spread_matrix().T, HALF)
    core = lax.axis_index("core").astype(jnp.int32).reshape(1)
    cells = features.transpose(0, 2, 1)
    cot = cotangent.transpose(1, 0, 2).reshape(ROWS, D)
    stats = gather_rows(local_stats(cells, count))
    bias, first = expand_bias(rel_table, spread, picks, cells)
    coef, picked, qkv, probs, plain, out, dattn, dshort, shared, tail, keep, send = forward(
        core,
        stats,
        picks,
        cells,
        first,
        bn_scale,
        bn_bias,
        ln1_gain,
        ln1_bias,
        w_qkv,
        ln2_gain,
        ln2_bias,
        fc1_bias,
        fc2_bias,
        bias,
        cot,
        w_short,
        w_out,
        w_fc1,
        w_fc2,
    )
    swap = [(0, 1), (1, 0)]
    keep = keep.reshape(PIECES, EARLY, 128)
    send = send.reshape(PIECES, EARLY, 128)
    mine = keep
    if count > 1:
        mine = keep + lax.ppermute(send, "core", swap)
        pieces = lax.all_to_all(mine, CHIPS, 0, 0)
    late_keep, late_send, dcells = attention_back(
        core,
        mine,
        coef,
        bn_scale,
        bn_bias,
        ln1_gain,
        ln1_bias,
        w_qkv,
        spread_back,
        picked,
        plain,
        qkv,
        probs,
        dattn,
        dshort,
        shared,
        tail,
    )
    scattered = scatter_cells(places, dcells)
    if count > 1:
        late = lax.ppermute(late_send, "core", swap)
        own = lax.all_to_all(second_message(pieces, late_keep, late), CHIPS, 0, 0)
        own = pass_after((scattered,), own)
        copies, totals = late_sum(own)
        own_late = lax.all_to_all(copies, CHIPS, 0, 0)
        other = lax.ppermute(own, "core", swap)
    else:
        totals = late_keep[0, 24:]
        own, other = keep, send
        own_late, other_late = late_keep, late_send
    grad_cells, dscale, dshift = cell_gradient(count, totals, coef, bn_scale, scattered, cells)
    g1, g2 = unpack(1 - core, other, unpack(core, own))
    if count > 1:
        own_late = pass_after((g1, grad_cells), own_late)
        other_late = lax.ppermute(own_late, "core", swap)
    grads = unpack_late(core, own_late)
    gout, gshort, gqkv = unpack_late(1 - core, other_late, grads[:3])[:3]
    db1, dgain2, dshift2, db2, table, dgain1, dshift1 = grads[3:]
    return (
        out.reshape(TOK, CROPS, D).transpose(1, 0, 2),
        grad_cells.transpose(0, 2, 1),
        dscale,
        dshift,
        gshort,
        dgain1,
        dshift1,
        gqkv,
        table,
        gout,
        dgain2,
        dshift2,
        g1,
        db1,
        g2,
        db2,
    )


def solution(mesh):
    count = mesh.size
    shape = (4, 4, 4, 2) if count == 128 else (1, 1, 1, 1)
    grid = jax.sharding.Mesh(mesh.devices.reshape(shape), ALL)
    split = P(ALL, None, None)
    same = P()
    in_specs = (split,) + (same,) * 14 + (split,)
    out_specs = (split, split) + (same,) * 14

    def run(*args):
        return on_device(count, *args)

    return jax.shard_map(run, mesh=grid, in_specs=in_specs, out_specs=out_specs, check_vma=False)
```
